32 devices in a mesh: rep: 4 (over z), shard: 8 (over y, x, core).
Axes of the slice: x: 2, y: 2, z: 4, core: 2. Of those that a mesh axis runs over, the one named last changes fastest.
Arguments:
- layer_input_state: bfloat16 [4096, 2048], P(('rep', 'shard')), may hold values from -6 to 6
- cotangent: bfloat16 [4096, 2048], P(('rep', 'shard')), may hold values from -6 to 6
- norm_gain_vectors: bfloat16 [2, 2048], replicated, may hold values from 0.5 to 1.5
- attention_router_weight: bfloat16 [2048, 4], replicated, may hold values from -0.09375 to 0.09375
- feed_router_weight: bfloat16 [2048, 4], replicated, may hold values from -0.09375 to 0.09375
- attention_query_weight: bfloat16 [4, 2048, 2048], P(None, 'shard'), may hold values from -0.125 to 0.125
- key_value_weight: bfloat16 [2, 2048, 2048], P(None, 'shard'), may hold values from -0.125 to 0.125
- attention_output_weight: bfloat16 [4, 2048, 2048], P(None, 'shard'), may hold values from -1 to 1
- feed_expert_weight: bfloat16 [4, 3, 2048, 5632], P(None, None, None, 'shard'), may hold values from -0.125 to 0.125
- attention_adapters: bfloat16 [2, 10, 2048, 128], P(None, None, 'shard'), may hold values from -0.25 to 0.25
- feed_adapter_width: bfloat16 [4, 3, 2048, 128], P(None, None, 'shard'), may hold values from -0.25 to 0.25
- feed_adapter_hidden: bfloat16 [4, 3, 128, 5632], P(None, None, None, 'shard'), may hold values from -0.15625 to 0.15625
- token_document: int32 [4, 1024], P('rep'), may hold values from 0 to 2, as said below
- document_adapter: int32 [4, 3], P('rep'), may hold values from 0 to 7
- attention_expert_pairs: int32 [4096, 2], P(('rep', 'shard')), may hold values from 0 to 3, all different within a row; in each aligned block of 128 rows (0 to 127, 128 to 255, ...) at most 80 rows name the same one
- feed_expert_pairs: int32 [4096, 2], P(('rep', 'shard')), may hold values from 0 to 3, all different within a row; in each aligned block of 128 rows (0 to 127, 128 to 255, ...) at most 80 rows name the same one
Outputs:
- layer_out: float32 [4096, 2048], P(('rep', 'shard'))
- grad_in: float32 [4096, 2048], P(('rep', 'shard'))
- attention_adapter_gradient: float32 [2, 10, 2048, 128], P(None, None, 'shard')
- grad_lora_ffn_d: float32 [4, 3, 2048, 128], P(None, None, 'shard')
- grad_lora_ffn_b: float32 [4, 3, 128, 5632], P(None, None, None, 'shard')
The draws below stay inside these ranges and needn't reach their ends.
Inputs may be any that keep to these rules, and one draw needn't show every extreme that they name: `token_document`: in each stream the ids are 0 on a first run of fewer than 128 tokens, 2 on a last run of fewer than 128 tokens, and 1 between. `attention_expert_pairs`: each row names two different experts; among the 128 rows of one device no expert is named by more than 80 rows, a bound that some block reaches. `feed_expert_pairs`: each row names two different experts; among the 128 rows of one device no expert is named by more than 80 rows, a bound that some block reaches.
All inputs are finite; a program needn't handle non-finite values.
Results may differ from the reference program's by a relative error of at most 0.017.
Values may be sent and summed in bfloat16 or wider, within the bound.
No kernel may reach another device: no remote copies, remote signals or barrier semaphores. Data moves between devices by JAX's collectives and lax.ppermute only.
A program may use at most 768 MiB of HBM per device.

```python
import math
import jax
import jax.numpy as jnp
import numpy as np
from jax import lax

MODEL_WIDTH = 2048
KVH = 16
HD = 128
EXPERT_HIDDEN = 5632
ATTEND_EXPERTS = 4
FEED_EXPERTS = 4
RANK = 16
ADAPT = 8
DOCS = 3
TOK_DEV = 128
CAP = 80
ADAPTER_COLUMNS = 128
SEQ = 1024
ALL_TOK = 4096
N_REP = 4


def draw_token_document(key, part):
    key = jax.random.fold_in(key, 11)
    head_key, tail_key = jax.random.split(key)
    head_len = jax.random.randint(head_key, (N_REP, 1), 1, TOK_DEV)
    tail_len = jax.random.randint(tail_key, (N_REP, 1), 1, TOK_DEV)
    where_at = jnp.arange(SEQ, dtype=jnp.int32)[None, :]
    return (where_at >= head_len).astype(jnp.int32) + (where_at >= SEQ - tail_len).astype(jnp.int32)


def place_ends(drawn, stream_key, low, top_value):
    spot = [jax.random.randint(jax.random.fold_in(stream_key, axis), (), 0, length) for axis, length in enumerate(drawn.shape)]
    widest = drawn.shape.index(max(drawn.shape))
    neighbour = spot[:widest] + [(spot[widest] + 1) % drawn.shape[widest]] + spot[widest + 1:]
    return drawn.at[tuple(spot)].set(low).at[tuple(neighbour)].set(top_value)


def block_levels(stream_key, shape, cuts, smallest, top_value):
    factor_of = 1.0
    for axis_at, shards_of in cuts:
        draws = jax.random.uniform(jax.random.fold_in(jax.random.fold_in(stream_key, 6), axis_at), (shards_of,), jnp.float32, smallest / len(cuts), top_value / len(cuts))
        factor_of = factor_of * jnp.repeat(jnp.exp(draws), shape[axis_at] // shards_of).reshape((-1,) + (1,) * (len(shape) - 1 - axis_at))
    return factor_of


def deal_out(key, own, number, rows, count, top, bound, skew):
    ranking = jax.random.permutation(key, count)
    crowded, usual = load_shares(count, rows * top, bound, skew, True), load_shares(count, rows * top, bound, skew, False)
    places = jnp.arange(count)

    def named(sizes, turn):
        used = int((sizes > 0).sum())
        fixed = max(1, used // 4)
        shifted = fixed + (places - fixed + turn * (used - fixed)) % max(1, count - fixed)
        return jnp.zeros((count,), jnp.int32).at[ranking[jnp.where(places < fixed, places, shifted)]].set(jnp.asarray(sizes, jnp.int32))

    sizes = jnp.where(number % 4 == 0, named(crowded, number // 4), named(usual, number - number // 4 - 1))
    mixed = jax.random.permutation(jax.random.fold_in(own, 3), count)
    donor, receiver = mixed[0:count // 2 * 2:2], mixed[1:count // 2 * 2:2]
    room = jnp.minimum(sizes[donor] - 1, bound - sizes[receiver]) // 2
    room = jnp.where((donor == ranking[0]) | (receiver == ranking[0]) | (sizes[receiver] == 0), 0, jnp.maximum(room, 0))
    shifted = jax.random.randint(jax.random.fold_in(own, 4), (count // 2,), 0, 1 << 20) % (room + 1)
    sizes = sizes.at[donor].add(-shifted).at[receiver].add(shifted)
    members = jnp.searchsorted(jnp.cumsum(sizes), jnp.arange(rows * top), side="right").astype(jnp.int32)
    grid = members.reshape(top, rows).T
    grid = grid[jax.random.permutation(jax.random.fold_in(own, 1), rows)]
    turn = jax.random.randint(jax.random.fold_in(own, 2), (rows, 1), 0, top)
    return jnp.take_along_axis(grid, (jnp.arange(top)[None, :] + turn) % top, axis=1)


def load_shares(number_of, total, limit, lean, full):
    loads = [(1 << 20) // math.isqrt(standing ** lean) + 1 for standing in range(1, number_of + 1)]
    largest = limit if full else min(limit, max(-(-total // number_of), total * loads[0] // sum(loads)))
    least = 1 if total - largest >= number_of - 1 else 0
    given, spare = [largest] + [least] * (number_of - 1), total - largest - least * (number_of - 1)
    while spare > 0:
        movable = [i for i in range(1, number_of) if given[i] < largest] or [i for i in range(1, number_of) if given[i] < limit]
        pool, left = sum([loads[i] for i in movable]), spare
        for i in movable:
            extra = min(limit - given[i], max(1, left * loads[i] // pool), spare)
            given[i] = given[i] + extra
            spare = spare - extra
    return np.array(given)


def centred(key, extent, scale, reach, pieces=(), kind=jnp.bfloat16):
    array = jax.random.normal(key, extent, jnp.float32) * scale
    if len(pieces) > 0:
        array = block_levels(key, extent, pieces, -0.22, 0.18) * array
    return jnp.clip(array, min=-reach, max=reach).astype(kind)


def setup_inputs(seed: int = 0) -> dict:
    key_list = jax.random.split(jax.random.key(seed), 17)
    layer_input_state = centred(key_list[0], (ALL_TOK, MODEL_WIDTH), 1.0, 6.0, ((0, 32),))
    cotangent = centred(key_list[1], (ALL_TOK, MODEL_WIDTH), 1.0, 6.0, ((0, 32),))
    norm_gain_vectors = jnp.clip(1.0 + 0.1 * jax.random.normal(key_list[2], (2, MODEL_WIDTH), jnp.float32), 0.5, 1.5).astype(jnp.bfloat16)
    attention_router_weight = centred(key_list[3], (MODEL_WIDTH, ATTEND_EXPERTS), (2 * MODEL_WIDTH) ** -0.5, 0.09375)
    feed_router_weight = centred(key_list[4], (MODEL_WIDTH, FEED_EXPERTS), (2 * MODEL_WIDTH) ** -0.5, 0.09375)
    attention_query_weight = centred(key_list[5], (ATTEND_EXPERTS, MODEL_WIDTH, MODEL_WIDTH), MODEL_WIDTH ** -0.5, 0.125, ((1, 8),))
    key_value_weight = centred(key_list[6], (2, MODEL_WIDTH, MODEL_WIDTH), MODEL_WIDTH ** -0.5, 0.125, ((1, 8),))
    attention_output_weight = centred(key_list[7], (ATTEND_EXPERTS, MODEL_WIDTH, MODEL_WIDTH), (max(MODEL_WIDTH // 64, 1)) ** -0.5, 1.0, ((1, 8),))
    feed_expert_weight = centred(key_list[8], (FEED_EXPERTS, 3, MODEL_WIDTH, EXPERT_HIDDEN), MODEL_WIDTH ** -0.5, 0.125, ((3, 8),))
    attention_adapters = centred(key_list[9], (2, 2 * ATTEND_EXPERTS + 2, MODEL_WIDTH, ADAPTER_COLUMNS), (MODEL_WIDTH // 4) ** -0.5, 0.25, ((2, 8),))
    feed_adapter_width = centred(key_list[10], (FEED_EXPERTS, 3, MODEL_WIDTH, ADAPTER_COLUMNS), (MODEL_WIDTH // 4) ** -0.5, 0.25, ((2, 8),))
    feed_adapter_hidden = centred(key_list[11], (FEED_EXPERTS, 3, ADAPTER_COLUMNS, EXPERT_HIDDEN), (EXPERT_HIDDEN // 4) ** -0.5, 0.15625, ((3, 8),))
    token_document = draw_token_document(jax.random.fold_in(key_list[16], 71), 0)
    document_adapter = place_ends(jax.random.randint(key_list[13], (N_REP, DOCS), 0, ADAPT), jax.random.fold_in(key_list[13], 1), 0, ADAPT - 1).astype(jnp.int32)
    attention_expert_pairs_keys = jax.random.split(jax.random.fold_in(key_list[14], 1), ALL_TOK // TOK_DEV)
    attention_expert_pairs_turns = jax.random.permutation(jax.random.fold_in(key_list[14], 3), ALL_TOK // TOK_DEV)
    attention_expert_pairs = jax.vmap(lambda own, number: deal_out(jax.random.fold_in(key_list[14], 2), own, number, TOK_DEV, ATTEND_EXPERTS, 2, CAP, 1))(attention_expert_pairs_keys, attention_expert_pairs_turns).reshape((ALL_TOK, 2))
    feed_expert_pairs_keys = jax.random.split(jax.random.fold_in(key_list[15], 1), ALL_TOK // TOK_DEV)
    feed_expert_pairs_turns = jax.random.permutation(jax.random.fold_in(key_list[15], 3), ALL_TOK // TOK_DEV)
    feed_expert_pairs = jax.vmap(lambda own, number: deal_out(jax.random.fold_in(key_list[15], 2), own, number, TOK_DEV, FEED_EXPERTS, 2, CAP, 1))(feed_expert_pairs_keys, feed_expert_pairs_turns).reshape((ALL_TOK, 2))
    return dict(layer_input_state=layer_input_state, cotangent=cotangent, norm_gain_vectors=norm_gain_vectors, attention_router_weight=attention_router_weight, feed_router_weight=feed_router_weight, attention_query_weight=attention_query_weight, key_value_weight=key_value_weight, attention_output_weight=attention_output_weight, feed_expert_weight=feed_expert_weight, attention_adapters=attention_adapters, feed_adapter_width=feed_adapter_width, feed_adapter_hidden=feed_adapter_hidden, token_document=token_document, document_adapter=document_adapter, attention_expert_pairs=attention_expert_pairs, feed_expert_pairs=feed_expert_pairs)


@jax.custom_vjp
def low(v):
    return lax.optimization_barrier(v.astype(jnp.bfloat16)).astype(jnp.float32)

@jax.custom_vjp
def adapter_backward_pass(v):
    return v

def low_keep(v):
    return (low(v), None)

def low_pass(kept, grad):
    return (grad,)

def back_keep(v):
    return (v, None)

def back_low(kept, grad):
    return (low(grad),)
low.defvjp(low_keep, low_pass)
adapter_backward_pass.defvjp(back_keep, back_low)
highest = lax.Precision.HIGHEST
epsilon = 1e-05

def matrix_product(left, right):
    return jnp.dot(left, right, precision=highest)

def rms_norm(values, gain):
    return values * lax.rsqrt(lax.optimization_barrier(jnp.mean(values * values, axis=-1, keepdims=True)) + epsilon) * gain

def rotation(place):
    freq = jnp.exp(-jnp.arange(HD // 2, dtype=jnp.float32) * (2.0 * math.log(10000.0) / HD))
    angles = place.astype(jnp.float32)[:, None] * freq[None, :]
    return (jnp.cos(angles), jnp.sin(angles))

def rope_apply(values, cosine, sine):
    row_count = values.shape[0]
    half_size = cosine.shape[1]
    shaped = values.reshape(row_count, -1, 2 * half_size)
    first_half = shaped[..., :half_size]
    second_half = shaped[..., half_size:]
    cos_b = cosine[:, None, :]
    sin_b = sine[:, None, :]
    turned = jnp.concatenate([first_half * cos_b - second_half * sin_b, second_half * cos_b + first_half * sin_b], axis=-1)
    return turned.reshape(row_count, -1)

def route_weights(logits, routes, count):
    picked = jnp.take_along_axis(logits, routes, axis=1)
    shares = jax.nn.softmax(picked, axis=1)
    table = (routes[:, :, None] == jnp.arange(count)[None, None, :]).astype(jnp.float32)
    return lax.optimization_barrier(jnp.sum(shares[:, :, None] * table, axis=1))

def adapter_branch_term(inputs, down_map, up_map, choose_rows):
    rank_vals = low(adapter_backward_pass(matrix_product(inputs, down_map) * choose_rows))
    return matrix_product(rank_vals, up_map)

def sequence_forward(token_total, attention_adapters, feed_adapter_width, feed_adapter_hidden, frozen_product):
    gains, attention_router_weight, feed_router_weight, attention_query_weight, key_value_weight, attention_output_weight, feed_expert_weight, segments, doc_adapters, attention_expert_pairs, feed_expert_pairs = frozen_product
    seq_len = token_total.shape[0]
    doc_count = doc_adapters.shape[0]
    doc_table = (segments[:, None] == jnp.arange(doc_count)[None, :]).astype(jnp.int32)
    doc_starts = lax.optimization_barrier(jnp.sum((segments[None, :] < jnp.arange(doc_count)[:, None]).astype(jnp.int32), axis=1))
    in_doc = jnp.arange(seq_len, dtype=jnp.int32) - lax.optimization_barrier(jnp.sum(doc_table * doc_starts[None, :], axis=1))
    which = lax.optimization_barrier(jnp.sum(doc_table * doc_adapters[None, :], axis=1))
    choose_rows = (jnp.arange(ADAPT * RANK) // RANK == which[:, None]).astype(jnp.float32)
    cosine, sine = rotation(in_doc)
    stream_pos = jnp.arange(seq_len)
    allowed = (segments[:, None] == segments[None, :]) & (stream_pos[None, :] <= stream_pos[:, None])
    first_normalized = low(rms_norm(token_total, gains[0]))
    attn_share = route_weights(matrix_product(first_normalized, attention_router_weight), attention_expert_pairs, ATTEND_EXPERTS)
    key_before_rotation = adapter_backward_pass(matrix_product(first_normalized, key_value_weight[0]) + adapter_branch_term(first_normalized, attention_adapters[0, ATTEND_EXPERTS], attention_adapters[1, ATTEND_EXPERTS].T, choose_rows))
    value_before_mixing = adapter_backward_pass(matrix_product(first_normalized, key_value_weight[1]) + adapter_branch_term(first_normalized, attention_adapters[0, ATTEND_EXPERTS + 1], attention_adapters[1, ATTEND_EXPERTS + 1].T, choose_rows))
    keys = low(rope_apply(key_before_rotation, cosine, sine)).reshape(seq_len, KVH, HD)
    values = low(value_before_mixing).reshape(seq_len, KVH, HD)

    def one_expert(weight_collection):
        w_query, a_query, b_query, w_output, a_output, b_output = weight_collection
        query_pre = adapter_backward_pass(matrix_product(first_normalized, w_query) + adapter_branch_term(first_normalized, a_query, b_query.T, choose_rows))
        queries = low(rope_apply(query_pre, cosine, sine)).reshape(seq_len, KVH, HD)
        scores = jnp.einsum('qhd,khd->hqk', queries, keys, precision=highest) * HD ** (-0.5)
        scores = jnp.where(allowed[None], adapter_backward_pass(scores), -1e+30)
        probs = low(jax.nn.softmax(scores, axis=-1))
        expert_mixture = jnp.einsum('hqk,khd->qhd', probs, values, precision=highest).reshape(seq_len, KVH * HD)
        expert_mixture = low(adapter_backward_pass(expert_mixture))
        return adapter_backward_pass(matrix_product(expert_mixture, w_output) + adapter_branch_term(expert_mixture, a_output, b_output.T, choose_rows))
    stacked_matrices = (attention_query_weight, attention_adapters[0, :ATTEND_EXPERTS], attention_adapters[1, :ATTEND_EXPERTS], attention_output_weight, attention_adapters[0, ATTEND_EXPERTS + 2:], attention_adapters[1, ATTEND_EXPERTS + 2:])
    expert_attn = lax.map(jax.checkpoint(one_expert), stacked_matrices)
    attended = token_total + jnp.einsum('se,esd->sd', attn_share, expert_attn, precision=highest)
    second_normalized = low(rms_norm(attended, gains[1]))
    ffn_share = route_weights(matrix_product(second_normalized, feed_router_weight), feed_expert_pairs, FEED_EXPERTS)

    def single_feed_expert(weight_collection):
        expert_matrix, adapter_large_side, adapter_small_side = weight_collection
        gate_before_activation = adapter_backward_pass(matrix_product(second_normalized, expert_matrix[0]) + adapter_branch_term(second_normalized, adapter_small_side[0], adapter_large_side[0], choose_rows))
        up_before_activation = adapter_backward_pass(matrix_product(second_normalized, expert_matrix[1]) + adapter_branch_term(second_normalized, adapter_small_side[1], adapter_large_side[1], choose_rows))
        hidden_activation = low(jax.nn.silu(gate_before_activation) * up_before_activation)
        return adapter_backward_pass(matrix_product(hidden_activation, expert_matrix[2].T) + adapter_branch_term(hidden_activation, adapter_large_side[2].T, adapter_small_side[2].T, choose_rows))
    feed_expert_output = lax.map(jax.checkpoint(single_feed_expert), (feed_expert_weight, feed_adapter_hidden, feed_adapter_width))
    return attended + jnp.einsum('se,esd->sd', ffn_share, feed_expert_output, precision=highest)

def reference(layer_input_state, cotangent, norm_gain_vectors, attention_router_weight, feed_router_weight, attention_query_weight, key_value_weight, attention_output_weight, feed_expert_weight, attention_adapters, feed_adapter_width, feed_adapter_hidden, token_document, document_adapter, attention_expert_pairs, feed_expert_pairs):
    gains = norm_gain_vectors.astype(jnp.float32)
    router_a = attention_router_weight.astype(jnp.float32)
    router_f = feed_router_weight.astype(jnp.float32)
    w_query = attention_query_weight.astype(jnp.float32)
    w_keyval = key_value_weight.astype(jnp.float32)
    w_output = attention_output_weight.astype(jnp.float32)
    expert_matrix = feed_expert_weight.astype(jnp.float32)
    adapter_lower_factor = attention_adapters.astype(jnp.float32)
    adapter_width_factor = feed_adapter_width.astype(jnp.float32)
    adapter_upper_factor = feed_adapter_hidden.astype(jnp.float32)
    token_total = layer_input_state.astype(jnp.float32).reshape(N_REP, SEQ, MODEL_WIDTH)
    grads_out = cotangent.astype(jnp.float32).reshape(N_REP, SEQ, MODEL_WIDTH)
    routes_a = attention_expert_pairs.reshape(N_REP, SEQ, 2)
    routes_f = feed_expert_pairs.reshape(N_REP, SEQ, 2)

    def per_stream(carry, stream):
        sequence_tokens, stream_grad, segments, doc_adapters, stream_ra, stream_rf = stream
        frozen_product = (gains, router_a, router_f, w_query, w_keyval, w_output, expert_matrix, segments, doc_adapters, stream_ra, stream_rf)

        def layer_forward_pass(token_input_rows, adapter_lower_input, adapter_width_input, adapter_upper_input):
            return sequence_forward(token_input_rows, adapter_lower_input, adapter_width_input, adapter_upper_input, frozen_product)
        layer_result, backward_function = jax.vjp(layer_forward_pass, sequence_tokens, adapter_lower_factor, adapter_width_factor, adapter_upper_factor)
        grad_tok, grad_a, grad_d, grad_b = backward_function(stream_grad)
        return ((carry[0] + grad_a, carry[1] + grad_d, carry[2] + grad_b), (layer_result, grad_tok))
    begin_offset = (jnp.zeros(adapter_lower_factor.shape, jnp.float32), jnp.zeros(adapter_width_factor.shape, jnp.float32), jnp.zeros(adapter_upper_factor.shape, jnp.float32))
    sums, per_rows = lax.scan(per_stream, begin_offset, (token_total, grads_out, token_document, document_adapter, routes_a, routes_f))
    layer_out = per_rows[0].reshape(ALL_TOK, MODEL_WIDTH)
    grad_in = per_rows[1].reshape(ALL_TOK, MODEL_WIDTH)
    return (layer_out, grad_in, sums[0], sums[1], sums[2])
```

```python
from functools import partial
import math

import jax
import jax.numpy as jnp
from jax import lax
from jax.experimental import pallas as pl
from jax.experimental.pallas import tpu as pltpu
from jax.sharding import PartitionSpec as P

HD = 128
RANK = 16
CAP = 80
EXPERTS = 4
CHUNK = 256
EPS = 1e-05
NEG = -1e30
F32 = jnp.float32
BF16 = jnp.bfloat16


def ein(spec, a, b):
    return jnp.einsum(spec, a, b, preferred_element_type=F32)


def rms_norm(gain, values):
    return values * lax.rsqrt(jnp.mean(values * values, axis=-1, keepdims=True) + EPS) * gain


def rms_back(values, gain, grad):
    unused, backward_function = jax.vjp(partial(rms_norm, gain), values)
    return backward_function(grad)[0]


def masks_of(n):
    return list(range(0, n, 2)) + list(range(1, n, 2))


def swap(x, n, d):
    return lax.ppermute(x, "shard", [(i, i ^ d) for i in range(n)])


def gather_blocks(x, n):
    if n == 8:
        half = x.shape[0] // 2
        y0, x1 = swap(x[:half], n, 4), swap(x[half:], n, 2)
        y1, x0 = swap(x[half:], n, 4), swap(x[:half], n, 2)
        d0, d1 = swap(y0, n, 2), swap(x1, n, 4)
        mine = [[x], [x0, x1], [y0, y1], [d0, d1]]
    else:
        mine = [[x]] + [[swap(x, n, d)] for d in range(2, n, 2)]
    mine = [p[0] if len(p) == 1 else jnp.concatenate(p) for p in mine]
    return jnp.stack(mine + [swap(p, n, 1) for p in mine])


def gather_small(x, n):
    out, d = x[None], 1
    while d < n:
        out = jnp.concatenate([out, swap(out, n, d)])
        d *= 2
    return jnp.stack([out[m] for m in masks_of(n)])


def sum_small(x, n):
    bits, d = n.bit_length() - 1, 1
    lead = x.ndim - 1
    x = x.reshape(x.shape[:lead] + (2,) * bits + (x.shape[lead] // n,))
    for k in range(bits):
        got = swap(x, n, d)
        x = x + jnp.flip(got, lead if k == 0 else lead + bits - k)
        d *= 2
    return x.reshape(x.shape[:lead] + (-1,))


def reduce_blocks(parts, n):
    h = n // 2
    near, far = parts[:h], parts[h:]
    got = swap(far, n, 1)
    q = near.astype(F32) + got.astype(F32)
    if n == 8:
        half = parts.shape[1] // 2
        low = q.astype(BF16)
        ra = swap(jnp.stack([low[1, :half], low[3, :half]]), n, 2).astype(F32)
        rb = swap(jnp.stack([low[2, half:], low[3, half:]]), n, 4).astype(F32)
        a0, a2 = q[0, :half] + ra[0], q[2, :half] + ra[1]
        b0, b1 = q[0, half:] + rb[0], q[1, half:] + rb[1]
        a0 = a0 + swap(a2.astype(BF16), n, 4).astype(F32)
        b0 = b0 + swap(b1.astype(BF16), n, 2).astype(F32)
        return jnp.concatenate([a0, b0])
    total = q[0]
    for i in range(1, h):
        total = total + swap(q[i].astype(BF16), n, 2 * i).astype(F32)
    return total


def reorder(stacked, me, n):
    where = position(me, n)
    return jnp.concatenate([lax.dynamic_slice_in_dim(stacked, where[j], 1, 0) for j in range(n)])


def position(me, n):
    mask = jnp.arange(n, dtype=jnp.int32) ^ me
    return jnp.where(mask % 2 == 0, mask // 2, n // 2 + mask // 2)


def reshard(w, me, n, axis):
    width = w.shape[-1] // n
    pieces = []
    for m in masks_of(n):
        piece = lax.dynamic_slice_in_dim(w, (me ^ m) * width, width, w.ndim - 1)
        pieces.append(piece if m == 0 else swap(piece, n, m))
    whole = reorder(jnp.stack(pieces), me, n)
    whole = jnp.moveaxis(whole, 0, axis)
    return whole.reshape(w.shape[:axis] + (n * w.shape[axis], width))


def turn(v, cos, sin):
    return v * cos + pltpu.roll(v, HD // 2, 1) * sin


def attend_kernel(
    where, qp, cs, sn, lo, hi, kp, vv, ct, st, mixed, qr, kr, lse, k_abs, v_abs, scores, mx, tot, acc
):
    b = pl.program_id(1)
    n, rows = kp.shape[0], qp.shape[0] * qp.shape[1]
    tok = kp.shape[1]

    @pl.when(b == 0)
    def start():
        def one(j, carry):
            at = where[j]
            k = turn(kp[at], ct[at], st[at]).astype(BF16)
            kr[at] = k
            begin = pl.multiple_of(j * tok, tok)
            k_abs[pl.ds(begin, tok), :] = k
            v_abs[pl.ds(begin, tok), :] = vv[at]
            return carry

        lax.fori_loop(0, n, one, 0)

    def flat(r):
        return r[...].reshape(rows, r.shape[-1])

    q = turn(flat(qp), flat(cs), flat(sn)).astype(BF16)
    qr[...] = q.reshape(qr.shape)
    first, last = flat(lo), flat(hi)
    count = (b * tok + tok + CHUNK - 1) // CHUNK
    mx[...] = jnp.full(mx.shape, NEG, F32)

    def score(j, carry):
        begin = pl.multiple_of(j * CHUNK, CHUNK)
        s = lax.dot_general(
            q, k_abs[pl.ds(begin, CHUNK), :], (((1,), (1,)), ((), ())), preferred_element_type=F32
        ) * HD ** (-0.5)
        at = begin + lax.broadcasted_iota(jnp.int32, s.shape, 1)
        s = jnp.where((at >= first) & (at <= last), s, NEG)
        scores[:, pl.ds(begin, CHUNK)] = s
        mx[...] = jnp.maximum(mx[...], jnp.maximum(s[:, :HD], s[:, HD:]))
        return carry

    lax.fori_loop(0, count, score, 0)
    top = jnp.max(mx[...], axis=1, keepdims=True)
    tot[...] = jnp.zeros(tot.shape, F32)
    acc[...] = jnp.zeros(acc.shape, F32)

    def mix(j, carry):
        begin = pl.multiple_of(j * CHUNK, CHUNK)
        p = jnp.exp(scores[:, pl.ds(begin, CHUNK)] - top)
        tot[...] += p[:, :HD] + p[:, HD:]
        acc[...] += jnp.dot(
            p.astype(BF16), v_abs[pl.ds(begin, CHUNK), :], preferred_element_type=F32
        )
        return carry

    lax.fori_loop(0, count, mix, 0)
    total = jnp.sum(tot[...], axis=1, keepdims=True)
    mixed[...] = (acc[...] / total).astype(BF16).reshape(mixed.shape)
    lse[...] = jnp.broadcast_to(top + jnp.log(total), (rows, HD)).reshape(lse.shape)


def attend_back_kernel(
    where, qr, gm, mixed, lse, cs, sn, lo, hi, kr, vv, ct, st, gq, gk, gv, k_abs, v_abs, dk, dv, dq
):
    b = pl.program_id(1)
    n, rows = kr.shape[0], qr.shape[0] * qr.shape[1]
    tok = kr.shape[1]
    scale = HD ** (-0.5)

    @pl.when(b == 0)
    def start():
        def one(j, carry):
            at = where[j]
            begin = pl.multiple_of(j * tok, tok)
            k_abs[pl.ds(begin, tok), :] = kr[at]
            v_abs[pl.ds(begin, tok), :] = vv[at]
            return carry

        lax.fori_loop(0, n, one, 0)
        dk[...] = jnp.zeros(dk.shape, F32)
        dv[...] = jnp.zeros(dv.shape, F32)

    def flat(r):
        return r[...].reshape(rows, r.shape[-1])

    q, g = flat(qr), flat(gm)
    delta = jnp.sum(flat(mixed).astype(F32) * g.astype(F32), axis=1, keepdims=True)
    log_total = flat(lse)[:, :1]
    first, last = flat(lo), flat(hi)
    count = (b * tok + tok + CHUNK - 1) // CHUNK
    dq[...] = jnp.zeros(dq.shape, F32)
    nt = (((1,), (1,)), ((), ()))
    tn = (((0,), (0,)), ((), ()))

    def step(j, carry):
        begin = pl.multiple_of(j * CHUNK, CHUNK)
        here = pl.ds(begin, CHUNK)
        k, v = k_abs[here, :], v_abs[here, :]
        s = lax.dot_general(q, k, nt, preferred_element_type=F32) * scale
        at = begin + lax.broadcasted_iota(jnp.int32, s.shape, 1)
        p = jnp.where((at >= first) & (at <= last), jnp.exp(s - log_total), 0.0)
        dp = lax.dot_general(g, v, nt, preferred_element_type=F32)
        ds = (p * (dp - delta)).astype(BF16)
        dq[...] += jnp.dot(ds, k, preferred_element_type=F32)
        dk[here, :] += lax.dot_general(ds, q, tn, preferred_element_type=F32)
        dv[here, :] += lax.dot_general(p.astype(BF16), g, tn, preferred_element_type=F32)
        return carry

    lax.fori_loop(0, count, step, 0)
    gq[...] = turn(dq[...] * scale, flat(cs), -flat(sn)).astype(BF16).reshape(gq.shape)

    @pl.when(b == n - 1)
    def finish():
        def one(j, carry):
            at = where[j]
            here = pl.ds(pl.multiple_of(j * tok, tok), tok)
            gk[at] = turn(dk[here, :] * scale, ct[at], -st[at]).astype(BF16)
            gv[at] = dv[here, :].astype(BF16)
            return carry

        lax.fori_loop(0, n, one, 0)


def slot_spec(width, per_head, n):
    if per_head:
        return pl.BlockSpec((EXPERTS, None, CAP, width), lambda h, b, where: (0, where[b], 0, h))
    return pl.BlockSpec((EXPERTS, None, CAP, width), lambda h, b, where: (0, where[b], 0, 0))


def token_spec(n, tok, per_head):
    if per_head:
        return pl.BlockSpec((n, tok, HD), lambda h, b, where: (0, 0, h))
    return pl.BlockSpec((n, tok, HD), lambda h, b, where: (0, 0, 0))


def attend(where, q_pre, cos_slot, sin_slot, lo, hi, k_pre, v, cos_tok, sin_tok):
    n, tok, own = k_pre.shape
    heads, seq, rows = own // HD, n * tok, EXPERTS * CAP
    qs, ss, one = slot_spec(HD, True, n), slot_spec(HD, False, n), slot_spec(1, False, n)
    kh, ks = token_spec(n, tok, True), token_spec(n, tok, False)
    slots = (EXPERTS, n, CAP, own)
    return pl.pallas_call(
        attend_kernel,
        grid_spec=pltpu.PrefetchScalarGridSpec(
            num_scalar_prefetch=1,
            grid=(heads, n),
            in_specs=[qs, ss, ss, one, one, kh, kh, ks, ks],
            out_specs=[qs, qs, kh, qs],
            scratch_shapes=[
                pltpu.VMEM((seq, HD), BF16),
                pltpu.VMEM((seq, HD), BF16),
                pltpu.VMEM((rows, seq + CHUNK), F32),
                pltpu.VMEM((rows, HD), F32),
                pltpu.VMEM((rows, HD), F32),
                pltpu.VMEM((rows, HD), F32),
            ],
        ),
        out_shape=[
            jax.ShapeDtypeStruct(slots, BF16),
            jax.ShapeDtypeStruct(slots, BF16),
            jax.ShapeDtypeStruct((n, tok, own), BF16),
            jax.ShapeDtypeStruct(slots, F32),
        ],
        compiler_params=pltpu.CompilerParams(vmem_limit_bytes=48 << 20),
        cost_estimate=pl.CostEstimate(
            flops=3 * rows * seq * own * n, bytes_accessed=16 << 20, transcendentals=rows * seq * n
        ),
        name="attend",
    )(where, q_pre, cos_slot, sin_slot, lo, hi, k_pre, v, cos_tok, sin_tok)


def attend_back(where, q_rot, gm, mixed, lse, cos_slot, sin_slot, lo, hi, k_rot, v, cos_tok, sin_tok):
    n, tok, own = k_rot.shape
    heads, seq, rows = own // HD, n * tok, EXPERTS * CAP
    qs, ss, one = slot_spec(HD, True, n), slot_spec(HD, False, n), slot_spec(1, False, n)
    kh, ks = token_spec(n, tok, True), token_spec(n, tok, False)
    return pl.pallas_call(
        attend_back_kernel,
        grid_spec=pltpu.PrefetchScalarGridSpec(
            num_scalar_prefetch=1,
            grid=(heads, n),
            in_specs=[qs, qs, qs, qs, ss, ss, one, one, kh, kh, ks, ks],
            out_specs=[qs, kh, kh],
            scratch_shapes=[
                pltpu.VMEM((seq, HD), BF16),
                pltpu.VMEM((seq, HD), BF16),
                pltpu.VMEM((seq, HD), F32),
                pltpu.VMEM((seq, HD), F32),
                pltpu.VMEM((rows, HD), F32),
            ],
        ),
        out_shape=[
            jax.ShapeDtypeStruct((EXPERTS, n, CAP, own), BF16),
            jax.ShapeDtypeStruct((n, tok, own), BF16),
            jax.ShapeDtypeStruct((n, tok, own), BF16),
        ],
        compiler_params=pltpu.CompilerParams(vmem_limit_bytes=48 << 20),
        cost_estimate=pl.CostEstimate(
            flops=7 * rows * seq * own * n, bytes_accessed=16 << 20, transcendentals=rows * seq * n
        ),
        name="attend_back",
    )(where, q_rot, gm, mixed, lse, cos_slot, sin_slot, lo, hi, k_rot, v, cos_tok, sin_tok)


def members(routes):
    names = jnp.arange(EXPERTS, dtype=jnp.int32)[None, :, None]
    member = (routes[:, :1] == names) | (routes[:, 1:] == names)
    tok = routes.shape[-1]
    before = (jnp.arange(tok)[:, None] < jnp.arange(tok)[None, :]).astype(BF16)
    rank = ein("met,tu->meu", member.astype(BF16), before).astype(jnp.int32)
    slots = jnp.arange(CAP, dtype=jnp.int32)[None, None, :, None]
    chosen = member[:, :, None, :] & (rank[:, :, None, :] == slots)
    return member, chosen


def shares_of(normed, router, member):
    logits = ein("mtd,de->met", normed, router)
    return jax.nn.softmax(jnp.where(member, logits, -jnp.inf), axis=1)


def pick_slots(chosen, values):
    return jnp.sum(jnp.where(chosen, values[:, :, None, :], 0), axis=-1).transpose(1, 0, 2)


def dispatch(chosen, tokens):
    slots = jnp.einsum("mect,mtd->emcd", chosen.astype(BF16), tokens, preferred_element_type=BF16)
    return slots.reshape(EXPERTS, -1, tokens.shape[-1])


def combine(chosen, slots, n):
    slots = slots.reshape(EXPERTS, n, CAP, -1)
    return ein("mect,emcd->mtd", chosen.astype(BF16), slots)


def route_back(share, grad_share, router):
    grad = share * (grad_share - jnp.sum(share * grad_share, axis=0, keepdims=True))
    return jnp.einsum(
        "et,de->td", grad, router.astype(F32), precision=lax.Precision.HIGHEST
    )


def live_rank(rank, select):
    e, k, s = rank.shape
    return jnp.sum(rank.reshape(e, k // RANK, RANK, s) * select[:, :, None, :], axis=1)


def spread(live, select):
    e, k, s = live.shape
    return (live[:, None] * select[:, :, None, :]).reshape(e, -1, s)


def local(
    n,
    reps,
    layer_input_state,
    cotangent,
    norm_gain_vectors,
    attention_router_weight,
    feed_router_weight,
    attention_query_weight,
    key_value_weight,
    attention_output_weight,
    feed_expert_weight,
    attention_adapters,
    feed_adapter_width,
    feed_adapter_hidden,
    token_document,
    document_adapter,
    attention_expert_pairs,
    feed_expert_pairs,
):
    tok, wide = layer_input_state.shape
    own = wide // n
    columns = attention_adapters.shape[3]
    me = lax.axis_index("shard")
    order = jnp.array(masks_of(n), jnp.int32) ^ me
    where = position(me, n)
    segments = token_document[0]
    seq = segments.shape[0]
    docs = document_adapter[0]
    doc_count = docs.shape[0]

    routes = jnp.concatenate([attention_expert_pairs.T, feed_expert_pairs.T])
    routes = gather_small(routes, n)
    x = layer_input_state.astype(F32)
    gain_one = norm_gain_vectors[0].astype(F32)
    gain_two = norm_gain_vectors[1].astype(F32)
    normed_own = rms_norm(gain_one, x).astype(BF16)
    normed = gather_blocks(normed_own, n)
    w_kv = reshard(key_value_weight, me, n, 1)
    w_query = reshard(attention_query_weight, me, n, 1)

    def one_hot(which):
        at = which[:, None] * RANK + jnp.arange(RANK)[None, :]
        return (at.reshape(-1)[:, None] == jnp.arange(columns)[None, :]).astype(BF16)

    pick = one_hot(docs)
    attn_small = ein("kc,pmwc->pmkw", pick, attention_adapters).astype(BF16)
    width_small = ein("kc,pmwc->pmkw", pick, feed_adapter_width).astype(BF16)
    hidden_small = ein("kc,epcf->epkf", pick, feed_adapter_hidden).astype(BF16)

    def gather_small_maps(maps):
        whole = reorder(gather_blocks(maps, n), me, n)
        return jnp.moveaxis(whole, 0, 2).reshape(maps.shape[0], maps.shape[1], -1)

    a_in = gather_small_maps(attn_small[0, : EXPERTS + 2])
    b_out = gather_small_maps(attn_small[1, EXPERTS + 2 :])
    width_all = gather_small_maps(width_small.reshape(EXPERTS * 3, -1, own))
    width_all = width_all.reshape(EXPERTS, 3, -1, wide)
    b_in, a_out = attn_small[1, : EXPERTS + 2], attn_small[0, EXPERTS + 2 :]
    grads_out_all = gather_blocks(cotangent, n)

    begins = jnp.sum((segments[None, :] < jnp.arange(doc_count)[:, None]).astype(jnp.int32), axis=1)
    doc = segments.reshape(n, tok)[order]
    place = order[:, None] * tok + jnp.arange(tok, dtype=jnp.int32)[None, :]
    doc_table = doc[None] == jnp.arange(doc_count, dtype=jnp.int32)[:, None, None]
    begin = jnp.sum(jnp.where(doc_table, begins[:, None, None], 0), axis=0)
    freq = jnp.exp(-jnp.arange(HD // 2, dtype=F32) * (2.0 * math.log(10000.0) / HD))
    angles = (place - begin).astype(F32)[..., None] * freq
    cos, sin = jnp.cos(angles), jnp.sin(angles)
    cos_tok = jnp.concatenate([cos, cos], axis=-1)
    sin_tok = jnp.concatenate([-sin, sin], axis=-1)
    select_tok = doc_table.astype(F32).reshape(1, doc_count, seq)

    def slot_facts(chosen):
        chose = chosen[:, :, None] & doc_table.transpose(1, 0, 2)[:, None, :, None, :]
        select = jnp.any(chose, axis=-1).astype(F32)
        return select.transpose(1, 2, 0, 3).reshape(EXPERTS, doc_count, n * CAP)

    member_a, chosen_a = members(routes[:, :2])
    member_f, chosen_f = members(routes[:, 2:])
    select_a, select_f = slot_facts(chosen_a), slot_facts(chosen_f)
    lo = pick_slots(chosen_a, begin[:, None])[..., None]
    hi = pick_slots(chosen_a, place[:, None])[..., None]

    def spread_table(table):
        return jnp.einsum(
            "mect,mtd->emcd", chosen_a.astype(F32), table, precision=lax.Precision.HIGHEST
        )

    cos_slot, sin_slot = spread_table(cos_tok), spread_table(sin_tok)

    def to_rank(maps, rows, select):
        e, k, s = maps.shape[0], maps.shape[1], rows.shape[1]
        rank = ein("ekd,esd->eks", maps, rows).reshape(e, doc_count, -1, s)
        return (rank * select[:, :, None, :]).reshape(e, k, s).astype(BF16)

    share_a = shares_of(normed, attention_router_weight, member_a)
    share_a_slot = pick_slots(chosen_a, share_a).reshape(EXPERTS, -1)
    rows_a = dispatch(chosen_a, normed)
    rank_q = to_rank(a_in[:EXPERTS], rows_a, select_a)
    q_pre = ein("esd,edh->esh", rows_a, w_query) + ein("eks,ekh->esh", rank_q, b_in[:EXPERTS])
    flat = normed.reshape(1, seq, wide)
    rank_kv = to_rank(a_in[EXPERTS:], jnp.broadcast_to(flat, (2, seq, wide)), select_tok)
    kv_pre = ein("sd,pdh->psh", flat[0], w_kv) + ein("pks,pkh->psh", rank_kv, b_in[EXPERTS:])
    k_pre = kv_pre[0].reshape(n, tok, own)
    values = kv_pre[1].astype(BF16).reshape(n, tok, own)
    mixed, q_rot, k_rot, lse = attend(
        where,
        q_pre.reshape(EXPERTS, n, CAP, own),
        cos_slot,
        sin_slot,
        lo,
        hi,
        k_pre,
        values,
        cos_tok,
        sin_tok,
    )
    mixed_rows = mixed.reshape(EXPERTS, n * CAP, own)
    rank_o = to_rank(a_out, mixed_rows, select_a)
    out_rows = ein("esh,ehd->esd", mixed_rows, attention_output_weight)
    out_rows = (out_rows + ein("eks,ekd->esd", rank_o, b_out)) * share_a_slot[..., None]
    attended = x + reduce_blocks(combine(chosen_a, out_rows.astype(BF16), n).astype(BF16), n)

    normed_two = gather_blocks(rms_norm(gain_two, attended).astype(BF16), n)
    share_f = shares_of(normed_two, feed_router_weight, member_f)
    share_f_slot = pick_slots(chosen_f, share_f).reshape(EXPERTS, -1)
    rows_f = dispatch(chosen_f, normed_two)
    rows_g = dispatch(chosen_f, grads_out_all)
    rank_gate = to_rank(width_all[:, 0], rows_f, select_f)
    rank_up = to_rank(width_all[:, 1], rows_f, select_f)
    back_down = to_rank(width_all[:, 2], rows_g, select_f)
    gate = ein("esd,edf->esf", rows_f, feed_expert_weight[:, 0])
    gate = gate + ein("eks,ekf->esf", rank_gate, hidden_small[:, 0])
    up = ein("esd,edf->esf", rows_f, feed_expert_weight[:, 1])
    up = up + ein("eks,ekf->esf", rank_up, hidden_small[:, 1])
    grad_inner = ein("esd,edf->esf", rows_g, feed_expert_weight[:, 2])
    grad_inner = grad_inner + ein("eks,ekf->esf", back_down, hidden_small[:, 2])
    sig = jax.nn.sigmoid(gate)
    inner_f = gate * sig * up
    inner = inner_f.astype(BF16)
    grad_share_f = jnp.sum(inner_f * grad_inner, axis=-1)
    scaled = grad_inner * share_f_slot[..., None]
    grad_gate = (scaled * up * sig * (1.0 + gate * (1.0 - sig))).astype(BF16)
    grad_up = (scaled * gate * sig).astype(BF16)
    back_gate = to_rank(hidden_small[:, 0], grad_gate, select_f)
    back_up = to_rank(hidden_small[:, 1], grad_up, select_f)
    grad_rows_f = ein("esf,edf->esd", grad_gate, feed_expert_weight[:, 0])
    grad_rows_f = grad_rows_f + ein("esf,edf->esd", grad_up, feed_expert_weight[:, 1])
    grad_rows_f = grad_rows_f + ein("eks,ekd->esd", back_gate, width_all[:, 0])
    grad_rows_f = grad_rows_f + ein("eks,ekd->esd", back_up, width_all[:, 1])
    grad_two_own = reduce_blocks(combine(chosen_f, grad_rows_f.astype(BF16), n).astype(BF16), n)
    rank_down = to_rank(hidden_small[:, 2], inner, select_f)
    ffn_rows = ein("esf,edf->esd", inner, feed_expert_weight[:, 2])
    ffn_rows = (ffn_rows + ein("eks,ekd->esd", rank_down, width_all[:, 2])) * share_f_slot[..., None]
    layer_out = attended + reduce_blocks(combine(chosen_f, ffn_rows.astype(BF16), n).astype(BF16), n)

    def own_tokens(chosen, slot_values):
        first = slot_values.reshape(EXPERTS, n, CAP)[:, 0]
        return jnp.sum(jnp.where(chosen[0], first[:, :, None], 0.0), axis=1)

    grad_share_f = sum_small(grad_share_f, n)
    grads_out = cotangent.astype(F32)
    grad_two_own = grad_two_own + route_back(
        share_f[0], own_tokens(chosen_f, grad_share_f), feed_router_weight
    )
    grad_attended = grads_out + rms_back(attended, gain_two, grad_two_own)

    grads_two = gather_blocks(grad_attended.astype(BF16), n)
    rows_ga = dispatch(chosen_a, grads_two)
    back_out = to_rank(b_out, rows_ga, select_a)
    grad_mixed = ein("esd,ehd->esh", rows_ga, attention_output_weight)
    grad_mixed = grad_mixed + ein("eks,ekh->esh", back_out, a_out)
    grad_share_a = sum_small(jnp.sum(mixed_rows.astype(F32) * grad_mixed, axis=-1), n)
    grad_mixed = (grad_mixed * share_a_slot[..., None]).astype(BF16)
    gq, gk, gv = attend_back(
        where,
        q_rot,
        grad_mixed.reshape(EXPERTS, n, CAP, own),
        mixed,
        lse,
        cos_slot,
        sin_slot,
        lo,
        hi,
        k_rot,
        values,
        cos_tok,
        sin_tok,
    )
    gq = gq.reshape(EXPERTS, n * CAP, own)
    gkv = jnp.stack([gk, gv]).reshape(2, seq, own)
    back_q = to_rank(b_in[:EXPERTS], gq, select_a)
    back_kv = to_rank(b_in[EXPERTS:], gkv, select_tok)
    grad_rows_a = ein("esh,edh->esd", gq, w_query) + ein("eks,ekd->esd", back_q, a_in[:EXPERTS])
    grad_normed = combine(chosen_a, grad_rows_a.astype(BF16), n).reshape(seq, wide)
    grad_normed = grad_normed + ein("sh,dh->sd", gkv[0], w_kv[0]) + ein("sh,dh->sd", gkv[1], w_kv[1])
    grad_normed = grad_normed + ein("pks,pkd->sd", back_kv, a_in[EXPERTS:])
    grad_normed = reduce_blocks(grad_normed.astype(BF16).reshape(n, tok, wide), n)
    grad_normed = grad_normed + route_back(
        share_a[0], own_tokens(chosen_a, grad_share_a), attention_router_weight
    )
    grad_in = grad_attended + rms_back(x, gain_one, grad_normed)

    def whole_rank(rank, select):
        live = live_rank(rank.astype(F32), select)
        return spread(sum_small(live.astype(BF16), n).astype(F32), select)

    def mine(rows):
        return lax.dynamic_slice_in_dim(rows, me * own, own, rows.ndim - 1)

    def grads(spec, rank, rows):
        return ein(spec, rank.astype(BF16), rows).astype(BF16)

    eks = "eks,esw->ekw"
    share_a_row, share_f_row = share_a_slot[:, None, :], share_f_slot[:, None, :]
    whole = [whole_rank(r, select_f) for r in (back_gate, back_up, rank_down)]
    rows_f_own, rows_g_own = mine(rows_f), mine(rows_g)
    width_grad = jnp.stack(
        [
            grads(eks, whole[0], rows_f_own),
            grads(eks, whole[1], rows_f_own),
            grads(eks, whole[2] * share_f_row, rows_g_own),
        ],
        axis=1,
    )
    hidden_grad = jnp.stack(
        [
            grads(eks, rank_gate, grad_gate),
            grads(eks, rank_up, grad_up),
            grads(eks, back_down * share_f_row, inner),
        ],
        axis=1,
    )
    whole_q = whole_rank(back_q, select_a)
    whole_kv = whole_rank(back_kv, select_tok)
    whole_o = whole_rank(rank_o, select_a)
    own_flat = mine(flat[0])
    attn_grad = jnp.stack(
        [
            jnp.concatenate(
                [
                    grads(eks, whole_q, mine(rows_a)),
                    grads("pks,sw->pkw", whole_kv, own_flat),
                    grads(eks, back_out * share_a_row, mixed_rows),
                ]
            ),
            jnp.concatenate(
                [
                    grads(eks, rank_q, gq),
                    grads(eks, rank_kv, gkv),
                    grads(eks, whole_o * share_a_row, mine(rows_ga)),
                ]
            ),
        ]
    )
    picks = lax.all_gather(document_adapter, "rep", axis=0, tiled=True)
    picks = jax.vmap(one_hot)(picks)

    def all_streams(g):
        return lax.all_gather(g, "rep", axis=0)

    attn_out = ein("rpmkw,rkc->pmwc", all_streams(attn_grad), picks)
    width_out = ein("rpmkw,rkc->pmwc", all_streams(width_grad), picks)
    hidden_out = ein("rpmkw,rkc->pmcw", all_streams(hidden_grad), picks)
    return (layer_out, grad_in, attn_out, width_out, hidden_out)


def solution(mesh):
    in_specs = (
        P(("rep", "shard"), None),
        P(("rep", "shard"), None),
        P(),
        P(),
        P(),
        P(None, "shard", None),
        P(None, "shard", None),
        P(None, "shard", None),
        P(None, None, None, "shard"),
        P(None, None, "shard", None),
        P(None, None, "shard", None),
        P(None, None, None, "shard"),
        P("rep", None),
        P("rep", None),
        P(("rep", "shard"), None),
        P(("rep", "shard"), None),
    )
    out_specs = (
        P(("rep", "shard"), None),
        P(("rep", "shard"), None),
        P(None, None, "shard", None),
        P(None, None, "shard", None),
        P(None, None, None, "shard"),
    )
    body = partial(local, mesh.shape["shard"], mesh.shape["rep"])
    return jax.shard_map(body, mesh=mesh, in_specs=in_specs, out_specs=out_specs, check_vma=False)
```

```python
from functools import partial
import math

import jax
import jax.numpy as jnp
from jax import lax
from jax.experimental import pallas as pl
from jax.experimental.pallas import tpu as pltpu
from jax.sharding import PartitionSpec as P

HD = 128
RANK = 16
CAP = 80
EXPERTS = 4
CHUNK = 256
EPS = 1e-05
NEG = -1e30
F32 = jnp.float32
BF16 = jnp.bfloat16


def ein(spec, a, b):
    return jnp.einsum(spec, a, b, preferred_element_type=F32)


def rms_norm(gain, values):
    return values * lax.rsqrt(jnp.mean(values * values, axis=-1, keepdims=True) + EPS) * gain


def rms_back(values, gain, grad):
    unused, backward_function = jax.vjp(partial(rms_norm, gain), values)
    return backward_function(grad)[0]


NT = (((1,), (1,)), ((), ()))
TN = (((0,), (0,)), ((), ()))


def dot_nt(a, b):
    return lax.dot_general(a, b, NT, preferred_element_type=F32)


def dot_tn(a, b):
    return lax.dot_general(a, b, TN, preferred_element_type=F32)


def dot_nn(a, b):
    return jnp.dot(a, b, preferred_element_type=F32)


def swap(x, n, d):
    return lax.ppermute(x, "shard", [(i, i ^ d) for i in range(n)])


def tie(*values):
    return lax.optimization_barrier(values)


def across(x, n):
    return {d: swap(x, n, d) if d else x for d in range(0, n, 2)}


def from_sibling(pieces, n):
    other = {m ^ 1: swap(p, n, 1) for m, p in pieces.items()}
    return [p for unused, p in sorted({**pieces, **other}.items())]


def gather_small(x, me, n):
    out, d = x[None], 1
    while d < n:
        out = jnp.concatenate([out, swap(out, n, d)])
        d *= 2
    return out[jnp.arange(n) ^ me]


def sum_small(x, n):
    d = 1
    while d < n:
        x = x + swap(x, n, d)
        d *= 2
    return x


def halve(near, far, n):
    q = near.astype(F32) + swap(far, n, 1).astype(F32)
    return q[0], [q[i].astype(BF16) for i in range(1, n // 2)]


def collect(total, low, n):
    for i, part in enumerate(low):
        total = total + swap(part, n, 2 * i + 2).astype(F32)
    return total


def reshard(ws, me, n):
    rows, width = ws[0].shape[1], ws[0].shape[2] // n
    count = sum(w.shape[0] for w in ws)
    out = jnp.zeros((count, n * rows, width), ws[0].dtype)
    for m in sorted(range(n), key=lambda m: -m):
        piece = jnp.concatenate([lax.dynamic_slice_in_dim(w, (me ^ m) * width, width, 2) for w in ws])
        piece = swap(piece, n, m) if m else piece
        out = lax.dynamic_update_slice_in_dim(out, piece, (me ^ m) * rows, 1)
    return out


def pack_maps(maps, n, spare=None):
    count, k, own = maps.shape
    groups = -(-count // n)
    fill = groups * n - count
    flat = [maps[i] for i in range(count)]
    if fill:
        rest = jnp.zeros((k, fill * own), maps.dtype)
        if spare is not None:
            rest = rest.at[: spare.shape[0], : spare.shape[1]].set(spare)
        flat.append(rest)
    rows = [jnp.concatenate(flat[g * n : (g + 1) * n], axis=1) for g in range(groups)]
    return jnp.concatenate(rows) if groups > 1 else rows[0]


def fill_hot(key, hot):
    n, tok = key.shape
    slot = lax.broadcasted_iota(jnp.int32, (CAP, tok), 0)
    for b in range(n):
        one = jnp.where(slot == key[b : b + 1, :], 1.0, 0.0)
        hot[b * CAP : (b + 1) * CAP, :] = one.astype(BF16)


def block_of(b, size):
    return pl.ds(pl.multiple_of(b * size, 16), size)


def fill_rows(me, hot, xs, base, rows):
    tok = hot.shape[1]
    for m, x in enumerate(xs):
        here = block_of(me[0] ^ m, CAP)
        rows[here, :] = dot_nn(hot[here, :], x[pl.ds(base, tok), :]).astype(BF16)


def fill_map(me, xs, index, out):
    n, k = len(xs), out.shape[0]
    own = out.shape[1] // n
    group, column = index // n, index % n
    for m, x in enumerate(xs):
        part = x[block_of(group, k), pl.ds(pl.multiple_of(column * own, own), own)]
        out[:, pl.ds(pl.multiple_of((me[0] ^ m) * own, own), own)] = part


def fill_select(hot, select_tok, sel):
    for b in range(select_tok.shape[0]):
        here = pl.ds(b * CAP, CAP)
        sel[here, :] = dot_nn(hot[here, :], select_tok[b])


def fill_share(hot, share, col):
    for b in range(share.shape[0]):
        here = pl.ds(b * CAP, CAP)
        one = jnp.sum(hot[here, :].astype(F32) * share[b : b + 1, :], axis=1, keepdims=True)
        col[here, :] = jnp.broadcast_to(one, (CAP, col.shape[1]))


def scatter_add(me, hot, y, acc, at):
    tok = hot.shape[1]
    n = acc.shape[0] // tok
    for b in range(n):
        mask = me[0] ^ b
        there = block_of(mask // 2 + (mask % 2) * (n // 2), tok)
        acc[there, at] += dot_tn(hot[pl.ds(b * CAP, CAP), :], y[pl.ds(b * CAP, CAP), :])


def copy_out(acc, rows, near, far, sem):
    half = acc.shape[0] // 2
    for side, ref in enumerate((near, far)):
        rows[:half, :] = acc[side * half : (side + 1) * half, :].astype(BF16)
        copy = pltpu.make_async_copy(rows.at[pl.ds(0, half)], ref, sem)
        copy.start()
        copy.wait()


def write_out(acc, near, far):
    half = acc.shape[0] // 2
    near[...] = acc[:half, :].astype(BF16).reshape(near.shape)
    far[...] = acc[half:, :].astype(BF16).reshape(far.shape)


def live_rows(staged, first, k):
    total = staged[first : first + RANK]
    for d in range(1, k // RANK):
        total = total + staged[first + d * RANK : first + (d + 1) * RANK]
    return total


def lanes(e, size):
    return pl.ds(pl.multiple_of(e * size, 128), size)


def turn(v, cos, sin):
    return v * cos + pltpu.roll(v, HD // 2, 1) * sin


def turn_heads(v, table, sign):
    cos, sin = table[:, :HD], table[:, HD:]
    heads = [turn(v[:, h : h + HD], cos, sign * sin) for h in range(0, v.shape[1], HD)]
    return heads[0] if len(heads) == 1 else jnp.concatenate(heads, axis=1)


def qkv_kernel(n, *refs):
    me, xs, refs = refs[0], refs[1 : 1 + n], refs[1 + n :]
    key, select_tok, hi, lo, w, b_in, q, kv, rank_q, rank_kv, rows_own, tok_own, a_in, *refs = refs
    hot, rows, sel, table = refs
    i = pl.program_id(0)
    tok, k = hi.shape[1], b_in.shape[0]
    own = w.shape[1]
    mine = pl.ds(pl.multiple_of(me[0] * own, own), own)
    fill_map(me, xs, i, a_in)

    @pl.when(i < EXPERTS)
    def query():
        fill_hot(key, hot)
        fill_rows(me, hot, xs, k, rows)
        fill_select(hot, select_tok, sel)
        for b in range(n):
            here = pl.ds(b * CAP, CAP)
            table[here, :] = dot_nn(hot[here, :], hi[b]) + dot_nn(hot[here, :], lo[b])
        rank = (dot_nt(rows[...], a_in[...]) * sel[...]).astype(BF16)
        rank_q[...] = rank
        pre = dot_nn(rows[...], w[...]) + dot_nn(rank, b_in[...])
        q[...] = turn_heads(pre, table[...], 1.0).astype(BF16)
        rows_own[...] = rows[:, mine]

    @pl.when(i >= EXPERTS)
    def key_value():
        group = n // 2
        some = pl.ds(0, group * tok)
        for half in range(2):
            for j in range(group):
                m = half * group + j
                b = me[0] ^ m
                here = pl.ds(j * tok, tok)
                rows[here, :] = xs[m][pl.ds(k, tok), :]
                sel[here, :] = select_tok[b].astype(F32)
                table[here, :] = hi[b].astype(F32) + lo[b].astype(F32)
            rank = (dot_nt(rows[some, :], a_in[...]) * sel[some, :]).astype(BF16)
            pre = dot_nn(rows[some, :], w[...]) + dot_nn(rank, b_in[...])
            turned = turn_heads(pre, table[some, :], 1.0)
            done = jnp.where(i == EXPERTS, turned, pre).astype(BF16)
            for j in range(group):
                there = block_of(me[0] ^ (half * group + j), tok)
                here = slice(j * tok, (j + 1) * tok)
                rank_kv[there, :] = rank[here]
                kv[there, :] = done[here]
                tok_own[there, :] = rows[here, mine]


def attend_kernel(key, begin, q, k, v, mixed, lse, scores, mx, tot, acc):
    b = pl.program_id(1)
    tok = begin.shape[1]
    rows = q.shape[0] * q.shape[1]
    slot = lax.broadcasted_iota(jnp.int32, (CAP, tok), 0)
    token = b * tok + lax.broadcasted_iota(jnp.int32, (CAP, tok), 1)
    first, last = [], []
    for e in range(EXPERTS):
        chosen = slot == key[e : e + 1, :]
        first.append(jnp.sum(jnp.where(chosen, begin[...], 0), axis=1, keepdims=True))
        last.append(jnp.sum(jnp.where(chosen, token, 0), axis=1, keepdims=True))
    first, last = jnp.concatenate(first), jnp.concatenate(last)
    query = q[...].reshape(rows, HD)
    count = (b * tok + tok + CHUNK - 1) // CHUNK
    mx[...] = jnp.full(mx.shape, NEG, F32)

    def score(j, carry):
        start = pl.multiple_of(j * CHUNK, CHUNK)
        s = dot_nt(query, k[pl.ds(start, CHUNK), :]) * HD ** (-0.5)
        at = start + lax.broadcasted_iota(jnp.int32, s.shape, 1)
        s = jnp.where((at >= first) & (at <= last), s, NEG)
        scores[:, pl.ds(start, CHUNK)] = s
        mx[...] = jnp.maximum(mx[...], jnp.maximum(s[:, :HD], s[:, HD:]))
        return carry

    lax.fori_loop(0, count, score, 0)
    top = jnp.max(mx[...], axis=1, keepdims=True)
    tot[...] = jnp.zeros(tot.shape, F32)
    acc[...] = jnp.zeros(acc.shape, F32)

    def mix(j, carry):
        start = pl.multiple_of(j * CHUNK, CHUNK)
        p = jnp.exp(scores[:, pl.ds(start, CHUNK)] - top)
        tot[...] += p[:, :HD] + p[:, HD:]
        acc[...] += dot_nn(p.astype(BF16), v[pl.ds(start, CHUNK), :])
        return carry

    lax.fori_loop(0, count, mix, 0)
    total = jnp.sum(tot[...], axis=1, keepdims=True)
    mixed[...] = (acc[...] / total).astype(BF16).reshape(mixed.shape)
    lse[...] = jnp.broadcast_to(top + jnp.log(total), (rows, HD)).reshape(lse.shape)


def attend_back_kernel(key, begin, q, g, mixed, lse, k, v, gq, gk, gv, dq):
    b = pl.program_id(1)
    tok = begin.shape[1]
    rows = q.shape[0] * q.shape[1]
    scale = HD ** (-0.5)

    @pl.when(b == 0)
    def start():
        gk[...] = jnp.zeros(gk.shape, F32)
        gv[...] = jnp.zeros(gv.shape, F32)

    slot = lax.broadcasted_iota(jnp.int32, (CAP, tok), 0)
    token = b * tok + lax.broadcasted_iota(jnp.int32, (CAP, tok), 1)
    first, last = [], []
    for e in range(EXPERTS):
        chosen = slot == key[e : e + 1, :]
        first.append(jnp.sum(jnp.where(chosen, begin[...], 0), axis=1, keepdims=True))
        last.append(jnp.sum(jnp.where(chosen, token, 0), axis=1, keepdims=True))
    first, last = jnp.concatenate(first), jnp.concatenate(last)

    def flat(r):
        return r[...].reshape(rows, HD)

    query, grad = flat(q), flat(g)
    delta = jnp.sum(flat(mixed).astype(F32) * grad.astype(F32), axis=1, keepdims=True)
    log_total = flat(lse)[:, :1]
    count = (b * tok + tok + CHUNK - 1) // CHUNK
    dq[...] = jnp.zeros(dq.shape, F32)

    def step(j, carry):
        begin_at = pl.multiple_of(j * CHUNK, CHUNK)
        here = pl.ds(begin_at, CHUNK)
        kc, vc = k[here, :], v[here, :]
        s = dot_nt(query, kc) * scale
        at = begin_at + lax.broadcasted_iota(jnp.int32, s.shape, 1)
        p = jnp.where((at >= first) & (at <= last), jnp.exp(s - log_total), 0.0)
        dp = dot_nt(grad, vc)
        ds = (p * (dp - delta)).astype(BF16)
        dq[...] += dot_nn(ds, kc)
        gk[here, :] += dot_tn(ds, query) * scale
        gv[here, :] += dot_tn(p.astype(BF16), grad)
        return carry

    lax.fori_loop(0, count, step, 0)
    gq[...] = (dq[...] * scale).reshape(gq.shape)


def out_kernel(n, first, stride, *refs):
    me, xs, refs = refs[0], refs[1 : 1 + n], refs[1 + n :]
    x, key, share, select_tok, down, w, near, far, live, maps, hot, sel, col, part, stage, acc = refs
    e = pl.program_id(0)
    k, slots = down.shape[0], x.shape[0]

    @pl.when(e == 0)
    def start():
        acc[...] = jnp.zeros(acc.shape, F32)
        stage[...] = jnp.zeros(stage.shape, F32)

    fill_map(me, xs, first + stride * e, maps)
    fill_hot(key, hot)
    fill_select(hot, select_tok, sel)
    fill_share(hot, share, col)
    rank = dot_nt(x[...], down[...]) * sel[...]
    stage[:, :k] = rank
    live[:, lanes(e, slots)] = live_rows(stage[...].T, 0, k).astype(BF16)
    rank = rank.astype(BF16)
    width = part.shape[1]
    for c in range(0, w.shape[1], width):
        at = pl.ds(c, width)
        y = dot_nn(x[...], w[:, at]) + dot_nn(rank, maps[:, at])
        part[...] = (y * col[:, :1]).astype(BF16)
        scatter_add(me, hot, part, acc, at)

    @pl.when(e == EXPERTS - 1)
    def finish():
        write_out(acc, near, far)


def back_kernel(n, first, stride, *refs):
    me, xs, ms, refs = refs[0], refs[1 : 1 + n], refs[1 + n : 1 + 2 * n], refs[1 + 2 * n :]
    key, select_tok, w, small, h, rank, rows_own, maps, hot, rows, sel = refs
    fill_map(me, ms, first + stride * pl.program_id(0), maps)
    fill_hot(key, hot)
    fill_rows(me, hot, xs, 0, rows)
    fill_select(hot, select_tok, sel)
    low = (dot_nt(rows[...], maps[...]) * sel[...]).astype(BF16)
    rank[...] = low
    h[...] = dot_nt(rows[...], w[...]) + dot_nn(low, small[...])
    rows_own[...] = rows[:, lanes(me[0], rows_own.shape[1])]


def mixed_back_kernel(n, *refs):
    me, xs, ms, refs = refs[0], refs[1 : 1 + n], refs[1 + n : 1 + 2 * n], refs[1 + 2 * n :]
    key, share, select_tok, w, small, mixed, g, a_grad, dshare, rows_own, maps, *refs = refs
    hot, rows, sel, col, stage = refs
    e = pl.program_id(0)
    fill_map(me, ms, e, maps)
    k, own, slots = small.shape[0], mixed.shape[1], mixed.shape[0]

    @pl.when(e == 0)
    def start():
        stage[...] = jnp.zeros(stage.shape, F32)

    fill_hot(key, hot)
    fill_rows(me, hot, xs, 0, rows)
    fill_select(hot, select_tok, sel)
    fill_share(hot, share, col)
    low = (dot_nt(rows[...], maps[...]) * sel[...]).astype(BF16)
    h = dot_nt(rows[...], w[...]) + dot_nn(low, small[...])
    stage[:, :1] = jnp.sum(mixed[...].astype(F32) * h, axis=1, keepdims=True)
    dshare[:, lanes(e, slots)] = stage[...].T[:8]
    g[...] = (h * col[:, :1]).astype(BF16)
    scaled = (low.astype(F32) * col[:, :k]).astype(BF16)
    a_grad[...] = dot_tn(scaled, mixed[...]).astype(BF16)
    rows_own[...] = rows[:, lanes(me[0], own)]


def feed_kernel(n, first, stride, *refs):
    me, xs, ms, refs = refs[0], refs[1 : 1 + n], refs[1 + n : 1 + 2 * n], refs[1 + 2 * n :]
    key, share, select_tok, wg, wu, hid, h, back_down, *refs = refs
    near, far, inner, live, dshare, h_grad, rows_own, *refs = refs
    hot, rows, sel, col, stage, both, gate, up, gg, gu, part, acc, sem = refs
    e = pl.program_id(0)
    k, own, slots = hid.shape[1], rows_own.shape[1], rows.shape[0]

    @pl.when(e == 0)
    def start():
        acc[...] = jnp.zeros(acc.shape, F32)
        stage[...] = jnp.zeros(stage.shape, F32)

    fill_hot(key, hot)
    fill_rows(me, hot, xs, 0, rows)
    fill_select(hot, select_tok, sel)
    fill_share(hot, share, col)
    fill_map(me, ms, first + stride * e, both.at[:k])
    fill_map(me, ms, first + stride * e + 1, both.at[k:])
    ranks = dot_nt(rows[...], both[...])
    rank_gate = (ranks[:, :k] * sel[...]).astype(BF16)
    rank_up = (ranks[:, k:] * sel[...]).astype(BF16)
    gate[...] = dot_nt(rows[...], wg[...]) + dot_nn(rank_gate, hid[0])
    up[...] = dot_nt(rows[...], wu[...]) + dot_nn(rank_up, hid[1])

    def point(b, carry):
        r = block_of(b, CAP)
        a, u, hh, s = gate[r, :], up[r, :], h[r, :], col[r, :1]
        sig = jax.nn.sigmoid(a)
        act = a * sig
        value = act * u
        inner[r, :] = value.astype(BF16)
        stage[r, 2 * k : 2 * k + 1] = jnp.sum(value * hh, axis=1, keepdims=True)
        scaled = hh * s
        gg[r, :] = (scaled * u * sig * (1.0 + a * (1.0 - sig))).astype(BF16)
        gu[r, :] = (scaled * act).astype(BF16)
        return carry

    lax.fori_loop(0, slots // CAP, point, 0)
    stage[:, :k] = dot_nt(gg[...], hid[0]) * sel[...]
    stage[:, k : 2 * k] = dot_nt(gu[...], hid[1]) * sel[...]
    staged = stage[...].T
    live[:RANK, lanes(e, slots)] = live_rows(staged, 0, k).astype(BF16)
    live[RANK:, lanes(e, slots)] = live_rows(staged, k, k).astype(BF16)
    dshare[:, lanes(e, slots)] = staged[2 * k : 2 * k + 8]
    h_grad[0] = dot_tn(rank_gate, gg[...]).astype(BF16)
    h_grad[1] = dot_tn(rank_up, gu[...]).astype(BF16)
    scaled = (back_down[...].astype(F32) * col[:, :k]).astype(BF16)
    h_grad[2] = dot_tn(scaled, inner[...]).astype(BF16)
    rows_own[...] = rows[:, lanes(me[0], own)]
    back = stage[:, : 2 * k].astype(BF16)
    width = part.shape[1]
    for c in range(0, wg.shape[1], width):
        at = pl.ds(c, width)
        y = dot_nn(gg[...], wg[:, at]) + dot_nn(gu[...], wu[:, at]) + dot_nn(back, both[:, at])
        part[...] = y.astype(BF16)
        scatter_add(me, hot, part, acc, at)

    @pl.when(e == EXPERTS - 1)
    def finish():
        copy_out(acc, rows, near, far, sem)


def qkv_back_kernel(n, *refs):
    me, xs, refs = refs[0], refs[1 : 1 + n], refs[1 + n :]
    key, select_tok, hi, lo, w, b_in, gq, gk, gv, rank_q, rank_kv, near, far, live, b_grad, *refs = refs
    maps, hot, sel, table, part, stage, acc, some_g = refs
    i = pl.program_id(0)
    tok, k = hi.shape[1], b_in.shape[0]
    slots, wide = gq.shape[0], maps.shape[1]
    seq = n * tok
    width = part.shape[1]
    fill_map(me, xs, i, maps)

    @pl.when(i == 0)
    def start():
        acc[...] = jnp.zeros(acc.shape, F32)
        stage[...] = jnp.zeros(stage.shape, F32)

    @pl.when(i < EXPERTS)
    def query():
        fill_hot(key, hot)
        fill_select(hot, select_tok, sel)
        for b in range(n):
            here = pl.ds(b * CAP, CAP)
            table[here, :] = dot_nn(hot[here, :], hi[b]) + dot_nn(hot[here, :], lo[b])
        g = turn_heads(gq[...], table[...], -1.0).astype(BF16)
        rank = dot_nt(g, b_in[...]) * sel[...]
        stage[:slots, :k] = rank
        live[:, lanes(i, slots)] = live_rows(stage[:slots, :].T, 0, k).astype(BF16)
        b_grad[...] = dot_tn(rank_q[...], g).astype(BF16)
        rank = rank.astype(BF16)
        for c in range(0, wide, width):
            at = pl.ds(c, width)
            y = dot_nt(g, w[at, :]) + dot_nn(rank, maps[:, at])
            part[...] = y.astype(BF16)
            scatter_add(me, hot, part, acc, at)

    @pl.when(i >= EXPERTS)
    def key_value():
        group = n // 2
        size = group * tok
        some = pl.ds(0, size)
        total = jnp.zeros(b_grad.shape, F32)
        for half in range(2):
            there = pl.ds(half * size, size)
            for j in range(group):
                b = me[0] ^ (2 * j + half)
                here = pl.ds(j * tok, tok)
                sel[here, :] = select_tok[b].astype(F32)
                both = hi[b].astype(F32) + lo[b].astype(F32)
                turned = turn_heads(gk[block_of(b, tok), :], both, -1.0)
                some_g[here, :] = jnp.where(i == EXPERTS, turned, gv[block_of(b, tok), :]).astype(BF16)
                total = total + dot_tn(rank_kv[block_of(b, tok), :], some_g[here, :])
            g = some_g[...]
            rank = dot_nt(g, b_in[...]) * sel[some, :]
            for j in range(group):
                stage[block_of(me[0] ^ (2 * j + half), tok), :k] = rank[j * tok : (j + 1) * tok]
            rank = rank.astype(BF16)
            for c in range(0, wide, width):
                at = pl.ds(c, width)
                acc[there, at] += dot_nt(g, w[at, :]) + dot_nn(rank, maps[:, at])
        b_grad[...] = total.astype(BF16)
        begin = EXPERTS * slots + (i - EXPERTS) * seq
        there = pl.ds(pl.multiple_of(begin, 128), seq)
        live[:, there] = live_rows(stage[:seq, :].T, 0, k).astype(BF16)

    @pl.when(i == EXPERTS + 1)
    def finish():
        write_out(acc, near, far)


def chunk_of(slots, wide):
    width = wide // 2
    while slots * width > 640 * 1024:
        width //= 2
    return width


def whole(shape):
    zeros = (0,) * len(shape)
    return pl.BlockSpec(shape, lambda *at: zeros, pipeline_mode=pl.Buffered(1))


def by_expert(shape, at=lambda i: i):
    rest = (0,) * len(shape)
    return pl.BlockSpec((None,) + shape, lambda i, *unused: (at(i),) + rest)


def shaped(shape, dtype):
    return jax.ShapeDtypeStruct(shape, dtype)


def run(kernel, name, steps, ins, outs, scratch, args, flops, scalars=1):
    call = pl.pallas_call(
        kernel,
        grid_spec=pltpu.PrefetchScalarGridSpec(
            num_scalar_prefetch=scalars,
            grid=steps,
            in_specs=ins,
            out_specs=[o[0] for o in outs],
            scratch_shapes=[pltpu.VMEM(*one) if isinstance(one, tuple) else one for one in scratch],
        ),
        out_shape=[shaped(o[1], o[2]) for o in outs],
        compiler_params=pltpu.CompilerParams(vmem_limit_bytes=62 << 20),
        cost_estimate=pl.CostEstimate(
            flops=int(flops), bytes_accessed=32 << 20, transcendentals=1 << 20
        ),
        name=name,
    )
    return call(*args)


def last_expert(i):
    return jnp.minimum(i, EXPERTS - 1)


def from_expert(i):
    return jnp.maximum(i - EXPERTS, 0)


def rows_spec(x, rows=None):
    return whole((x.shape[0] if rows is None else rows, x.shape[1]))


def sides(n, tok, wide):
    shape = (n // 2, tok, wide)
    return [(whole(shape), shape, BF16)] * 2


def qkv(me, pieces, key, select_tok, hi, lo, w, b_in):
    n, tok, k = select_tok.shape
    wide, own, slots, seq = pieces[0].shape[1], w.shape[2], n * CAP, n * tok
    return run(
        partial(qkv_kernel, n),
        "qkv",
        (EXPERTS + 2,),
        [rows_spec(p) for p in pieces]
        + [by_expert((n, tok), last_expert), whole(select_tok.shape), whole(hi.shape),
           whole(lo.shape), by_expert((wide, own)), by_expert((k, own))],
        [
            (by_expert((slots, own), last_expert), (EXPERTS, slots, own), BF16),
            (by_expert((seq, own), from_expert), (2, seq, own), BF16),
            (by_expert((slots, k), last_expert), (EXPERTS, slots, k), BF16),
            (by_expert((seq, k), from_expert), (2, seq, k), BF16),
            (by_expert((slots, own), last_expert), (EXPERTS, slots, own), BF16),
            (whole((seq, own)), (seq, own), BF16),
        ],
        [((k, wide), BF16), ((slots, tok), BF16), ((max(slots, seq // 2), wide), BF16),
         ((max(slots, seq // 2), k), F32), ((max(slots, seq // 2), 2 * HD), F32)],
        (me, *pieces, key, select_tok, hi, lo, w, b_in),
        2 * wide * own * (EXPERTS * slots + 2 * seq) * 1.5,
    )


def attend(key, begin, q, k, v):
    n, tok = begin.shape[0], begin.shape[2]
    own, seq, rows = q.shape[2], n * tok, EXPERTS * CAP
    slot_spec = pl.BlockSpec((EXPERTS, None, CAP, HD), lambda h, b: (0, b, 0, h))
    all_spec = pl.BlockSpec((seq, HD), lambda h, b: (0, h))
    shape = (EXPERTS, n, CAP, own)
    mixed, lse = run(
        attend_kernel,
        "attend",
        (own // HD, n),
        [pl.BlockSpec((None, EXPERTS, tok), lambda h, b: (b, 0, 0)),
         pl.BlockSpec((None, 1, tok), lambda h, b: (b, 0, 0)), slot_spec, all_spec, all_spec],
        [(slot_spec, shape, BF16), (slot_spec, shape, F32)],
        [((rows, seq + CHUNK), F32), ((rows, HD), F32), ((rows, HD), F32), ((rows, HD), F32)],
        (key, begin, q.reshape(shape), k, v),
        3 * rows * seq * own * n,
        0,
    )
    return mixed.reshape(q.shape), lse


def attend_back(key, begin, q, g, mixed, lse, k, v):
    n, tok = begin.shape[0], begin.shape[2]
    own, seq, rows = q.shape[2], n * tok, EXPERTS * CAP
    slot_spec = pl.BlockSpec((EXPERTS, None, CAP, HD), lambda h, b: (0, b, 0, h))
    all_spec = pl.BlockSpec((seq, HD), lambda h, b: (0, h))
    shape = (EXPERTS, n, CAP, own)
    gq, gk, gv = run(
        attend_back_kernel,
        "attend_back",
        (own // HD, n),
        [pl.BlockSpec((None, EXPERTS, tok), lambda h, b: (b, 0, 0)),
         pl.BlockSpec((None, 1, tok), lambda h, b: (b, 0, 0)),
         slot_spec, slot_spec, slot_spec, slot_spec, all_spec, all_spec],
        [(slot_spec, shape, F32), (all_spec, (seq, own), F32), (all_spec, (seq, own), F32)],
        [((rows, HD), F32)],
        (key, begin, q.reshape(shape), g.reshape(shape), mixed.reshape(shape), lse, k, v),
        7 * rows * seq * own * n,
        0,
    )
    return gq.reshape(q.shape), gk, gv


def weight_spec(w, p=None):
    if p is None:
        return by_expert(w.shape[1:])
    return pl.BlockSpec((None, None) + w.shape[2:], lambda e, *unused: (e, p, 0, 0))


def project_out(name, me, x, key, share, select_tok, down, w, pieces, groups, first, stride, p=None):
    n, tok, k = select_tok.shape
    wide, slots, deep = pieces[0].shape[1], n * CAP, x.shape[2]
    down_spec = by_expert((k, deep)) if p is None else weight_spec(down, p)
    return run(
        partial(out_kernel, n, first, stride),
        name,
        (EXPERTS,),
        [rows_spec(m, groups * k) for m in pieces]
        + [by_expert((slots, deep)), by_expert((n, tok)), by_expert((n, tok)), whole(select_tok.shape),
           down_spec, weight_spec(w, p)],
        sides(n, tok, wide) + [(whole((RANK, EXPERTS * slots)), (RANK, EXPERTS * slots), BF16)],
        [((k, wide), BF16), ((slots, tok), BF16), ((slots, k), F32), ((slots, 128), F32),
         ((slots, chunk_of(slots, wide)), BF16), ((slots, 128), F32), ((n * tok, wide), F32)],
        (me, *pieces, x, key, share, select_tok, down, w),
        2 * wide * deep * EXPERTS * slots * 1.5,
    )


def feed_back_down(me, tokens, pieces, groups, first, stride, key, select_tok, w, small):
    n, tok, k = select_tok.shape
    wide, slots, deep = pieces[0].shape[1], n * CAP, w.shape[2]
    own = wide // n
    return run(
        partial(back_kernel, n, first, stride),
        "feed_down_back",
        (EXPERTS,),
        [rows_spec(m) for m in tokens] + [rows_spec(m, groups * k) for m in pieces]
        + [by_expert((n, tok)), whole(select_tok.shape), weight_spec(w, 2), weight_spec(small, 2)],
        [(by_expert((slots, deep)), (EXPERTS, slots, deep), F32),
         (by_expert((slots, k)), (EXPERTS, slots, k), BF16),
         (by_expert((slots, own)), (EXPERTS, slots, own), BF16)],
        [((k, wide), BF16), ((slots, tok), BF16), ((slots, wide), BF16), ((slots, k), F32)],
        (me, *tokens, *pieces, key, select_tok, w, small),
        2 * wide * deep * EXPERTS * slots * 1.3,
    )


def mixed_back(me, tokens, pieces, groups, key, share, select_tok, w, small, mixed):
    n, tok, k = select_tok.shape
    wide, slots, own = pieces[0].shape[1], n * CAP, w.shape[1]
    return run(
        partial(mixed_back_kernel, n),
        "mixed_back",
        (EXPERTS,),
        [rows_spec(m) for m in tokens] + [rows_spec(m, groups * k) for m in pieces]
        + [by_expert((n, tok)), by_expert((n, tok)), whole(select_tok.shape),
           weight_spec(w), by_expert((k, own)), by_expert((slots, own))],
        [(by_expert((slots, own)), (EXPERTS, slots, own), BF16),
         (by_expert((k, own)), (EXPERTS, k, own), BF16),
         (whole((8, EXPERTS * slots)), (8, EXPERTS * slots), F32),
         (by_expert((slots, own)), (EXPERTS, slots, own), BF16)],
        [((k, wide), BF16), ((slots, tok), BF16), ((slots, wide), BF16), ((slots, k), F32),
         ((slots, 128), F32), ((slots, 128), F32)],
        (me, *tokens, *pieces, key, share, select_tok, w, small, mixed),
        2 * wide * own * EXPERTS * slots * 1.5,
    )


def feed(me, tokens, pieces, groups, first, stride, key, share, select_tok, w, hid, h, back_down):
    n, tok, k = select_tok.shape
    wide, slots, deep = pieces[0].shape[1], n * CAP, w.shape[2]
    own = wide // n
    return run(
        partial(feed_kernel, n, first, stride),
        "feed",
        (EXPERTS,),
        [rows_spec(m) for m in tokens] + [rows_spec(m, groups * k) for m in pieces]
        + [by_expert((n, tok)), by_expert((n, tok)),
           whole(select_tok.shape), weight_spec(w, 0), weight_spec(w, 1), by_expert((3, k, deep)),
           by_expert((slots, deep)), by_expert((slots, k))],
        [(pl.BlockSpec(memory_space=pl.ANY), (n // 2 * tok, wide), BF16)] * 2
        + [(by_expert((slots, deep)), (EXPERTS, slots, deep), BF16),
           (whole((2 * RANK, EXPERTS * slots)), (2 * RANK, EXPERTS * slots), BF16),
           (whole((8, EXPERTS * slots)), (8, EXPERTS * slots), F32),
           (by_expert((3, k, deep)), (EXPERTS, 3, k, deep), BF16),
           (by_expert((slots, own)), (EXPERTS, slots, own), BF16)],
        [((slots, tok), BF16), ((slots, wide), BF16), ((slots, k), F32), ((slots, 128), F32),
         ((slots, 128), F32), ((2 * k, wide), BF16), ((slots, deep), F32), ((slots, deep), F32),
         ((slots, deep), BF16), ((slots, deep), BF16), ((slots, chunk_of(slots, wide)), BF16),
         ((n * tok, wide), F32), pltpu.SemaphoreType.DMA],
        (me, *tokens, *pieces, key, share, select_tok, w, w, hid, h, back_down),
        8 * wide * deep * EXPERTS * slots * 1.3,
    )


def qkv_back(me, pieces, key, select_tok, hi, lo, w, b_in, gq, gk, gv, rank_q, rank_kv):
    n, tok, k = select_tok.shape
    wide, own, slots, seq = pieces[0].shape[1], w.shape[2], n * CAP, n * tok
    total = EXPERTS * slots + 2 * seq
    most = max(slots, seq // 2)
    return run(
        partial(qkv_back_kernel, n),
        "qkv_back",
        (EXPERTS + 2,),
        [rows_spec(m, k) for m in pieces]
        + [by_expert((n, tok), last_expert), whole(select_tok.shape), whole(hi.shape),
           whole(lo.shape), by_expert((wide, own)), by_expert((k, own)),
           by_expert((slots, own), last_expert), whole((seq, own)), whole((seq, own)),
           by_expert((slots, k), last_expert), by_expert((seq, k), from_expert)],
        sides(n, tok, wide)
        + [(whole((RANK, total)), (RANK, total), BF16),
           (by_expert((k, own)), (EXPERTS + 2, k, own), BF16)],
        [((k, wide), BF16), ((slots, tok), BF16), ((most, k), F32), ((slots, 2 * HD), F32),
         ((slots, chunk_of(slots, wide)), BF16), ((max(slots, seq), 128), F32), ((seq, wide), F32),
         ((seq // 2, own), BF16)],
        (me, *pieces, key, select_tok, hi, lo, w, b_in, gq, gk, gv, rank_q, rank_kv),
        2 * wide * own * (EXPERTS * slots + 2 * seq) * 1.5,
    )


def members(routes):
    names = jnp.arange(EXPERTS, dtype=jnp.int32)[None, :, None]
    member = (routes[:, :1] == names) | (routes[:, 1:] == names)
    tok = routes.shape[-1]
    before = (jnp.arange(tok)[:, None] < jnp.arange(tok)[None, :]).astype(BF16)
    rank = ein("met,tu->meu", member.astype(BF16), before).astype(jnp.int32)
    return jnp.where(member, rank, -1)


def own_shares(normed, router, routes):
    names = jnp.arange(EXPERTS, dtype=jnp.int32)[:, None]
    member = (routes[:1] == names) | (routes[1:] == names)
    logits = ein("td,de->et", normed, router)
    return jax.nn.softmax(jnp.where(member, logits, -jnp.inf), axis=0)


def route_back(share, grad_share, router):
    grad = share * (grad_share - jnp.sum(share * grad_share, axis=0, keepdims=True))
    return jnp.einsum("et,de->td", grad, router.astype(F32), precision=lax.Precision.HIGHEST)


def local(
    n,
    reps,
    layer_input_state,
    cotangent,
    norm_gain_vectors,
    attention_router_weight,
    feed_router_weight,
    attention_query_weight,
    key_value_weight,
    attention_output_weight,
    feed_expert_weight,
    attention_adapters,
    feed_adapter_width,
    feed_adapter_hidden,
    token_document,
    document_adapter,
    attention_expert_pairs,
    feed_expert_pairs,
):
    tok, wide = layer_input_state.shape
    own, slots = wide // n, n * CAP
    columns = attention_adapters.shape[3]
    me = lax.axis_index("shard")
    me_ref = me.reshape(1).astype(jnp.int32)
    segments = token_document[0]
    seq = segments.shape[0]
    docs = document_adapter[0]
    doc_count = docs.shape[0]
    k = doc_count * RANK

    def one_hot(which):
        at = which[:, None] * RANK + jnp.arange(RANK)[None, :]
        return (at.reshape(-1)[:, None] == jnp.arange(columns)[None, :]).astype(BF16)

    pick = one_hot(docs)
    attn_small = ein("kc,pmwc->pmkw", pick, attention_adapters).astype(BF16)
    width_small = ein("kc,pmwc->pmkw", pick, feed_adapter_width).astype(BF16)
    hidden_small = ein("kc,epcf->epkf", pick, feed_adapter_hidden).astype(BF16)
    b_in, a_out = attn_small[1, : EXPERTS + 2], attn_small[0, EXPERTS + 2 :]

    x = layer_input_state.astype(F32)
    gain_one = norm_gain_vectors[0].astype(F32)
    gain_two = norm_gain_vectors[1].astype(F32)
    normed_own = rms_norm(gain_one, x).astype(BF16)
    routes = jnp.concatenate([attention_expert_pairs.T, feed_expert_pairs.T])
    own_a = own_shares(normed_own, attention_router_weight, routes[:2])
    own_hi = own_a.astype(BF16)
    own_lo = (own_a - lax.reduce_precision(own_a, 8, 7)).astype(BF16)
    spare = jnp.stack([routes.astype(BF16).reshape(-1), own_hi.reshape(-1), own_lo.reshape(-1)])
    first = jnp.concatenate([pack_maps(attn_small[0, : EXPERTS + 2], n, spare), normed_own])
    weights = [attention_query_weight, key_value_weight]
    if n == 8:
        cut = (first.shape[0] // 2 + 15) // 16 * 16
        y0, x1 = swap(first[:cut], n, 4), swap(first[cut:], n, 2)
        y1, x0 = swap(first[cut:], n, 4), swap(first[:cut], n, 2)
        y0, x1, *weights = tie(y0, x1, *weights)
        d0, d1 = swap(y0, n, 2), swap(x1, n, 4)
        chips = {0: first}
        for m, p in ((2, (x0, x1)), (4, (y0, y1)), (6, (d0, d1))):
            chips[m] = jnp.concatenate(p)
    else:
        chips = across(first, n)
    pieces = from_sibling(chips, n)
    w_in = reshard(weights, me, n)

    facts = jnp.stack([p[:3, (EXPERTS + 2) * own : (EXPERTS + 2) * own + EXPERTS * tok] for p in pieces])
    facts = facts[jnp.arange(n) ^ me].reshape(n, 3, EXPERTS, tok)
    routes = facts[:, 0].astype(jnp.int32)
    share_a = facts[:, 1].astype(F32) + facts[:, 2].astype(F32)

    second = jnp.concatenate([attn_small[1, EXPERTS + 2 :], width_small.reshape(-1, k, own)])
    groups = -(-second.shape[0] // n)
    second, cotangent_sent, w_in = tie(pack_maps(second, n), cotangent, w_in)
    map_chips, cotangent_chips = across(second, n), across(cotangent_sent, n)

    begins = jnp.sum((segments[None, :] < jnp.arange(doc_count)[:, None]).astype(jnp.int32), axis=1)
    doc = segments.reshape(n, tok)
    place = jnp.arange(seq, dtype=jnp.int32).reshape(n, tok)
    doc_table = doc[None] == jnp.arange(doc_count, dtype=jnp.int32)[:, None, None]
    begin = jnp.sum(jnp.where(doc_table, begins[:, None, None], 0), axis=0)
    freq = jnp.exp(-jnp.arange(HD // 2, dtype=F32) * (2.0 * math.log(10000.0) / HD))
    angles = (place - begin).astype(F32)[..., None] * freq
    cos, sin = jnp.cos(angles), jnp.sin(angles)
    table = jnp.concatenate([cos, cos, -sin, sin], axis=-1)
    table_hi = table.astype(BF16)
    table_lo = (table - lax.reduce_precision(table, 8, 7)).astype(BF16)
    chosen_doc = jnp.arange(k, dtype=jnp.int32)[None, None, :] // RANK
    select_tok = (doc[:, :, None] == chosen_doc).astype(BF16)
    select_row = doc_table.astype(F32).reshape(1, doc_count, seq)

    slot_a, slot_f = members(routes[:, :2]), members(routes[:, 2:])
    routes_f_own = feed_expert_pairs.T
    key_a, key_f = slot_a.transpose(1, 0, 2), slot_f.transpose(1, 0, 2)

    def slot_select(slot):
        hot = slot[:, :, None, :] == jnp.arange(CAP, dtype=jnp.int32)[None, None, :, None]
        chose = hot[:, :, None] & doc_table.transpose(1, 0, 2)[:, None, :, None, :]
        select = jnp.any(chose, axis=-1).astype(F32)
        return select.transpose(1, 2, 0, 3).reshape(EXPERTS, doc_count, slots)

    select_a, select_f = slot_select(slot_a), slot_select(slot_f)

    share_ae = share_a.transpose(1, 0, 2)
    q, kv, rank_q, rank_kv, rows_a_own, normed_own_columns = qkv(
        me_ref, pieces, key_a, select_tok, table_hi, table_lo, w_in, b_in
    )
    q, *sent = tie(q, *map_chips.values())
    maps = from_sibling(dict(zip(map_chips, sent)), n)
    mixed, lse = attend(slot_a, begin[:, None], q, kv[0], kv[1])
    mixed, *sent = tie(mixed, *cotangent_chips.values())
    grads_out_all = from_sibling(dict(zip(cotangent_chips, sent)), n)
    near, far, live_o = project_out(
        "attend_out", me_ref, mixed, key_a, share_ae, select_tok, a_out, attention_output_weight, maps, groups, 0, 1
    )
    attn_total, attn_low = halve(near, far, n)
    *attn_low, key_late = tie(*attn_low, key_f)

    w_feed = jnp.swapaxes(feed_expert_weight, 2, 3)
    grad_inner, back_down, rows_g_own = feed_back_down(
        me_ref, grads_out_all, maps, groups, EXPERTS + 2, 3, key_late, select_tok, w_feed, hidden_small
    )
    attn_total, grad_inner = tie(attn_total, grad_inner)
    attended = x + collect(attn_total, attn_low, n)
    normed_two_own = rms_norm(gain_two, attended).astype(BF16)
    normed_two = from_sibling(across(normed_two_own, n), n)
    own_f = own_shares(normed_two_own, feed_router_weight, routes_f_own)
    share_f = gather_small(own_f, me, n)
    share_fe = share_f.transpose(1, 0, 2)
    near, far, inner, live_f, dshare_f, hidden_grad, rows_f_own = feed(
        me_ref, normed_two, maps, groups, EXPERTS, 3, key_f, share_fe, select_tok, w_feed, hidden_small,
        grad_inner, back_down,
    )
    near, far = near.reshape(n // 2, tok, wide), far.reshape(n // 2, tok, wide)
    two_total, two_low = halve(near, far, n)
    *two_low, inner, dshare_f, docs_sent = tie(*two_low, inner, dshare_f, docs)
    near, far, live_d = project_out(
        "feed_out", me_ref, inner, key_f, share_fe, select_tok, hidden_small, w_feed, maps, groups, EXPERTS + 2, 3, 2
    )
    grad_two_own = collect(two_total, two_low, n)

    def own_tokens(slot, dshare):
        mine = lax.dynamic_slice_in_dim(dshare.reshape(EXPERTS, n, CAP), me, 1, 1)[:, 0]
        hot = lax.dynamic_slice_in_dim(slot, me, 1, 0)[0][:, None, :] == jnp.arange(CAP)[None, :, None]
        return jnp.sum(jnp.where(hot, mine[:, :, None], 0.0), axis=1)

    dshare_f = sum_small(dshare_f, n)[:1]
    grad_two_own = grad_two_own + route_back(own_f, own_tokens(slot_f, dshare_f), feed_router_weight)
    grad_attended = cotangent.astype(F32) + rms_back(attended, gain_two, grad_two_own)

    grad_sent, near, far = tie(grad_attended.astype(BF16), near, far)
    out_total, out_low = halve(near, far, n)
    chips = across(grad_sent, n)
    out_total, *sent = tie(out_total, *out_low, *chips.values())
    out_low, sent = sent[: n // 2 - 1], sent[n // 2 - 1 :]
    grads_two = from_sibling(dict(zip(chips, sent)), n)
    grad_mixed, a_out_grad, dshare_a, rows_ga_own = mixed_back(
        me_ref, grads_two, maps, groups, key_a, share_ae, select_tok, attention_output_weight, a_out, mixed
    )
    live_f, live_o = lax.psum((jnp.concatenate([live_f, live_d]), live_o), "shard")
    grad_mixed, *out_low = tie(grad_mixed, *out_low)
    gq, gk, gv = attend_back(slot_a, begin[:, None], q, grad_mixed, mixed, lse, kv[0], kv[1])
    gq, live_f, live_o = tie(gq, live_f, live_o)
    layer_out = attended + collect(out_total, out_low, n)
    near, far, live_in, b_in_grad = qkv_back(
        me_ref, pieces, key_a, select_tok, table_hi, table_lo, w_in, b_in, gq, gk, gv, rank_q, rank_kv
    )
    in_total, in_low = halve(near, far, n)
    *in_low, dshare_a, live_in, b_in_grad = tie(*in_low, dshare_a, live_in, b_in_grad)
    grad_normed = collect(in_total, in_low, n)
    dshare_a = sum_small(dshare_a, n)[:1]
    grad_normed = grad_normed + route_back(own_a, own_tokens(slot_a, dshare_a), attention_router_weight)
    grad_in = grad_attended + rms_back(x, gain_one, grad_normed)

    def spread(live, select):
        both = live.astype(F32)[:, None] * select[:, :, None, :]
        return both.reshape(live.shape[0], k, live.shape[2]).astype(BF16)

    def of_slots(live):
        return live.reshape(RANK, EXPERTS, slots).transpose(1, 0, 2)

    def grads(rank, rows):
        return ein("eks,esw->ekw", rank, rows).astype(BF16)

    def slot_row(share, slot):
        hot = slot[:, :, None, :] == jnp.arange(CAP, dtype=jnp.int32)[None, None, :, None]
        row = jnp.sum(jnp.where(hot, share[:, :, None, :], 0.0), axis=-1)
        return row.transpose(1, 0, 2).reshape(EXPERTS, 1, slots)

    scaled_f, scaled_a = select_f * slot_row(share_f, slot_f), select_a * slot_row(share_a, slot_a)
    width_grad = jnp.stack(
        [
            grads(spread(of_slots(live_f[:RANK]), select_f), rows_f_own),
            grads(spread(of_slots(live_f[RANK : 2 * RANK]), select_f), rows_f_own),
            grads(spread(of_slots(live_f[2 * RANK :]), scaled_f), rows_g_own),
        ],
        axis=1,
    )
    b_out_grad = grads(spread(of_slots(live_o), scaled_a), rows_ga_own)
    live_in = sum_small(live_in, n)
    live_kv = live_in[:, EXPERTS * slots :].reshape(RANK, 2, seq).transpose(1, 0, 2)
    a_in_grad = jnp.concatenate(
        [
            grads(spread(of_slots(live_in[:, : EXPERTS * slots]), select_a), rows_a_own),
            ein("pks,sw->pkw", spread(live_kv, select_row), normed_own_columns).astype(BF16),
        ]
    )

    def all_streams(g):
        mine = lax.axis_index("rep")
        out = lax.dynamic_update_slice_in_dim(jnp.zeros((reps,) + g.shape, g.dtype), g[None], mine, 0)
        for d in range(1, reps):
            got = lax.ppermute(g, "rep", [(i, i ^ d) for i in range(reps)])
            out = lax.dynamic_update_slice_in_dim(out, got[None], mine ^ d, 0)
        return out

    picks = jax.vmap(one_hot)(all_streams(docs_sent))
    hidden_out = ein("rpekf,rkc->pecf", lax.all_gather(hidden_grad, "rep"), picks)
    width_out = ein("rpmkw,rkc->pmwc", lax.all_gather(width_grad, "rep"), picks)
    early = all_streams(jnp.concatenate([a_out_grad, b_out_grad]))
    late_b, late_a = all_streams(b_in_grad), all_streams(a_in_grad)
    attn = jnp.concatenate([late_a, early[:, :EXPERTS], late_b, early[:, EXPERTS:]], axis=1)
    attn = attn.reshape(reps, 2, -1, k, own)
    attn_out = ein("rpmkw,rkc->pmwc", attn, picks)
    return (layer_out, grad_in, attn_out, width_out, hidden_out)


def solution(mesh):
    in_specs = (
        P(("rep", "shard"), None),
        P(("rep", "shard"), None),
        P(),
        P(),
        P(),
        P(None, "shard", None),
        P(None, "shard", None),
        P(None, "shard", None),
        P(None, None, None, "shard"),
        P(None, None, "shard", None),
        P(None, None, "shard", None),
        P(None, None, None, "shard"),
        P("rep", None),
        P("rep", None),
        P(("rep", "shard"), None),
        P(("rep", "shard"), None),
    )
    out_specs = (
        P(("rep", "shard"), None),
        P(("rep", "shard"), None),
        P(None, None, "shard", None),
        P(None, None, "shard", None),
        P(None, None, None, "shard"),
    )
    body = partial(local, mesh.shape["shard"], mesh.shape["rep"])
    return jax.shard_map(body, mesh=mesh, in_specs=in_specs, out_specs=out_specs, check_vma=False)
```

```python
from functools import partial
import math

import jax
import jax.numpy as jnp
from jax import lax
from jax.experimental import pallas as pl
from jax.experimental.pallas import tpu as pltpu
from jax.sharding import PartitionSpec as P

HD = 128
RANK = 16
CAP = 80
EXPERTS = 4
CHUNK = 256
EPS = 1e-05
NEG = -1e30
F32 = jnp.float32
BF16 = jnp.bfloat16


def ein(spec, a, b):
    return jnp.einsum(spec, a, b, preferred_element_type=F32)


def rms_norm(gain, values):
    return values * lax.rsqrt(jnp.mean(values * values, axis=-1, keepdims=True) + EPS) * gain


def rms_back(values, gain, grad):
    unused, backward_function = jax.vjp(partial(rms_norm, gain), values)
    return backward_function(grad)[0]


NT = (((1,), (1,)), ((), ()))
TN = (((0,), (0,)), ((), ()))


def dot_nt(a, b):
    return lax.dot_general(a, b, NT, preferred_element_type=F32)


def dot_tn(a, b):
    return lax.dot_general(a, b, TN, preferred_element_type=F32)


def dot_nn(a, b):
    return jnp.dot(a, b, preferred_element_type=F32)


def swap(x, n, d):
    return lax.ppermute(x, "shard", [(i, i ^ d) for i in range(n)])


def tie(*values):
    return lax.optimization_barrier(values)


def across(x, n):
    return {d: swap(x, n, d) if d else x for d in range(0, n, 2)}


def from_sibling(pieces, n):
    other = {m ^ 1: swap(p, n, 1) for m, p in pieces.items()}
    return [p for unused, p in sorted({**pieces, **other}.items())]


def gather_small(x, me, n):
    mine = jnp.stack(list(across(x, n).values()))
    mask = jnp.arange(n) ^ me
    return jnp.concatenate([mine, swap(mine, n, 1)])[mask // 2 + mask % 2 * (n // 2)]


def sum_small(x, n):
    d = 1
    while d < n:
        x = x + swap(x, n, d)
        d *= 2
    return x


def halve(near, far, n):
    q = near.astype(F32) + swap(far, n, 1).astype(F32)
    return q[0], [q[i].astype(BF16) for i in range(1, n // 2)]


def added(parts):
    return sum([part.astype(F32) for part in parts[1:]], parts[0].astype(F32))


def quarter(near, far, n):
    q = near.astype(F32) + swap(far, n, 1).astype(F32)
    cut = q.shape[1] // 2
    qa, qb = q[:, :cut], q[:, cut:]
    sent = [jnp.stack([qa[1], qa[3]]).astype(BF16), jnp.stack([qb[2], qb[3]]).astype(BF16)]
    return [qa[0], qa[2], qb[0], qb[1]], sent


def collect_quarters(kept, got, n):
    a0, a2, b0, b1 = kept
    ra, rb = got[0].astype(F32), got[1].astype(F32)
    a2, b1 = (a2 + ra[1]).astype(BF16), (b1 + rb[1]).astype(BF16)
    a0 = a0 + ra[0] + swap(a2, n, 4).astype(F32)
    b0 = b0 + rb[0] + swap(b1, n, 2).astype(F32)
    return jnp.concatenate([a0, b0])


def collect(total, low, n):
    for i, part in enumerate(low):
        total = total + swap(part, n, 2 * i + 2).astype(F32)
    return total


def reshard(ws, me, n):
    rows, width = ws[0].shape[1], ws[0].shape[2] // n
    count = sum(w.shape[0] for w in ws)
    out = jnp.zeros((count, n * rows, width), ws[0].dtype)
    for m in sorted(range(n), key=lambda m: -m):
        piece = jnp.concatenate([lax.dynamic_slice_in_dim(w, (me ^ m) * width, width, 2) for w in ws])
        piece = swap(piece, n, m) if m else piece
        out = lax.dynamic_update_slice_in_dim(out, piece, (me ^ m) * rows, 1)
    return out


def pack_maps(maps, n, spare=None):
    count, k, own = maps.shape
    groups = -(-count // n)
    fill = groups * n - count
    flat = [maps[i] for i in range(count)]
    if fill:
        rest = jnp.zeros((k, fill * own), maps.dtype)
        if spare is not None:
            rest = rest.at[: spare.shape[0], : spare.shape[1]].set(spare)
        flat.append(rest)
    rows = [jnp.concatenate(flat[g * n : (g + 1) * n], axis=1) for g in range(groups)]
    return jnp.concatenate(rows) if groups > 1 else rows[0]


def fill_hot(key, hot):
    n, tok = key.shape
    slot = lax.broadcasted_iota(jnp.int32, (CAP, tok), 0)
    for b in range(n):
        one = jnp.where(slot == key[b : b + 1, :], 1.0, 0.0)
        hot[b * CAP : (b + 1) * CAP, :] = one.astype(BF16)


def block_of(b, size):
    return pl.ds(pl.multiple_of(b * size, 16), size)


def fill_rows(me, hot, xs, base, rows):
    tok = hot.shape[1]
    for m, x in enumerate(xs):
        here = block_of(me[0] ^ m, CAP)
        rows[here, :] = dot_nn(hot[here, :], x[pl.ds(base, tok), :]).astype(BF16)


def fill_map(me, xs, index, out):
    n, k = len(xs), out.shape[0]
    own = out.shape[1] // n
    group, column = index // n, index % n
    for m, x in enumerate(xs):
        part = x[block_of(group, k), pl.ds(pl.multiple_of(column * own, own), own)]
        out[:, pl.ds(pl.multiple_of((me[0] ^ m) * own, own), own)] = part


def fill_select(hot, select_tok, sel):
    for b in range(select_tok.shape[0]):
        here = pl.ds(b * CAP, CAP)
        sel[here, :] = dot_nn(hot[here, :], select_tok[b])


def fill_share(hot, share, col):
    for b in range(share.shape[0]):
        here = pl.ds(b * CAP, CAP)
        one = jnp.sum(hot[here, :].astype(F32) * share[b : b + 1, :], axis=1, keepdims=True)
        col[here, :] = jnp.broadcast_to(one, (CAP, col.shape[1]))


def scatter_add(me, hot, y, acc, at):
    tok = hot.shape[1]
    n = acc.shape[0] // tok
    for b in range(n):
        mask = me[0] ^ b
        there = block_of(mask // 2 + (mask % 2) * (n // 2), tok)
        acc[there, at] += dot_tn(hot[pl.ds(b * CAP, CAP), :], y[pl.ds(b * CAP, CAP), :])


def copy_out(acc, rows, near, far, sem):
    half = acc.shape[0] // 2
    for side, ref in enumerate((near, far)):
        rows[:half, :] = acc[side * half : (side + 1) * half, :].astype(BF16)
        copy = pltpu.make_async_copy(rows.at[pl.ds(0, half)], ref, sem)
        copy.start()
        copy.wait()


def write_out(acc, near, far):
    half = acc.shape[0] // 2
    near[...] = acc[:half, :].astype(BF16).reshape(near.shape)
    far[...] = acc[half:, :].astype(BF16).reshape(far.shape)


def live_rows(staged, first, k):
    total = staged[first : first + RANK]
    for d in range(1, k // RANK):
        total = total + staged[first + d * RANK : first + (d + 1) * RANK]
    return total


def lanes(e, size):
    return pl.ds(pl.multiple_of(e * size, 128), size)


def turn(v, cos, sin):
    return v * cos + pltpu.roll(v, HD // 2, 1) * sin


def turn_heads(v, table, sign):
    cos, sin = table[:, :HD], table[:, HD:]
    heads = [turn(v[:, h : h + HD], cos, sign * sin) for h in range(0, v.shape[1], HD)]
    return heads[0] if len(heads) == 1 else jnp.concatenate(heads, axis=1)


def qkv_kernel(n, *refs):
    me, xs, refs = refs[0], refs[1 : 1 + n], refs[1 + n :]
    key, select_tok, hi, lo, w, b_in, q, kv, rank_q, rank_kv, rows_own, tok_own, a_in, wide_w, *refs = refs
    hot, rows, sel, table = refs
    i = pl.program_id(0)
    tok, k, slots = hi.shape[1], b_in.shape[0], hot.shape[0]
    own = w.shape[1]
    mine = pl.ds(pl.multiple_of(me[0] * own, own), own)

    @pl.when(i == 0)
    def start():
        a_in[...] = jnp.zeros(a_in.shape, BF16)

    fill_map(me, xs, i, a_in.at[:k])
    wide_w[:, :own] = w[...]
    wide_w[:, own:] = a_in[...].T

    @pl.when(i < EXPERTS)
    def query():
        fill_hot(key, hot)
        fill_rows(me, hot, xs, k, rows)
        fill_select(hot, select_tok, sel)
        for b in range(n):
            here = pl.ds(b * CAP, CAP)
            table[here, :] = dot_nn(hot[here, :], hi[b]) + dot_nn(hot[here, :], lo[b])
        both = dot_nn(rows[:slots, :], wide_w[...])
        rank = (both[:, own : own + k] * sel[:slots, :]).astype(BF16)
        rank_q[...] = rank
        pre = both[:, :own] + dot_nn(rank, b_in[...])
        q[...] = turn_heads(pre, table[:slots, :], 1.0).astype(BF16)
        rows_own[...] = rows[:slots, mine]

    @pl.when(i >= EXPERTS)
    def key_value():
        group = n // 2
        some = pl.ds(0, group * tok)
        for half in range(2):
            for j in range(group):
                m = half * group + j
                b = me[0] ^ m
                here = pl.ds(j * tok, tok)
                rows[here, :] = xs[m][pl.ds(k, tok), :]
                sel[here, :] = select_tok[b].astype(F32)
                table[here, :] = hi[b].astype(F32) + lo[b].astype(F32)
            both = dot_nn(rows[some, :], wide_w[...])
            rank = (both[:, own : own + k] * sel[some, :]).astype(BF16)
            pre = both[:, :own] + dot_nn(rank, b_in[...])
            turned = turn_heads(pre, table[some, :], 1.0)
            done = jnp.where(i == EXPERTS, turned, pre).astype(BF16)
            for j in range(group):
                there = block_of(me[0] ^ (half * group + j), tok)
                here = slice(j * tok, (j + 1) * tok)
                rank_kv[there, :] = rank[here]
                kv[there, :] = done[here]
                tok_own[there, :] = rows[here, mine]


def limits(key, begin, b):
    tok = begin.shape[1]
    slot = lax.broadcasted_iota(jnp.int32, (CAP, tok), 0)
    token = b * tok + lax.broadcasted_iota(jnp.int32, (CAP, tok), 1)
    first, last = [], []
    for e in range(EXPERTS):
        chosen = slot == key[e : e + 1, :]
        first.append(jnp.sum(jnp.where(chosen, begin[...], 0), axis=1, keepdims=True))
        last.append(jnp.sum(jnp.where(chosen, token, 0), axis=1, keepdims=True))
    return jnp.concatenate(first), jnp.concatenate(last)


def attend_kernel(key, begin, q, k, v, mixed, lse, scores, mx, tot, acc):
    b = pl.program_id(0)
    tok, own = begin.shape[1], q.shape[2]
    rows = q.shape[0] * q.shape[1]
    first, last = limits(key, begin, b)
    query = q[...].reshape(rows, own)
    heads = [slice(h, h + HD) for h in range(0, own, HD)]
    count = (b * tok + tok + CHUNK - 1) // CHUNK
    mx[...] = jnp.full(mx.shape, NEG, F32)

    def score(j, carry):
        start = pl.multiple_of(j * CHUNK, CHUNK)
        here = pl.ds(start, CHUNK)
        at = start + lax.broadcasted_iota(jnp.int32, (rows, CHUNK), 1)
        seen = (at >= first) & (at <= last)
        raw = [dot_nt(query[:, h], k[here, h]) for h in heads]
        for i, h in enumerate(heads):
            s = jnp.where(seen, raw[i] * HD ** (-0.5), NEG)
            scores[i, :, here] = s
            mx[:, h] = jnp.maximum(mx[:, h], jnp.maximum(s[:, :HD], s[:, HD:]))
        return carry

    lax.fori_loop(0, count, score, 0)
    top = [jnp.max(mx[:, h], axis=1, keepdims=True) for h in heads]
    tot[...] = jnp.zeros(tot.shape, F32)
    acc[...] = jnp.zeros(acc.shape, F32)

    def mix(j, carry):
        here = pl.ds(pl.multiple_of(j * CHUNK, CHUNK), CHUNK)
        for i, h in enumerate(heads):
            p = jnp.exp(scores[i, :, here] - top[i])
            tot[:, h] += p[:, :HD] + p[:, HD:]
            acc[:, h] += dot_nn(p.astype(BF16), v[here, h])
        return carry

    lax.fori_loop(0, count, mix, 0)
    for i, h in enumerate(heads):
        total = jnp.sum(tot[:, h], axis=1, keepdims=True)
        mixed[:, :, h] = (acc[:, h] / total).astype(BF16).reshape(EXPERTS, CAP, HD)
        spread = jnp.broadcast_to(top[i] + jnp.log(total), (rows, HD))
        lse[:, :, h] = spread.reshape(EXPERTS, CAP, HD)


def attend_back_kernel(key, begin, q, g, mixed, lse, k, v, gq, gk, gv, dq):
    b = pl.program_id(0)
    tok, own = begin.shape[1], q.shape[2]
    rows = q.shape[0] * q.shape[1]
    scale = HD ** (-0.5)

    @pl.when(b == 0)
    def start():
        gk[...] = jnp.zeros(gk.shape, F32)
        gv[...] = jnp.zeros(gv.shape, F32)

    first, last = limits(key, begin, b)

    def flat(r):
        return r[...].reshape(rows, own)

    query, grad = flat(q), flat(g)
    heads = [slice(h, h + HD) for h in range(0, own, HD)]
    product = flat(mixed).astype(F32) * grad.astype(F32)
    delta = [jnp.sum(product[:, h], axis=1, keepdims=True) for h in heads]
    logs = flat(lse)
    log_total = [logs[:, h.start : h.start + 1] for h in heads]
    count = (b * tok + tok + CHUNK - 1) // CHUNK
    dq[...] = jnp.zeros(dq.shape, F32)

    def step(j, carry):
        begin_at = pl.multiple_of(j * CHUNK, CHUNK)
        here = pl.ds(begin_at, CHUNK)
        at = begin_at + lax.broadcasted_iota(jnp.int32, (rows, CHUNK), 1)
        seen = (at >= first) & (at <= last)
        raw = [dot_nt(query[:, h], k[here, h]) for h in heads]
        dps = [dot_nt(grad[:, h], v[here, h]) for h in heads]
        for i, h in enumerate(heads):
            p = jnp.where(seen, jnp.exp(raw[i] * scale - log_total[i]), 0.0)
            ds = (p * (dps[i] - delta[i])).astype(BF16)
            dq[:, h] += dot_nn(ds, k[here, h])
            gk[here, h] += dot_tn(ds, query[:, h]) * scale
            gv[here, h] += dot_tn(p.astype(BF16), grad[:, h])
        return carry

    lax.fori_loop(0, count, step, 0)
    gq[...] = (dq[...] * scale).reshape(gq.shape)


def out_kernel(n, first, stride, *refs):
    me, xs, refs = refs[0], refs[1 : 1 + n], refs[1 + n :]
    x, key, share, select_tok, down, w, near, far, live, maps, hot, sel, col, part, stage, acc = refs
    e = pl.program_id(0)
    k, slots = down.shape[0], x.shape[0]

    @pl.when(e == 0)
    def start():
        acc[...] = jnp.zeros(acc.shape, F32)
        stage[...] = jnp.zeros(stage.shape, F32)

    fill_map(me, xs, first + stride * e, maps)
    fill_hot(key, hot)
    fill_select(hot, select_tok, sel)
    fill_share(hot, share, col)
    rank = dot_nt(x[...], down[...]) * sel[...]
    stage[:, :k] = rank
    live[:, lanes(e, slots)] = live_rows(stage[...].T, 0, k).astype(BF16)
    rank = rank.astype(BF16)
    width = part.shape[1]
    for c in range(0, w.shape[1], width):
        at = pl.ds(c, width)
        y = dot_nn(x[...], w[:, at]) + dot_nn(rank, maps[:, at])
        part[...] = (y * col[:, :1]).astype(BF16)
        scatter_add(me, hot, part, acc, at)

    @pl.when(e == EXPERTS - 1)
    def finish():
        write_out(acc, near, far)


def back_kernel(n, first, stride, *refs):
    me, xs, ms, refs = refs[0], refs[1 : 1 + n], refs[1 + n : 1 + 2 * n], refs[1 + 2 * n :]
    key, select_tok, w, small, h, rank, rows_own, maps, hot, rows, sel = refs
    deep = w.shape[0]
    maps[:deep, :] = w[...]
    fill_map(me, ms, first + stride * pl.program_id(0), maps.at[deep:])
    fill_hot(key, hot)
    fill_rows(me, hot, xs, 0, rows)
    fill_select(hot, select_tok, sel)
    both = dot_nt(rows[...], maps[...])
    low = (both[:, deep:] * sel[...]).astype(BF16)
    rank[...] = low
    h[...] = both[:, :deep] + dot_nn(low, small[...])
    rows_own[...] = rows[:, lanes(me[0], rows_own.shape[1])]


def mixed_back_kernel(n, *refs):
    me, xs, ms, refs = refs[0], refs[1 : 1 + n], refs[1 + n : 1 + 2 * n], refs[1 + 2 * n :]
    key, share, select_tok, w, small, mixed, g, a_grad, dshare, rows_own, maps, *refs = refs
    hot, rows, sel, col, stage = refs
    e = pl.program_id(0)
    k, own, slots = small.shape[0], mixed.shape[1], mixed.shape[0]
    maps[:own, :] = w[...]
    fill_map(me, ms, e, maps.at[own:])

    @pl.when(e == 0)
    def start():
        stage[...] = jnp.zeros(stage.shape, F32)

    fill_hot(key, hot)
    fill_rows(me, hot, xs, 0, rows)
    fill_select(hot, select_tok, sel)
    fill_share(hot, share, col)
    both = dot_nt(rows[...], maps[...])
    low = (both[:, own:] * sel[...]).astype(BF16)
    h = both[:, :own] + dot_nn(low, small[...])
    stage[:, :1] = jnp.sum(mixed[...].astype(F32) * h, axis=1, keepdims=True)
    dshare[:, lanes(e, slots)] = stage[...].T[:8]
    g[...] = (h * col[:, :1]).astype(BF16)
    scaled = (low.astype(F32) * col[:, :k]).astype(BF16)
    a_grad[...] = dot_tn(scaled, mixed[...]).astype(BF16)
    rows_own[...] = rows[:, lanes(me[0], own)]


def feed_kernel(n, first, stride, *refs):
    me, xs, ms, refs = refs[0], refs[1 : 1 + n], refs[1 + n : 1 + 2 * n], refs[1 + 2 * n :]
    key, share, select_tok, wg, wu, hid, h, back_down, *refs = refs
    near, far, inner, live, dshare, h_grad, rows_own, *refs = refs
    hot, rows, sel, col, stage, both, gate, up, gg, gu, part, acc, sem = refs
    e = pl.program_id(0)
    k, own, slots = hid.shape[1], rows_own.shape[1], rows.shape[0]

    @pl.when(e == 0)
    def start():
        acc[...] = jnp.zeros(acc.shape, F32)
        stage[...] = jnp.zeros(stage.shape, F32)

    fill_hot(key, hot)
    fill_rows(me, hot, xs, 0, rows)
    fill_select(hot, select_tok, sel)
    fill_share(hot, share, col)
    fill_map(me, ms, first + stride * e, both.at[:k])
    fill_map(me, ms, first + stride * e + 1, both.at[k:])
    ranks = dot_nt(rows[...], both[...])
    rank_gate = (ranks[:, :k] * sel[...]).astype(BF16)
    rank_up = (ranks[:, k:] * sel[...]).astype(BF16)
    gate[...] = dot_nt(rows[...], wg[...]) + dot_nn(rank_gate, hid[0])
    up[...] = dot_nt(rows[...], wu[...]) + dot_nn(rank_up, hid[1])

    def point(b, carry):
        r = block_of(b, CAP)
        a, u, hh, s = gate[r, :], up[r, :], h[r, :], col[r, :1]
        sig = jax.nn.sigmoid(a)
        act = a * sig
        value = act * u
        inner[r, :] = value.astype(BF16)
        stage[r, 2 * k : 2 * k + 1] = jnp.sum(value * hh, axis=1, keepdims=True)
        scaled = hh * s
        gg[r, :] = (scaled * u * sig * (1.0 + a * (1.0 - sig))).astype(BF16)
        gu[r, :] = (scaled * act).astype(BF16)
        return carry

    lax.fori_loop(0, slots // CAP, point, 0)
    stage[:, :k] = dot_nt(gg[...], hid[0]) * sel[...]
    stage[:, k : 2 * k] = dot_nt(gu[...], hid[1]) * sel[...]
    stage[:, 128 : 128 + k] = dot_nt(inner[...], hid[2]) * sel[...]
    staged = stage[...].T
    live[:RANK, lanes(e, slots)] = live_rows(staged, 0, k).astype(BF16)
    live[RANK : 2 * RANK, lanes(e, slots)] = live_rows(staged, k, k).astype(BF16)
    live[2 * RANK :, lanes(e, slots)] = live_rows(staged, 128, k).astype(BF16)
    dshare[:, lanes(e, slots)] = staged[2 * k : 2 * k + 8]
    h_grad[0] = dot_tn(rank_gate, gg[...]).astype(BF16)
    h_grad[1] = dot_tn(rank_up, gu[...]).astype(BF16)
    scaled = (back_down[...].astype(F32) * col[:, :k]).astype(BF16)
    h_grad[2] = dot_tn(scaled, inner[...]).astype(BF16)
    rows_own[...] = rows[:, lanes(me[0], own)]
    back = stage[:, : 2 * k].astype(BF16)
    width = part.shape[1]
    for c in range(0, wg.shape[1], width):
        at = pl.ds(c, width)
        y = dot_nn(gg[...], wg[:, at]) + dot_nn(gu[...], wu[:, at]) + dot_nn(back, both[:, at])
        part[...] = y.astype(BF16)
        scatter_add(me, hot, part, acc, at)

    @pl.when(e == EXPERTS - 1)
    def finish():
        copy_out(acc, rows, near, far, sem)


def qkv_rank_kernel(
    key, select_tok, hi, lo, b_in, gq, gk, gv, rank_q, rank_kv,
    out_q, out_kv, back_q, back_kv, live, b_grad,
    hot, sel, table, stage,
):
    i = pl.program_id(0)
    n, tok, k = hi.shape[0], hi.shape[1], b_in.shape[0]
    slots, seq = gq.shape[0], gk.shape[0]

    @pl.when(i == 0)
    def start():
        stage[...] = jnp.zeros(stage.shape, F32)

    @pl.when(i < EXPERTS)
    def query():
        fill_hot(key, hot)
        fill_select(hot, select_tok, sel)
        for b in range(n):
            here = pl.ds(b * CAP, CAP)
            table[here, :] = dot_nn(hot[here, :], hi[b]) + dot_nn(hot[here, :], lo[b])
        g = turn_heads(gq[...], table[...], -1.0).astype(BF16)
        out_q[...] = g
        rank = dot_nt(g, b_in[...]) * sel[...]
        stage[:slots, :k] = rank
        back_q[...] = rank.astype(BF16)
        live[:, lanes(i, slots)] = live_rows(stage[:slots, :].T, 0, k).astype(BF16)
        b_grad[...] = dot_tn(rank_q[...], g).astype(BF16)

    @pl.when(i >= EXPERTS)
    def key_value():
        for b in range(n):
            here = pl.ds(b * tok, tok)
            both = hi[b].astype(F32) + lo[b].astype(F32)
            turned = turn_heads(gk[here, :], both, -1.0)
            out_kv[here, :] = jnp.where(i == EXPERTS, turned, gv[here, :]).astype(BF16)
            stage[here, k : 2 * k] = select_tok[b].astype(F32)
        g = out_kv[...]
        rank = dot_nt(g, b_in[...]) * stage[:seq, k : 2 * k]
        stage[:seq, :k] = rank
        back_kv[...] = rank.astype(BF16)
        b_grad[...] = dot_tn(rank_kv[...], g).astype(BF16)
        begin = EXPERTS * slots + (i - EXPERTS) * seq
        there = pl.ds(pl.multiple_of(begin, 128), seq)
        live[:, there] = live_rows(stage[:seq, :].T, 0, k).astype(BF16)


def qkv_back_kernel(n, *refs):
    me, xs, refs = refs[0], refs[1 : 1 + n], refs[1 + n :]
    key, w, gq, gkv, back_q, back_kv, near, far, maps, hot, part, acc, some_g, some_rank = refs
    i = pl.program_id(0)
    tok = hot.shape[1]
    wide = maps.shape[1]
    width = part.shape[1]
    fill_map(me, xs, i, maps)

    @pl.when(i == 0)
    def start():
        acc[...] = jnp.zeros(acc.shape, F32)

    @pl.when(i < EXPERTS)
    def query():
        fill_hot(key, hot)
        for c in range(0, wide, width):
            at = pl.ds(c, width)
            y = dot_nt(gq[...], w[at, :]) + dot_nn(back_q[...], maps[:, at])
            part[...] = y.astype(BF16)
            scatter_add(me, hot, part, acc, at)

    @pl.when(i >= EXPERTS)
    def key_value():
        group = n // 2
        size = group * tok
        for half in range(2):
            there = pl.ds(half * size, size)
            for j in range(group):
                block = block_of(me[0] ^ (2 * j + half), tok)
                some_g[j * tok : (j + 1) * tok, :] = gkv[block, :]
                some_rank[j * tok : (j + 1) * tok, :] = back_kv[block, :]
            for c in range(0, wide, width):
                at = pl.ds(c, width)
                acc[there, at] += dot_nt(some_g[...], w[at, :]) + dot_nn(some_rank[...], maps[:, at])

    @pl.when(i == EXPERTS + 1)
    def finish():
        write_out(acc, near, far)


def chunk_of(slots, wide):
    width = wide // 2
    while slots * width > 640 * 1024:
        width //= 2
    return width


def whole(shape):
    zeros = (0,) * len(shape)
    return pl.BlockSpec(shape, lambda *at: zeros, pipeline_mode=pl.Buffered(1))


def by_expert(shape, at=lambda i: i):
    rest = (0,) * len(shape)
    return pl.BlockSpec((None,) + shape, lambda i, *unused: (at(i),) + rest)


def shaped(shape, dtype):
    return jax.ShapeDtypeStruct(shape, dtype)


def run(kernel, name, steps, ins, outs, scratch, args, flops, scalars=1):
    call = pl.pallas_call(
        kernel,
        grid_spec=pltpu.PrefetchScalarGridSpec(
            num_scalar_prefetch=scalars,
            grid=steps,
            in_specs=ins,
            out_specs=[o[0] for o in outs],
            scratch_shapes=[pltpu.VMEM(*one) if isinstance(one, tuple) else one for one in scratch],
        ),
        out_shape=[shaped(o[1], o[2]) for o in outs],
        compiler_params=pltpu.CompilerParams(vmem_limit_bytes=62 << 20),
        cost_estimate=pl.CostEstimate(
            flops=int(flops), bytes_accessed=32 << 20, transcendentals=1 << 20
        ),
        name=name,
    )
    return call(*args)


def last_expert(i):
    return jnp.minimum(i, EXPERTS - 1)


def from_expert(i):
    return jnp.maximum(i - EXPERTS, 0)


def rows_spec(x, rows=None):
    return whole((x.shape[0] if rows is None else rows, x.shape[1]))


def sides(n, tok, wide):
    shape = (n // 2, tok, wide)
    return [(whole(shape), shape, BF16)] * 2


def qkv(me, pieces, key, select_tok, hi, lo, w, b_in):
    n, tok, k = select_tok.shape
    wide, own, slots, seq = pieces[0].shape[1], w.shape[2], n * CAP, n * tok
    return run(
        partial(qkv_kernel, n),
        "qkv",
        (EXPERTS + 2,),
        [rows_spec(p) for p in pieces]
        + [by_expert((n, tok), last_expert), whole(select_tok.shape), whole(hi.shape),
           whole(lo.shape), by_expert((wide, own)), by_expert((k, own))],
        [
            (by_expert((slots, own), last_expert), (EXPERTS, slots, own), BF16),
            (by_expert((seq, own), from_expert), (2, seq, own), BF16),
            (by_expert((slots, k), last_expert), (EXPERTS, slots, k), BF16),
            (by_expert((seq, k), from_expert), (2, seq, k), BF16),
            (by_expert((slots, own), last_expert), (EXPERTS, slots, own), BF16),
            (whole((seq, own)), (seq, own), BF16),
        ],
        [((128, wide), BF16), ((wide, own + 128), BF16), ((slots, tok), BF16),
         ((max(slots, seq // 2), wide), BF16),
         ((max(slots, seq // 2), k), F32), ((max(slots, seq // 2), 2 * HD), F32)],
        (me, *pieces, key, select_tok, hi, lo, w, b_in),
        2 * wide * own * (EXPERTS * slots + 2 * seq) * 1.5,
    )


def attend_specs(n, tok, own):
    slot_spec = pl.BlockSpec((EXPERTS, None, CAP, own), lambda b: (0, b, 0, 0))
    tokens = [pl.BlockSpec((None, EXPERTS, tok), lambda b: (b, 0, 0)),
              pl.BlockSpec((None, 1, tok), lambda b: (b, 0, 0))]
    return slot_spec, tokens, whole((n * tok, own)), (EXPERTS, n, CAP, own)


def attend(key, begin, q, k, v):
    n, tok = begin.shape[0], begin.shape[2]
    own, seq, rows = q.shape[2], n * tok, EXPERTS * CAP
    slot_spec, tokens, all_spec, shape = attend_specs(n, tok, own)
    mixed, lse = run(
        attend_kernel,
        "attend",
        (n,),
        tokens + [slot_spec, all_spec, all_spec],
        [(slot_spec, shape, BF16), (slot_spec, shape, F32)],
        [((own // HD, rows, seq), F32), ((rows, own), F32), ((rows, own), F32), ((rows, own), F32)],
        (key, begin, q.reshape(shape), k, v),
        3 * rows * seq * own * n,
        0,
    )
    return mixed.reshape(q.shape), lse


def attend_back(key, begin, q, g, mixed, lse, k, v):
    n, tok = begin.shape[0], begin.shape[2]
    own, seq, rows = q.shape[2], n * tok, EXPERTS * CAP
    slot_spec, tokens, all_spec, shape = attend_specs(n, tok, own)
    gq, gk, gv = run(
        attend_back_kernel,
        "attend_back",
        (n,),
        tokens + [slot_spec] * 4 + [all_spec] * 2,
        [(slot_spec, shape, F32), (all_spec, (seq, own), F32), (all_spec, (seq, own), F32)],
        [((rows, own), F32)],
        (key, begin, q.reshape(shape), g.reshape(shape), mixed.reshape(shape), lse, k, v),
        7 * rows * seq * own * n,
        0,
    )
    return gq.reshape(q.shape), gk, gv


def weight_spec(w, p=None):
    if p is None:
        return by_expert(w.shape[1:])
    return pl.BlockSpec((None, None) + w.shape[2:], lambda e, *unused: (e, p, 0, 0))


def project_out(name, me, x, key, share, select_tok, down, w, pieces, groups, first, stride, p=None):
    n, tok, k = select_tok.shape
    wide, slots, deep = pieces[0].shape[1], n * CAP, x.shape[2]
    down_spec = by_expert((k, deep)) if p is None else weight_spec(down, p)
    return run(
        partial(out_kernel, n, first, stride),
        name,
        (EXPERTS,),
        [rows_spec(m, groups * k) for m in pieces]
        + [by_expert((slots, deep)), by_expert((n, tok)), by_expert((n, tok)), whole(select_tok.shape),
           down_spec, weight_spec(w, p)],
        sides(n, tok, wide) + [(whole((RANK, EXPERTS * slots)), (RANK, EXPERTS * slots), BF16)],
        [((k, wide), BF16), ((slots, tok), BF16), ((slots, k), F32), ((slots, 128), F32),
         ((slots, chunk_of(slots, wide)), BF16), ((slots, 128), F32), ((n * tok, wide), F32)],
        (me, *pieces, x, key, share, select_tok, down, w),
        2 * wide * deep * EXPERTS * slots * 1.5,
    )


def feed_back_down(me, tokens, pieces, groups, first, stride, key, select_tok, w, small):
    n, tok, k = select_tok.shape
    wide, slots, deep = pieces[0].shape[1], n * CAP, w.shape[2]
    own = wide // n
    return run(
        partial(back_kernel, n, first, stride),
        "feed_down_back",
        (EXPERTS,),
        [rows_spec(m) for m in tokens] + [rows_spec(m, groups * k) for m in pieces]
        + [by_expert((n, tok)), whole(select_tok.shape), weight_spec(w, 2), weight_spec(small, 2)],
        [(by_expert((slots, deep)), (EXPERTS, slots, deep), F32),
         (by_expert((slots, k)), (EXPERTS, slots, k), BF16),
         (by_expert((slots, own)), (EXPERTS, slots, own), BF16)],
        [((deep + k, wide), BF16), ((slots, tok), BF16), ((slots, wide), BF16), ((slots, k), F32)],
        (me, *tokens, *pieces, key, select_tok, w, small),
        2 * wide * deep * EXPERTS * slots * 1.3,
    )


def mixed_back(me, tokens, pieces, groups, key, share, select_tok, w, small, mixed):
    n, tok, k = select_tok.shape
    wide, slots, own = pieces[0].shape[1], n * CAP, w.shape[1]
    return run(
        partial(mixed_back_kernel, n),
        "mixed_back",
        (EXPERTS,),
        [rows_spec(m) for m in tokens] + [rows_spec(m, groups * k) for m in pieces]
        + [by_expert((n, tok)), by_expert((n, tok)), whole(select_tok.shape),
           weight_spec(w), by_expert((k, own)), by_expert((slots, own))],
        [(by_expert((slots, own)), (EXPERTS, slots, own), BF16),
         (by_expert((k, own)), (EXPERTS, k, own), BF16),
         (whole((8, EXPERTS * slots)), (8, EXPERTS * slots), F32),
         (by_expert((slots, own)), (EXPERTS, slots, own), BF16)],
        [((own + k, wide), BF16), ((slots, tok), BF16), ((slots, wide), BF16), ((slots, k), F32),
         ((slots, 128), F32), ((slots, 128), F32)],
        (me, *tokens, *pieces, key, share, select_tok, w, small, mixed),
        2 * wide * own * EXPERTS * slots * 1.5,
    )


def feed(me, tokens, pieces, groups, first, stride, key, share, select_tok, w, hid, h, back_down):
    n, tok, k = select_tok.shape
    wide, slots, deep = pieces[0].shape[1], n * CAP, w.shape[2]
    own = wide // n
    return run(
        partial(feed_kernel, n, first, stride),
        "feed",
        (EXPERTS,),
        [rows_spec(m) for m in tokens] + [rows_spec(m, groups * k) for m in pieces]
        + [by_expert((n, tok)), by_expert((n, tok)),
           whole(select_tok.shape), weight_spec(w, 0), weight_spec(w, 1), by_expert((3, k, deep)),
           by_expert((slots, deep)), by_expert((slots, k))],
        [(pl.BlockSpec(memory_space=pl.ANY), (n // 2 * tok, wide), BF16)] * 2
        + [(by_expert((slots, deep)), (EXPERTS, slots, deep), BF16),
           (whole((3 * RANK, EXPERTS * slots)), (3 * RANK, EXPERTS * slots), BF16),
           (whole((8, EXPERTS * slots)), (8, EXPERTS * slots), F32),
           (by_expert((3, k, deep)), (EXPERTS, 3, k, deep), BF16),
           (by_expert((slots, own)), (EXPERTS, slots, own), BF16)],
        [((slots, tok), BF16), ((slots, wide), BF16), ((slots, k), F32), ((slots, 128), F32),
         ((slots, 256), F32), ((2 * k, wide), BF16), ((slots, deep), F32), ((slots, deep), F32),
         ((slots, deep), BF16), ((slots, deep), BF16), ((slots, chunk_of(slots, wide)), BF16),
         ((n * tok, wide), F32), pltpu.SemaphoreType.DMA],
        (me, *tokens, *pieces, key, share, select_tok, w, w, hid, h, back_down),
        8 * wide * deep * EXPERTS * slots * 1.3,
    )


def qkv_rank(key, select_tok, hi, lo, b_in, gq, gk, gv, rank_q, rank_kv):
    n, tok, k = select_tok.shape
    own, slots, seq = gq.shape[2], n * CAP, n * tok
    total = EXPERTS * slots + 2 * seq
    return run(
        qkv_rank_kernel,
        "qkv_rank",
        (EXPERTS + 2,),
        [by_expert((n, tok), last_expert), whole(select_tok.shape), whole(hi.shape),
         whole(lo.shape), by_expert((k, own)),
         by_expert((slots, own), last_expert), whole((seq, own)), whole((seq, own)),
         by_expert((slots, k), last_expert), by_expert((seq, k), from_expert)],
        [(by_expert((slots, own), last_expert), (EXPERTS, slots, own), BF16),
         (by_expert((seq, own), from_expert), (2, seq, own), BF16),
         (by_expert((slots, k), last_expert), (EXPERTS, slots, k), BF16),
         (by_expert((seq, k), from_expert), (2, seq, k), BF16),
         (whole((RANK, total)), (RANK, total), BF16),
         (by_expert((k, own)), (EXPERTS + 2, k, own), BF16)],
        [((slots, tok), BF16), ((slots, k), F32), ((slots, 2 * HD), F32), ((max(slots, seq), 128), F32)],
        (key, select_tok, hi, lo, b_in, gq, gk, gv, rank_q, rank_kv),
        4 * k * own * (EXPERTS * slots + 2 * seq),
        0,
    )


def qkv_back(me, pieces, key, w, gq, gkv, back_q, back_kv):
    n, tok = key.shape[1:]
    k, own, slots, seq = back_q.shape[2], w.shape[2], n * CAP, n * tok
    wide = pieces[0].shape[1]
    return run(
        partial(qkv_back_kernel, n),
        "qkv_back",
        (EXPERTS + 2,),
        [rows_spec(m, k) for m in pieces]
        + [by_expert((n, tok), last_expert), by_expert((wide, own)),
           by_expert((slots, own), last_expert), by_expert((seq, own), from_expert),
           by_expert((slots, k), last_expert), by_expert((seq, k), from_expert)],
        sides(n, tok, wide),
        [((k, wide), BF16), ((slots, tok), BF16), ((slots, chunk_of(slots, wide)), BF16),
         ((seq, wide), F32), ((seq // 2, own), BF16), ((seq // 2, k), BF16)],
        (me, *pieces, key, w, gq, gkv, back_q, back_kv),
        2 * wide * own * (EXPERTS * slots + 2 * seq) * 1.5,
    )


def members(routes):
    names = jnp.arange(EXPERTS, dtype=jnp.int32)[None, :, None]
    member = (routes[:, :1] == names) | (routes[:, 1:] == names)
    tok = routes.shape[-1]
    before = (jnp.arange(tok)[:, None] < jnp.arange(tok)[None, :]).astype(BF16)
    rank = ein("met,tu->meu", member.astype(BF16), before).astype(jnp.int32)
    return jnp.where(member, rank, -1)


def own_shares(normed, router, routes):
    names = jnp.arange(EXPERTS, dtype=jnp.int32)[:, None]
    member = (routes[:1] == names) | (routes[1:] == names)
    logits = ein("td,de->et", normed, router)
    return jax.nn.softmax(jnp.where(member, logits, -jnp.inf), axis=0)


def route_back(share, grad_share, router):
    grad = share * (grad_share - jnp.sum(share * grad_share, axis=0, keepdims=True))
    return jnp.einsum("et,de->td", grad, router.astype(F32), precision=lax.Precision.HIGHEST)


def local(
    n,
    reps,
    layer_input_state,
    cotangent,
    norm_gain_vectors,
    attention_router_weight,
    feed_router_weight,
    attention_query_weight,
    key_value_weight,
    attention_output_weight,
    feed_expert_weight,
    attention_adapters,
    feed_adapter_width,
    feed_adapter_hidden,
    token_document,
    document_adapter,
    attention_expert_pairs,
    feed_expert_pairs,
):
    tok, wide = layer_input_state.shape
    own, slots = wide // n, n * CAP
    columns = attention_adapters.shape[3]
    me = lax.axis_index("shard")
    me_ref = me.reshape(1).astype(jnp.int32)
    segments = token_document[0]
    seq = segments.shape[0]
    docs = document_adapter[0]
    doc_count = docs.shape[0]
    k = doc_count * RANK

    def one_hot(which):
        at = which[:, None] * RANK + jnp.arange(RANK)[None, :]
        return (at.reshape(-1)[:, None] == jnp.arange(columns)[None, :]).astype(BF16)

    pick = one_hot(docs)
    attn_small = ein("kc,pmwc->pmkw", pick, attention_adapters).astype(BF16)
    width_small = ein("kc,pmwc->pmkw", pick, feed_adapter_width).astype(BF16)
    hidden_small = ein("kc,epcf->epkf", pick, feed_adapter_hidden).astype(BF16)
    b_in, a_out = attn_small[1, : EXPERTS + 2], attn_small[0, EXPERTS + 2 :]

    x = layer_input_state.astype(F32)
    gain_one = norm_gain_vectors[0].astype(F32)
    gain_two = norm_gain_vectors[1].astype(F32)
    normed_own = rms_norm(gain_one, x).astype(BF16)
    routes = jnp.concatenate([attention_expert_pairs.T, feed_expert_pairs.T])
    own_a = own_shares(normed_own, attention_router_weight, routes[:2])
    own_hi = own_a.astype(BF16)
    own_lo = (own_a - lax.reduce_precision(own_a, 8, 7)).astype(BF16)
    spare = jnp.stack([routes.astype(BF16).reshape(-1), own_hi.reshape(-1), own_lo.reshape(-1)])
    first = jnp.concatenate([pack_maps(attn_small[0, : EXPERTS + 2], n, spare), normed_own])
    weights = [attention_query_weight, key_value_weight]
    if n == 8:
        cut = (first.shape[0] // 2 + 15) // 16 * 16
        y0, x1 = swap(first[:cut], n, 4), swap(first[cut:], n, 2)
        y1, x0 = swap(first[cut:], n, 4), swap(first[:cut], n, 2)
        y0, x1, *weights = tie(y0, x1, *weights)
        d0, d1 = swap(y0, n, 2), swap(x1, n, 4)
        chips = {0: first}
        for m, p in ((2, (x0, x1)), (4, (y0, y1)), (6, (d0, d1))):
            chips[m] = jnp.concatenate(p)
    else:
        chips = across(first, n)
    pieces = from_sibling(chips, n)
    w_in = reshard(weights, me, n)

    facts = jnp.stack([p[:3, (EXPERTS + 2) * own : (EXPERTS + 2) * own + EXPERTS * tok] for p in pieces])
    facts = facts[jnp.arange(n) ^ me].reshape(n, 3, EXPERTS, tok)
    routes = facts[:, 0].astype(jnp.int32)
    share_a = facts[:, 1].astype(F32) + facts[:, 2].astype(F32)

    second = jnp.concatenate([attn_small[1, EXPERTS + 2 :], width_small.reshape(-1, k, own)])
    groups = -(-second.shape[0] // n)
    second, w_in = tie(pack_maps(second, n), w_in)
    map_chips = across(second, n)

    begins = jnp.sum((segments[None, :] < jnp.arange(doc_count)[:, None]).astype(jnp.int32), axis=1)
    doc = segments.reshape(n, tok)
    place = jnp.arange(seq, dtype=jnp.int32).reshape(n, tok)
    doc_table = doc[None] == jnp.arange(doc_count, dtype=jnp.int32)[:, None, None]
    begin = jnp.sum(jnp.where(doc_table, begins[:, None, None], 0), axis=0)
    freq = jnp.exp(-jnp.arange(HD // 2, dtype=F32) * (2.0 * math.log(10000.0) / HD))
    angles = (place - begin).astype(F32)[..., None] * freq
    cos, sin = jnp.cos(angles), jnp.sin(angles)
    table = jnp.concatenate([cos, cos, -sin, sin], axis=-1)
    table_hi = table.astype(BF16)
    table_lo = (table - lax.reduce_precision(table, 8, 7)).astype(BF16)
    chosen_doc = jnp.arange(k, dtype=jnp.int32)[None, None, :] // RANK
    select_tok = (doc[:, :, None] == chosen_doc).astype(BF16)
    select_row = doc_table.astype(F32).reshape(1, doc_count, seq)

    slot_a, slot_f = members(routes[:, :2]), members(routes[:, 2:])
    routes_f_own = feed_expert_pairs.T
    key_a, key_f = slot_a.transpose(1, 0, 2), slot_f.transpose(1, 0, 2)

    def slot_select(slot):
        hot = slot[:, :, None, :] == jnp.arange(CAP, dtype=jnp.int32)[None, None, :, None]
        chose = hot[:, :, None] & doc_table.transpose(1, 0, 2)[:, None, :, None, :]
        select = jnp.any(chose, axis=-1).astype(F32)
        return select.transpose(1, 2, 0, 3).reshape(EXPERTS, doc_count, slots)

    select_a, select_f = slot_select(slot_a), slot_select(slot_f)

    def send(g):
        return [lax.ppermute(g, "rep", [(i, i ^ d) for i in range(reps)]) if d else g for d in range(reps)]

    share_ae = share_a.transpose(1, 0, 2)
    q, kv, rank_q, rank_kv, rows_a_own, normed_own_columns = qkv(
        me_ref, pieces, key_a, select_tok, table_hi, table_lo, w_in, b_in
    )
    q, cotangent_sent, *sent = tie(q, cotangent, *map_chips.values())
    cotangent_chips = across(cotangent_sent, n)
    maps = from_sibling(dict(zip(map_chips, sent)), n)
    mixed, lse = attend(slot_a, begin[:, None], q, kv[0], kv[1])
    near, far, live_o = project_out(
        "attend_out", me_ref, mixed, key_a, share_ae, select_tok, a_out, attention_output_weight, maps, groups, 0, 1
    )
    near, far, *sent = tie(near, far, *cotangent_chips.values())
    attn_total, attn_low = halve(near, far, n)
    grads_out_all = from_sibling(dict(zip(cotangent_chips, sent)), n)
    *attn_low, key_late = tie(*attn_low, key_f)

    w_feed = jnp.swapaxes(feed_expert_weight, 2, 3)
    grad_inner, back_down, rows_g_own = feed_back_down(
        me_ref, grads_out_all, maps, groups, EXPERTS + 2, 3, key_late, select_tok, w_feed, hidden_small
    )
    attn_total, grad_inner = tie(attn_total, grad_inner)
    attended = x + collect(attn_total, attn_low, n)
    normed_two_own = rms_norm(gain_two, attended).astype(BF16)
    normed_two = from_sibling(across(normed_two_own, n), n)
    own_f = own_shares(normed_two_own, feed_router_weight, routes_f_own)
    share_f = gather_small(own_f, me, n)
    share_fe = share_f.transpose(1, 0, 2)
    near, far, inner, live_f, dshare_f, hidden_grad, rows_f_own = feed(
        me_ref, normed_two, maps, groups, EXPERTS, 3, key_f, share_fe, select_tok, w_feed, hidden_small,
        grad_inner, back_down,
    )
    near, far = near.reshape(n // 2, tok, wide), far.reshape(n // 2, tok, wide)
    two_total, two_low = halve(near, far, n)
    *two_low, inner, dshare_f, live_f, live_o = tie(*two_low, inner, dshare_f, live_f, live_o)
    live_f = jnp.concatenate([live_f, live_o])
    live_f = live_f + swap(live_f, n, 1)
    near, far, unused = project_out(
        "feed_out", me_ref, inner, key_f, share_fe, select_tok, hidden_small, w_feed, maps, groups, EXPERTS + 2, 3, 2
    )
    grad_two_own = collect(two_total, two_low, n)

    def own_tokens(slot, dshare):
        mine = lax.dynamic_slice_in_dim(dshare.reshape(EXPERTS, n, CAP), me, 1, 1)[:, 0]
        hot = lax.dynamic_slice_in_dim(slot, me, 1, 0)[0][:, None, :] == jnp.arange(CAP)[None, :, None]
        return jnp.sum(jnp.where(hot, mine[:, :, None], 0.0), axis=1)

    dshare_f = sum_small(dshare_f, n)[:1]
    grad_two_own = grad_two_own + route_back(own_f, own_tokens(slot_f, dshare_f), feed_router_weight)
    grad_attended = cotangent.astype(F32) + rms_back(attended, gain_two, grad_two_own)

    grad_sent, near, far = tie(grad_attended.astype(BF16), near, far)
    out_total, out_low = halve(near, far, n)
    chips = across(grad_sent, n)
    out_total, *sent = tie(out_total, *out_low, *chips.values())
    out_low, sent = sent[: n // 2 - 1], sent[n // 2 - 1 :]
    grads_two = from_sibling(dict(zip(chips, sent)), n)
    mixed_late, live_f = tie(mixed, live_f)
    live_f_sent = list(across(live_f, n).values())
    grad_mixed, a_out_grad, dshare_a, rows_ga_own = mixed_back(
        me_ref, grads_two, maps, groups, key_a, share_ae, select_tok, attention_output_weight, a_out, mixed_late
    )
    grad_mixed, *sent = tie(grad_mixed, *live_f_sent, *out_low)
    live_f_sent, out_low = sent[: n // 2], sent[n // 2 :]
    live_f = added(live_f_sent)
    live_f, live_o = live_f[: 3 * RANK], live_f[3 * RANK :]

    def spread(live, select):
        both = live.astype(F32)[:, None] * select[:, :, None, :]
        return both.reshape(live.shape[0], k, live.shape[2]).astype(BF16)

    def of_slots(live):
        return live.reshape(RANK, EXPERTS, slots).transpose(1, 0, 2)

    def grads(rank, rows):
        return ein("eks,esw->ekw", rank, rows).astype(BF16)

    def slot_row(share, slot):
        hot = slot[:, :, None, :] == jnp.arange(CAP, dtype=jnp.int32)[None, None, :, None]
        row = jnp.sum(jnp.where(hot, share[:, :, None, :], 0.0), axis=-1)
        return row.transpose(1, 0, 2).reshape(EXPERTS, 1, slots)

    def by_stream(sent):
        out = jnp.zeros((reps,) + sent[0].shape, sent[0].dtype)
        for d, got in enumerate(sent):
            out = lax.dynamic_update_slice_in_dim(out, got[None], lax.axis_index("rep") ^ d, 0)
        return out

    scaled_f, scaled_a = select_f * slot_row(share_f, slot_f), select_a * slot_row(share_a, slot_a)
    width_grad = jnp.stack(
        [
            grads(spread(of_slots(live_f[:RANK]), select_f), rows_f_own),
            grads(spread(of_slots(live_f[RANK : 2 * RANK]), select_f), rows_f_own),
            grads(spread(of_slots(live_f[2 * RANK :]), scaled_f), rows_g_own),
        ],
        axis=1,
    )
    b_out_grad = grads(spread(of_slots(live_o), scaled_a), rows_ga_own)
    noted = jnp.zeros((1, k, own), BF16).at[0, 0, :doc_count].set(docs.astype(BF16))
    early_grad = jnp.concatenate([a_out_grad, b_out_grad, noted])
    width_grad, early_grad, lse_late = tie(width_grad, early_grad, lse)
    hidden_all, width_all = lax.all_gather(hidden_grad, "rep"), lax.all_gather(width_grad, "rep")
    early_sent = send(early_grad)
    gq, gk, gv = attend_back(slot_a, begin[:, None], q, grad_mixed, mixed, lse_late, kv[0], kv[1])
    gq, *early_sent = tie(gq, *early_sent)
    layer_out = attended + collect(out_total, out_low, n)
    gq, gkv, back_q, back_kv, live_in, b_in_grad = qkv_rank(
        key_a, select_tok, table_hi, table_lo, b_in, gq, gk, gv, rank_q, rank_kv
    )
    dshare_a = dshare_a[0].astype(BF16).reshape(RANK, -1)
    spare = -dshare_a.shape[1] % 128
    live_in = jnp.concatenate([live_in, jnp.pad(dshare_a, ((0, 0), (0, spare)))], axis=1)
    live_in = live_in + swap(live_in, n, 1)
    gq, live_in, b_in_grad = tie(gq, live_in, b_in_grad)
    live_sent, late_b_sent = list(across(live_in, n).values()), send(b_in_grad)
    near, far = qkv_back(me_ref, pieces, key_a, w_in, gq, gkv, back_q, back_kv)
    near, far, *sent = tie(near, far, *live_sent, *late_b_sent)
    live_sent, late_b_sent = sent[: n // 2], sent[n // 2 :]
    in_total, in_low = (quarter if n == 8 else halve)(near, far, n)
    *in_low, first_sent = tie(*in_low, live_sent[0])
    in_got = [swap(part, n, 2 * i + 2) for i, part in enumerate(in_low)]
    live_in = added([first_sent] + live_sent[1:])
    width = EXPERTS * slots + 2 * seq
    dshare_a = live_in[:, width : width + EXPERTS * slots // RANK]
    live_kv = live_in[:, EXPERTS * slots : width].reshape(RANK, 2, seq).transpose(1, 0, 2)
    a_in_grad = jnp.concatenate(
        [
            grads(spread(of_slots(live_in[:, : EXPERTS * slots]), select_a), rows_a_own),
            ein("pks,sw->pkw", spread(live_kv, select_row), normed_own_columns).astype(BF16),
        ]
    )
    a_in_grad, hidden_all, *in_got = tie(a_in_grad, hidden_all, *in_got)
    late_a_sent = send(a_in_grad)
    grad_normed = collect_quarters(in_total, in_got, n) if n == 8 else added([in_total] + in_got)
    grad_normed = grad_normed + route_back(own_a, own_tokens(slot_a, dshare_a), attention_router_weight)
    grad_normed, width_all = tie(grad_normed, width_all)
    grad_in = grad_attended + rms_back(x, gain_one, grad_normed)

    early = by_stream(early_sent)
    picks = jax.vmap(one_hot)(early[:, 2 * EXPERTS, 0, :doc_count].astype(jnp.int32))
    hidden_out = ein("rpekf,rkc->pecf", hidden_all, picks)
    width_out = ein("rpmkw,rkc->pmwc", width_all, picks)
    late_b, late_a = by_stream(late_b_sent), by_stream(late_a_sent)
    attn = jnp.concatenate([late_a, early[:, :EXPERTS], late_b, early[:, EXPERTS : 2 * EXPERTS]], axis=1)
    attn = attn.reshape(reps, 2, -1, k, own)
    attn_out = ein("rpmkw,rkc->pmwc", attn, picks)
    return (layer_out, grad_in, attn_out, width_out, hidden_out)


def solution(mesh):
    in_specs = (
        P(("rep", "shard"), None),
        P(("rep", "shard"), None),
        P(),
        P(),
        P(),
        P(None, "shard", None),
        P(None, "shard", None),
        P(None, "shard", None),
        P(None, None, None, "shard"),
        P(None, None, "shard", None),
        P(None, None, "shard", None),
        P(None, None, None, "shard"),
        P("rep", None),
        P("rep", None),
        P(("rep", "shard"), None),
        P(("rep", "shard"), None),
    )
    out_specs = (
        P(("rep", "shard"), None),
        P(("rep", "shard"), None),
        P(None, None, "shard", None),
        P(None, None, "shard", None),
        P(None, None, None, "shard"),
    )
    body = partial(local, mesh.shape["shard"], mesh.shape["rep"])
    return jax.shard_map(body, mesh=mesh, in_specs=in_specs, out_specs=out_specs, check_vma=False)
```

```python
from functools import partial
import math

import jax
import jax.numpy as jnp
from jax import lax
from jax.experimental import pallas as pl
from jax.experimental.pallas import tpu as pltpu
from jax.sharding import PartitionSpec as P

HD = 128
RANK = 16
CAP = 80
EXPERTS = 4
CHUNK = 256
EPS = 1e-05
NEG = -1e30
F32 = jnp.float32
BF16 = jnp.bfloat16


def ein(spec, a, b):
    return jnp.einsum(spec, a, b, preferred_element_type=F32)


def rms_norm(gain, values):
    return values * lax.rsqrt(jnp.mean(values * values, axis=-1, keepdims=True) + EPS) * gain


def rms_back(values, gain, grad):
    unused, backward_function = jax.vjp(partial(rms_norm, gain), values)
    return backward_function(grad)[0]


NT = (((1,), (1,)), ((), ()))
TN = (((0,), (0,)), ((), ()))


def dot_nt(a, b):
    return lax.dot_general(a, b, NT, preferred_element_type=F32)


def dot_tn(a, b):
    return lax.dot_general(a, b, TN, preferred_element_type=F32)


def dot_nn(a, b):
    return jnp.dot(a, b, preferred_element_type=F32)


def swap(x, n, d):
    return lax.ppermute(x, "shard", [(i, i ^ d) for i in range(n)])


def tie(*values):
    return lax.optimization_barrier(values)


def across(x, n):
    return {d: swap(x, n, d) if d else x for d in range(0, n, 2)}


def from_sibling(pieces, n):
    other = {m ^ 1: swap(p, n, 1) for m, p in pieces.items()}
    return [p for unused, p in sorted({**pieces, **other}.items())]


def gather_small(x, me, n):
    mine = jnp.stack(list(across(x, n).values()))
    mask = jnp.arange(n) ^ me
    return jnp.concatenate([mine, swap(mine, n, 1)])[mask // 2 + mask % 2 * (n // 2)]


def halve(near, far, n):
    q = near.astype(F32) + swap(far, n, 1).astype(F32)
    return q[0], [q[i].astype(BF16) for i in range(1, n // 2)]


def added(parts):
    return sum([part.astype(F32) for part in parts[1:]], parts[0].astype(F32))


def quarter(near, far, n):
    q = near.astype(F32) + swap(far, n, 1).astype(F32)
    cut = q.shape[1] // 2
    qa, qb = q[:, :cut], q[:, cut:]
    sent = [jnp.stack([qa[1], qa[3]]).astype(BF16), jnp.stack([qb[2], qb[3]]).astype(BF16)]
    return [qa[0], qa[2], qb[0], qb[1]], sent


def collect_quarters(kept, got, n):
    a0, a2, b0, b1 = kept
    ra, rb = got[0].astype(F32), got[1].astype(F32)
    a2, b1 = (a2 + ra[1]).astype(BF16), (b1 + rb[1]).astype(BF16)
    a0 = a0 + ra[0] + swap(a2, n, 4).astype(F32)
    b0 = b0 + rb[0] + swap(b1, n, 2).astype(F32)
    return jnp.concatenate([a0, b0])


def collect(total, low, n):
    for i, part in enumerate(low):
        total = total + swap(part, n, 2 * i + 2).astype(F32)
    return total


def reshard(ws, me, n):
    rows, width = ws[0].shape[1], ws[0].shape[2] // n
    count = sum(w.shape[0] for w in ws)
    out = jnp.zeros((count, n * rows, width), ws[0].dtype)
    for m in sorted(range(n), key=lambda m: -m):
        piece = jnp.concatenate([lax.dynamic_slice_in_dim(w, (me ^ m) * width, width, 2) for w in ws])
        piece = swap(piece, n, m) if m else piece
        out = lax.dynamic_update_slice_in_dim(out, piece, (me ^ m) * rows, 1)
    return out


def pack_maps(maps, n, spare=None):
    count, k, own = maps.shape
    groups = -(-count // n)
    fill = groups * n - count
    flat = [maps[i] for i in range(count)]
    if fill:
        rest = jnp.zeros((k, fill * own), maps.dtype)
        if spare is not None:
            rest = rest.at[: spare.shape[0], : spare.shape[1]].set(spare)
        flat.append(rest)
    rows = [jnp.concatenate(flat[g * n : (g + 1) * n], axis=1) for g in range(groups)]
    return jnp.concatenate(rows) if groups > 1 else rows[0]


def fill_hot(key, hot):
    n, tok = key.shape
    slot = lax.broadcasted_iota(jnp.int32, (CAP, tok), 0)
    for b in range(n):
        one = jnp.where(slot == key[b : b + 1, :], 1.0, 0.0)
        hot[b * CAP : (b + 1) * CAP, :] = one.astype(BF16)


def block_of(b, size):
    return pl.ds(pl.multiple_of(b * size, 16), size)


def fill_rows(me, hot, xs, base, rows):
    tok = hot.shape[1]
    for m, x in enumerate(xs):
        here = block_of(me[0] ^ m, CAP)
        rows[here, :] = dot_nn(hot[here, :], x[pl.ds(base, tok), :]).astype(BF16)


def fill_map(me, xs, index, out):
    n, k = len(xs), out.shape[0]
    own = out.shape[1] // n
    group, column = index // n, index % n
    for m, x in enumerate(xs):
        part = x[block_of(group, k), pl.ds(pl.multiple_of(column * own, own), own)]
        out[:, pl.ds(pl.multiple_of((me[0] ^ m) * own, own), own)] = part


def fill_select(hot, select_tok, sel):
    for b in range(select_tok.shape[0]):
        here = pl.ds(b * CAP, CAP)
        sel[here, :] = dot_nn(hot[here, :], select_tok[b])


def fill_share(hot, share, col):
    for b in range(share.shape[0]):
        here = pl.ds(b * CAP, CAP)
        one = jnp.sum(hot[here, :].astype(F32) * share[b : b + 1, :], axis=1, keepdims=True)
        col[here, :] = jnp.broadcast_to(one, (CAP, col.shape[1]))


def scatter_add(me, hot, y, acc, at):
    tok = hot.shape[1]
    n = acc.shape[0] // tok
    for b in range(n):
        mask = me[0] ^ b
        there = block_of(mask // 2 + (mask % 2) * (n // 2), tok)
        acc[there, at] += dot_tn(hot[pl.ds(b * CAP, CAP), :], y[pl.ds(b * CAP, CAP), :])


def copy_out(acc, rows, near, far, sem):
    half = acc.shape[0] // 2
    for side, ref in enumerate((near, far)):
        rows[:half, :] = acc[side * half : (side + 1) * half, :].astype(BF16)
        copy = pltpu.make_async_copy(rows.at[pl.ds(0, half)], ref, sem)
        copy.start()
        copy.wait()


def write_out(acc, near, far):
    half = acc.shape[0] // 2
    near[...] = acc[:half, :].astype(BF16).reshape(near.shape)
    far[...] = acc[half:, :].astype(BF16).reshape(far.shape)


def live_rows(staged, first, k):
    total = staged[first : first + RANK]
    for d in range(1, k // RANK):
        total = total + staged[first + d * RANK : first + (d + 1) * RANK]
    return total


def lanes(e, size):
    return pl.ds(pl.multiple_of(e * size, 128), size)


def turn(v, cos, sin):
    return v * cos + pltpu.roll(v, HD // 2, 1) * sin


def turn_heads(v, table, sign):
    cos, sin = table[:, :HD], table[:, HD:]
    heads = [turn(v[:, h : h + HD], cos, sign * sin) for h in range(0, v.shape[1], HD)]
    return heads[0] if len(heads) == 1 else jnp.concatenate(heads, axis=1)


def qkv_kernel(n, *refs):
    me, xs, refs = refs[0], refs[1 : 1 + n], refs[1 + n :]
    key, select_tok, hi, lo, w, b_in, q, kv, rank_q, rank_kv, rows_own, tok_own, a_in, wide_w, *refs = refs
    hot, rows, sel, table = refs
    i = pl.program_id(0)
    tok, k, slots = hi.shape[1], b_in.shape[0], hot.shape[0]
    own = w.shape[1]
    mine = pl.ds(pl.multiple_of(me[0] * own, own), own)

    @pl.when(i == 0)
    def start():
        a_in[...] = jnp.zeros(a_in.shape, BF16)

    fill_map(me, xs, i, a_in.at[:k])
    wide_w[:, :own] = w[...]
    wide_w[:, own:] = a_in[...].T

    @pl.when(i < EXPERTS)
    def query():
        fill_hot(key, hot)
        fill_rows(me, hot, xs, k, rows)
        fill_select(hot, select_tok, sel)
        for b in range(n):
            here = pl.ds(b * CAP, CAP)
            table[here, :] = dot_nn(hot[here, :], hi[b]) + dot_nn(hot[here, :], lo[b])
        both = dot_nn(rows[:slots, :], wide_w[...])
        rank = (both[:, own : own + k] * sel[:slots, :]).astype(BF16)
        rank_q[...] = rank
        pre = both[:, :own] + dot_nn(rank, b_in[...])
        q[...] = turn_heads(pre, table[:slots, :], 1.0).astype(BF16)
        rows_own[...] = rows[:slots, mine]

    @pl.when(i >= EXPERTS)
    def key_value():
        group = n // 2
        some = pl.ds(0, group * tok)
        for half in range(2):
            for j in range(group):
                m = half * group + j
                b = me[0] ^ m
                here = pl.ds(j * tok, tok)
                rows[here, :] = xs[m][pl.ds(k, tok), :]
                sel[here, :] = select_tok[b].astype(F32)
                table[here, :] = hi[b].astype(F32) + lo[b].astype(F32)
            both = dot_nn(rows[some, :], wide_w[...])
            rank = (both[:, own : own + k] * sel[some, :]).astype(BF16)
            pre = both[:, :own] + dot_nn(rank, b_in[...])
            turned = turn_heads(pre, table[some, :], 1.0)
            done = jnp.where(i == EXPERTS, turned, pre).astype(BF16)
            for j in range(group):
                there = block_of(me[0] ^ (half * group + j), tok)
                here = slice(j * tok, (j + 1) * tok)
                rank_kv[there, :] = rank[here]
                kv[there, :] = done[here]
                tok_own[there, :] = rows[here, mine]


def limits(key, begin, b):
    tok = begin.shape[1]
    slot = lax.broadcasted_iota(jnp.int32, (CAP, tok), 0)
    token = b * tok + lax.broadcasted_iota(jnp.int32, (CAP, tok), 1)
    first, last = [], []
    for e in range(EXPERTS):
        chosen = slot == key[e : e + 1, :]
        first.append(jnp.sum(jnp.where(chosen, begin[...], 0), axis=1, keepdims=True))
        last.append(jnp.sum(jnp.where(chosen, token, 0), axis=1, keepdims=True))
    return jnp.concatenate(first), jnp.concatenate(last)


def attend_kernel(key, begin, q, k, v, mixed, lse, scores, mx, tot, acc):
    b = pl.program_id(0)
    tok, own = begin.shape[1], q.shape[2]
    rows = q.shape[0] * q.shape[1]
    first, last = limits(key, begin, b)
    query = q[...].reshape(rows, own)
    heads = [slice(h, h + HD) for h in range(0, own, HD)]
    count = (b * tok + tok + CHUNK - 1) // CHUNK
    mx[...] = jnp.full(mx.shape, NEG, F32)

    def score(j, carry):
        start = pl.multiple_of(j * CHUNK, CHUNK)
        here = pl.ds(start, CHUNK)
        at = start + lax.broadcasted_iota(jnp.int32, (rows, CHUNK), 1)
        seen = (at >= first) & (at <= last)
        raw = [dot_nt(query[:, h], k[here, h]) for h in heads]
        for i, h in enumerate(heads):
            s = jnp.where(seen, raw[i] * HD ** (-0.5), NEG)
            scores[i, :, here] = s
            mx[:, h] = jnp.maximum(mx[:, h], jnp.maximum(s[:, :HD], s[:, HD:]))
        return carry

    lax.fori_loop(0, count, score, 0)
    top = [jnp.max(mx[:, h], axis=1, keepdims=True) for h in heads]
    tot[...] = jnp.zeros(tot.shape, F32)
    acc[...] = jnp.zeros(acc.shape, F32)

    def mix(j, carry):
        here = pl.ds(pl.multiple_of(j * CHUNK, CHUNK), CHUNK)
        for i, h in enumerate(heads):
            p = jnp.exp(scores[i, :, here] - top[i])
            tot[:, h] += p[:, :HD] + p[:, HD:]
            acc[:, h] += dot_nn(p.astype(BF16), v[here, h])
        return carry

    lax.fori_loop(0, count, mix, 0)
    for i, h in enumerate(heads):
        total = jnp.sum(tot[:, h], axis=1, keepdims=True)
        mixed[:, :, h] = (acc[:, h] / total).astype(BF16).reshape(EXPERTS, CAP, HD)
        spread = jnp.broadcast_to(top[i] + jnp.log(total), (rows, HD))
        lse[:, :, h] = spread.reshape(EXPERTS, CAP, HD)


def attend_back_kernel(key, begin, q, g, mixed, lse, k, v, gq, gk, gv, dq):
    b = pl.program_id(0)
    tok, own = begin.shape[1], q.shape[2]
    rows = q.shape[0] * q.shape[1]
    scale = HD ** (-0.5)

    @pl.when(b == 0)
    def start():
        gk[...] = jnp.zeros(gk.shape, F32)
        gv[...] = jnp.zeros(gv.shape, F32)

    first, last = limits(key, begin, b)

    def flat(r):
        return r[...].reshape(rows, own)

    query, grad = flat(q), flat(g)
    heads = [slice(h, h + HD) for h in range(0, own, HD)]
    product = flat(mixed).astype(F32) * grad.astype(F32)
    delta = [jnp.sum(product[:, h], axis=1, keepdims=True) for h in heads]
    logs = flat(lse)
    log_total = [logs[:, h.start : h.start + 1] for h in heads]
    count = (b * tok + tok + CHUNK - 1) // CHUNK
    dq[...] = jnp.zeros(dq.shape, F32)

    def step(j, carry):
        begin_at = pl.multiple_of(j * CHUNK, CHUNK)
        here = pl.ds(begin_at, CHUNK)
        at = begin_at + lax.broadcasted_iota(jnp.int32, (rows, CHUNK), 1)
        seen = (at >= first) & (at <= last)
        raw = [dot_nt(query[:, h], k[here, h]) for h in heads]
        dps = [dot_nt(grad[:, h], v[here, h]) for h in heads]
        for i, h in enumerate(heads):
            p = jnp.where(seen, jnp.exp(raw[i] * scale - log_total[i]), 0.0)
            ds = (p * (dps[i] - delta[i])).astype(BF16)
            dq[:, h] += dot_nn(ds, k[here, h])
            gk[here, h] += dot_tn(ds, query[:, h]) * scale
            gv[here, h] += dot_tn(p.astype(BF16), grad[:, h])
        return carry

    lax.fori_loop(0, count, step, 0)
    gq[...] = (dq[...] * scale).reshape(gq.shape)


def out_kernel(n, first, stride, *refs):
    me, xs, refs = refs[0], refs[1 : 1 + n], refs[1 + n :]
    x, key, share, select_tok, down, w, near, far, live, maps, hot, sel, col, part, stage, acc = refs
    e = pl.program_id(0)
    k, slots = down.shape[0], x.shape[0]

    @pl.when(e == 0)
    def start():
        acc[...] = jnp.zeros(acc.shape, F32)
        stage[...] = jnp.zeros(stage.shape, F32)

    fill_map(me, xs, first + stride * e, maps)
    fill_hot(key, hot)
    fill_select(hot, select_tok, sel)
    fill_share(hot, share, col)
    rank = dot_nt(x[...], down[...]) * sel[...]
    stage[:, :k] = rank
    live[:, lanes(e, slots)] = live_rows(stage[...].T, 0, k).astype(BF16)
    rank = rank.astype(BF16)
    width = part.shape[1]
    for c in range(0, w.shape[1], width):
        at = pl.ds(c, width)
        y = dot_nn(x[...], w[:, at]) + dot_nn(rank, maps[:, at])
        part[...] = (y * col[:, :1]).astype(BF16)
        scatter_add(me, hot, part, acc, at)

    @pl.when(e == EXPERTS - 1)
    def finish():
        write_out(acc, near, far)


def back_kernel(n, first, stride, *refs):
    me, xs, ms, refs = refs[0], refs[1 : 1 + n], refs[1 + n : 1 + 2 * n], refs[1 + 2 * n :]
    key, select_tok, w, small, h, rank, rows_own, maps, hot, rows, sel = refs
    deep = w.shape[0]
    maps[:deep, :] = w[...]
    fill_map(me, ms, first + stride * pl.program_id(0), maps.at[deep:])
    fill_hot(key, hot)
    fill_rows(me, hot, xs, 0, rows)
    fill_select(hot, select_tok, sel)
    both = dot_nt(rows[...], maps[...])
    low = (both[:, deep:] * sel[...]).astype(BF16)
    rank[...] = low
    h[...] = both[:, :deep] + dot_nn(low, small[...])
    rows_own[...] = rows[:, lanes(me[0], rows_own.shape[1])]


def mixed_back_kernel(n, *refs):
    me, xs, ms, refs = refs[0], refs[1 : 1 + n], refs[1 + n : 1 + 2 * n], refs[1 + 2 * n :]
    key, share, select_tok, w, small, mixed, g, a_grad, dshare, rows_own, maps, *refs = refs
    hot, rows, sel, col, stage = refs
    e = pl.program_id(0)
    k, own, slots = small.shape[0], mixed.shape[1], mixed.shape[0]
    maps[:own, :] = w[...]
    fill_map(me, ms, e, maps.at[own:])

    @pl.when(e == 0)
    def start():
        stage[...] = jnp.zeros(stage.shape, F32)

    fill_hot(key, hot)
    fill_rows(me, hot, xs, 0, rows)
    fill_select(hot, select_tok, sel)
    fill_share(hot, share, col)
    both = dot_nt(rows[...], maps[...])
    low = (both[:, own:] * sel[...]).astype(BF16)
    h = both[:, :own] + dot_nn(low, small[...])
    stage[:, :1] = jnp.sum(mixed[...].astype(F32) * h, axis=1, keepdims=True)
    dshare[:, lanes(e, slots)] = stage[...].T[:8]
    g[...] = (h * col[:, :1]).astype(BF16)
    scaled = (low.astype(F32) * col[:, :k]).astype(BF16)
    a_grad[...] = dot_tn(scaled, mixed[...]).astype(BF16)
    rows_own[...] = rows[:, lanes(me[0], own)]


def feed_kernel(n, first, stride, *refs):
    me, xs, ms, refs = refs[0], refs[1 : 1 + n], refs[1 + n : 1 + 2 * n], refs[1 + 2 * n :]
    key, share, select_tok, wg, wu, hid, h, back_down, *refs = refs
    near, far, inner, live, dshare, h_grad, rows_own, *refs = refs
    hot, rows, sel, col, stage, both, gate, up, gg, gu, part, acc, sem = refs
    e = pl.program_id(0)
    k, own, slots = hid.shape[1], rows_own.shape[1], rows.shape[0]

    @pl.when(e == 0)
    def start():
        acc[...] = jnp.zeros(acc.shape, F32)
        stage[...] = jnp.zeros(stage.shape, F32)

    fill_hot(key, hot)
    fill_rows(me, hot, xs, 0, rows)
    fill_select(hot, select_tok, sel)
    fill_share(hot, share, col)
    fill_map(me, ms, first + stride * e, both.at[:k])
    fill_map(me, ms, first + stride * e + 1, both.at[k:])
    ranks = dot_nt(rows[...], both[...])
    rank_gate = (ranks[:, :k] * sel[...]).astype(BF16)
    rank_up = (ranks[:, k:] * sel[...]).astype(BF16)
    gate[...] = dot_nt(rows[...], wg[...]) + dot_nn(rank_gate, hid[0])
    up[...] = dot_nt(rows[...], wu[...]) + dot_nn(rank_up, hid[1])

    def point(b, carry):
        r = block_of(b, CAP)
        a, u, hh, s = gate[r, :], up[r, :], h[r, :], col[r, :1]
        sig = jax.nn.sigmoid(a)
        act = a * sig
        value = act * u
        inner[r, :] = value.astype(BF16)
        stage[r, 2 * k : 2 * k + 1] = jnp.sum(value * hh, axis=1, keepdims=True)
        scaled = hh * s
        gg[r, :] = (scaled * u * sig * (1.0 + a * (1.0 - sig))).astype(BF16)
        gu[r, :] = (scaled * act).astype(BF16)
        return carry

    lax.fori_loop(0, slots // CAP, point, 0)
    stage[:, :k] = dot_nt(gg[...], hid[0]) * sel[...]
    stage[:, k : 2 * k] = dot_nt(gu[...], hid[1]) * sel[...]
    stage[:, 128 : 128 + k] = dot_nt(inner[...], hid[2]) * sel[...]
    staged = stage[...].T
    live[:RANK, lanes(e, slots)] = live_rows(staged, 0, k).astype(BF16)
    live[RANK : 2 * RANK, lanes(e, slots)] = live_rows(staged, k, k).astype(BF16)
    live[2 * RANK :, lanes(e, slots)] = live_rows(staged, 128, k).astype(BF16)
    dshare[:, lanes(e, slots)] = staged[2 * k : 2 * k + 8]
    h_grad[0] = dot_tn(rank_gate, gg[...]).astype(BF16)
    h_grad[1] = dot_tn(rank_up, gu[...]).astype(BF16)
    scaled = (back_down[...].astype(F32) * col[:, :k]).astype(BF16)
    h_grad[2] = dot_tn(scaled, inner[...]).astype(BF16)
    rows_own[...] = rows[:, lanes(me[0], own)]
    back = stage[:, : 2 * k].astype(BF16)
    width = part.shape[1]
    for c in range(0, wg.shape[1], width):
        at = pl.ds(c, width)
        y = dot_nn(gg[...], wg[:, at]) + dot_nn(gu[...], wu[:, at]) + dot_nn(back, both[:, at])
        part[...] = y.astype(BF16)
        scatter_add(me, hot, part, acc, at)

    @pl.when(e == EXPERTS - 1)
    def finish():
        copy_out(acc, rows, near, far, sem)


def qkv_rank_kernel(
    key, select_tok, hi, lo, b_in, gq, gk, gv, rank_q, rank_kv,
    out_q, out_kv, back_q, back_kv, live, b_grad,
    hot, sel, table, stage,
):
    i = pl.program_id(0)
    n, tok, k = hi.shape[0], hi.shape[1], b_in.shape[0]
    slots, seq = gq.shape[0], gk.shape[0]

    @pl.when(i == 0)
    def start():
        stage[...] = jnp.zeros(stage.shape, F32)

    @pl.when(i < EXPERTS)
    def query():
        fill_hot(key, hot)
        fill_select(hot, select_tok, sel)
        for b in range(n):
            here = pl.ds(b * CAP, CAP)
            table[here, :] = dot_nn(hot[here, :], hi[b]) + dot_nn(hot[here, :], lo[b])
        g = turn_heads(gq[...], table[...], -1.0).astype(BF16)
        out_q[...] = g
        rank = dot_nt(g, b_in[...]) * sel[...]
        stage[:slots, :k] = rank
        back_q[...] = rank.astype(BF16)
        live[:, lanes(i, slots)] = live_rows(stage[:slots, :].T, 0, k).astype(BF16)
        b_grad[...] = dot_tn(rank_q[...], g).astype(BF16)

    @pl.when(i >= EXPERTS)
    def key_value():
        for b in range(n):
            here = pl.ds(b * tok, tok)
            both = hi[b].astype(F32) + lo[b].astype(F32)
            turned = turn_heads(gk[here, :], both, -1.0)
            out_kv[here, :] = jnp.where(i == EXPERTS, turned, gv[here, :]).astype(BF16)
            stage[here, k : 2 * k] = select_tok[b].astype(F32)
        g = out_kv[...]
        rank = dot_nt(g, b_in[...]) * stage[:seq, k : 2 * k]
        stage[:seq, :k] = rank
        back_kv[...] = rank.astype(BF16)
        b_grad[...] = dot_tn(rank_kv[...], g).astype(BF16)
        begin = EXPERTS * slots + (i - EXPERTS) * seq
        there = pl.ds(pl.multiple_of(begin, 128), seq)
        live[:, there] = live_rows(stage[:seq, :].T, 0, k).astype(BF16)


def qkv_back_kernel(n, *refs):
    me, xs, refs = refs[0], refs[1 : 1 + n], refs[1 + n :]
    key, w, gq, gkv, back_q, back_kv, near, far, maps, hot, part, acc, some_g, some_rank = refs
    i = pl.program_id(0)
    tok = hot.shape[1]
    wide = maps.shape[1]
    width = part.shape[1]
    fill_map(me, xs, i, maps)

    @pl.when(i == 0)
    def start():
        acc[...] = jnp.zeros(acc.shape, F32)

    @pl.when(i < EXPERTS)
    def query():
        fill_hot(key, hot)
        for c in range(0, wide, width):
            at = pl.ds(c, width)
            y = dot_nt(gq[...], w[at, :]) + dot_nn(back_q[...], maps[:, at])
            part[...] = y.astype(BF16)
            scatter_add(me, hot, part, acc, at)

    @pl.when(i >= EXPERTS)
    def key_value():
        group = n // 2
        size = group * tok
        for half in range(2):
            there = pl.ds(half * size, size)
            for j in range(group):
                block = block_of(me[0] ^ (2 * j + half), tok)
                some_g[j * tok : (j + 1) * tok, :] = gkv[block, :]
                some_rank[j * tok : (j + 1) * tok, :] = back_kv[block, :]
            for c in range(0, wide, width):
                at = pl.ds(c, width)
                acc[there, at] += dot_nt(some_g[...], w[at, :]) + dot_nn(some_rank[...], maps[:, at])

    @pl.when(i == EXPERTS + 1)
    def finish():
        write_out(acc, near, far)


def chunk_of(slots, wide):
    width = wide // 2
    while slots * width > 640 * 1024:
        width //= 2
    return width


def whole(shape):
    zeros = (0,) * len(shape)
    return pl.BlockSpec(shape, lambda *at: zeros, pipeline_mode=pl.Buffered(1))


def by_expert(shape, at=lambda i: i):
    rest = (0,) * len(shape)
    return pl.BlockSpec((None,) + shape, lambda i, *unused: (at(i),) + rest)


def shaped(shape, dtype):
    return jax.ShapeDtypeStruct(shape, dtype)


def run(kernel, name, steps, ins, outs, scratch, args, flops, scalars=1):
    call = pl.pallas_call(
        kernel,
        grid_spec=pltpu.PrefetchScalarGridSpec(
            num_scalar_prefetch=scalars,
            grid=steps,
            in_specs=ins,
            out_specs=[o[0] for o in outs],
            scratch_shapes=[pltpu.VMEM(*one) if isinstance(one, tuple) else one for one in scratch],
        ),
        out_shape=[shaped(o[1], o[2]) for o in outs],
        compiler_params=pltpu.CompilerParams(vmem_limit_bytes=62 << 20),
        cost_estimate=pl.CostEstimate(
            flops=int(flops), bytes_accessed=32 << 20, transcendentals=1 << 20
        ),
        name=name,
    )
    return call(*args)


def last_expert(i):
    return jnp.minimum(i, EXPERTS - 1)


def from_expert(i):
    return jnp.maximum(i - EXPERTS, 0)


def rows_spec(x, rows=None):
    return whole((x.shape[0] if rows is None else rows, x.shape[1]))


def sides(n, tok, wide):
    shape = (n // 2, tok, wide)
    return [(whole(shape), shape, BF16)] * 2


def qkv(me, pieces, key, select_tok, hi, lo, w, b_in):
    n, tok, k = select_tok.shape
    wide, own, slots, seq = pieces[0].shape[1], w.shape[2], n * CAP, n * tok
    return run(
        partial(qkv_kernel, n),
        "qkv",
        (EXPERTS + 2,),
        [rows_spec(p) for p in pieces]
        + [by_expert((n, tok), last_expert), whole(select_tok.shape), whole(hi.shape),
           whole(lo.shape), by_expert((wide, own)), by_expert((k, own))],
        [
            (by_expert((slots, own), last_expert), (EXPERTS, slots, own), BF16),
            (by_expert((seq, own), from_expert), (2, seq, own), BF16),
            (by_expert((slots, k), last_expert), (EXPERTS, slots, k), BF16),
            (by_expert((seq, k), from_expert), (2, seq, k), BF16),
            (by_expert((slots, own), last_expert), (EXPERTS, slots, own), BF16),
            (whole((seq, own)), (seq, own), BF16),
        ],
        [((128, wide), BF16), ((wide, own + 128), BF16), ((slots, tok), BF16),
         ((max(slots, seq // 2), wide), BF16),
         ((max(slots, seq // 2), k), F32), ((max(slots, seq // 2), 2 * HD), F32)],
        (me, *pieces, key, select_tok, hi, lo, w, b_in),
        2 * wide * own * (EXPERTS * slots + 2 * seq) * 1.5,
    )


def attend_specs(n, tok, own):
    slot_spec = pl.BlockSpec((EXPERTS, None, CAP, own), lambda b: (0, b, 0, 0))
    tokens = [pl.BlockSpec((None, EXPERTS, tok), lambda b: (b, 0, 0)),
              pl.BlockSpec((None, 1, tok), lambda b: (b, 0, 0))]
    return slot_spec, tokens, whole((n * tok, own)), (EXPERTS, n, CAP, own)


def attend(key, begin, q, k, v):
    n, tok = begin.shape[0], begin.shape[2]
    own, seq, rows = q.shape[2], n * tok, EXPERTS * CAP
    slot_spec, tokens, all_spec, shape = attend_specs(n, tok, own)
    mixed, lse = run(
        attend_kernel,
        "attend",
        (n,),
        tokens + [slot_spec, all_spec, all_spec],
        [(slot_spec, shape, BF16), (slot_spec, shape, F32)],
        [((own // HD, rows, seq), F32), ((rows, own), F32), ((rows, own), F32), ((rows, own), F32)],
        (key, begin, q.reshape(shape), k, v),
        3 * rows * seq * own * n,
        0,
    )
    return mixed.reshape(q.shape), lse


def attend_back(key, begin, q, g, mixed, lse, k, v):
    n, tok = begin.shape[0], begin.shape[2]
    own, seq, rows = q.shape[2], n * tok, EXPERTS * CAP
    slot_spec, tokens, all_spec, shape = attend_specs(n, tok, own)
    gq, gk, gv = run(
        attend_back_kernel,
        "attend_back",
        (n,),
        tokens + [slot_spec] * 4 + [all_spec] * 2,
        [(slot_spec, shape, F32), (all_spec, (seq, own), F32), (all_spec, (seq, own), F32)],
        [((rows, own), F32)],
        (key, begin, q.reshape(shape), g.reshape(shape), mixed.reshape(shape), lse, k, v),
        7 * rows * seq * own * n,
        0,
    )
    return gq.reshape(q.shape), gk, gv


def weight_spec(w, p=None):
    if p is None:
        return by_expert(w.shape[1:])
    return pl.BlockSpec((None, None) + w.shape[2:], lambda e, *unused: (e, p, 0, 0))


def project_out(name, me, x, key, share, select_tok, down, w, pieces, groups, first, stride, p=None):
    n, tok, k = select_tok.shape
    wide, slots, deep = pieces[0].shape[1], n * CAP, x.shape[2]
    down_spec = by_expert((k, deep)) if p is None else weight_spec(down, p)
    return run(
        partial(out_kernel, n, first, stride),
        name,
        (EXPERTS,),
        [rows_spec(m, groups * k) for m in pieces]
        + [by_expert((slots, deep)), by_expert((n, tok)), by_expert((n, tok)), whole(select_tok.shape),
           down_spec, weight_spec(w, p)],
        sides(n, tok, wide) + [(whole((RANK, EXPERTS * slots)), (RANK, EXPERTS * slots), BF16)],
        [((k, wide), BF16), ((slots, tok), BF16), ((slots, k), F32), ((slots, 128), F32),
         ((slots, chunk_of(slots, wide)), BF16), ((slots, 128), F32), ((n * tok, wide), F32)],
        (me, *pieces, x, key, share, select_tok, down, w),
        2 * wide * deep * EXPERTS * slots * 1.5,
    )


def feed_back_down(me, tokens, pieces, groups, first, stride, key, select_tok, w, small):
    n, tok, k = select_tok.shape
    wide, slots, deep = pieces[0].shape[1], n * CAP, w.shape[2]
    own = wide // n
    return run(
        partial(back_kernel, n, first, stride),
        "feed_down_back",
        (EXPERTS,),
        [rows_spec(m) for m in tokens] + [rows_spec(m, groups * k) for m in pieces]
        + [by_expert((n, tok)), whole(select_tok.shape), weight_spec(w, 2), weight_spec(small, 2)],
        [(by_expert((slots, deep)), (EXPERTS, slots, deep), F32),
         (by_expert((slots, k)), (EXPERTS, slots, k), BF16),
         (by_expert((slots, own)), (EXPERTS, slots, own), BF16)],
        [((deep + k, wide), BF16), ((slots, tok), BF16), ((slots, wide), BF16), ((slots, k), F32)],
        (me, *tokens, *pieces, key, select_tok, w, small),
        2 * wide * deep * EXPERTS * slots * 1.3,
    )


def mixed_back(me, tokens, pieces, groups, key, share, select_tok, w, small, mixed):
    n, tok, k = select_tok.shape
    wide, slots, own = pieces[0].shape[1], n * CAP, w.shape[1]
    return run(
        partial(mixed_back_kernel, n),
        "mixed_back",
        (EXPERTS,),
        [rows_spec(m) for m in tokens] + [rows_spec(m, groups * k) for m in pieces]
        + [by_expert((n, tok)), by_expert((n, tok)), whole(select_tok.shape),
           weight_spec(w), by_expert((k, own)), by_expert((slots, own))],
        [(by_expert((slots, own)), (EXPERTS, slots, own), BF16),
         (by_expert((k, own)), (EXPERTS, k, own), BF16),
         (whole((8, EXPERTS * slots)), (8, EXPERTS * slots), F32),
         (by_expert((slots, own)), (EXPERTS, slots, own), BF16)],
        [((own + k, wide), BF16), ((slots, tok), BF16), ((slots, wide), BF16), ((slots, k), F32),
         ((slots, 128), F32), ((slots, 128), F32)],
        (me, *tokens, *pieces, key, share, select_tok, w, small, mixed),
        2 * wide * own * EXPERTS * slots * 1.5,
    )


def feed(me, tokens, pieces, groups, first, stride, key, share, select_tok, w, hid, h, back_down):
    n, tok, k = select_tok.shape
    wide, slots, deep = pieces[0].shape[1], n * CAP, w.shape[2]
    own = wide // n
    return run(
        partial(feed_kernel, n, first, stride),
        "feed",
        (EXPERTS,),
        [rows_spec(m) for m in tokens] + [rows_spec(m, groups * k) for m in pieces]
        + [by_expert((n, tok)), by_expert((n, tok)),
           whole(select_tok.shape), weight_spec(w, 0), weight_spec(w, 1), by_expert((3, k, deep)),
           by_expert((slots, deep)), by_expert((slots, k))],
        [(pl.BlockSpec(memory_space=pl.ANY), (n // 2 * tok, wide), BF16)] * 2
        + [(by_expert((slots, deep)), (EXPERTS, slots, deep), BF16),
           (whole((3 * RANK, EXPERTS * slots)), (3 * RANK, EXPERTS * slots), BF16),
           (whole((8, EXPERTS * slots)), (8, EXPERTS * slots), F32),
           (by_expert((3, k, deep)), (EXPERTS, 3, k, deep), BF16),
           (by_expert((slots, own)), (EXPERTS, slots, own), BF16)],
        [((slots, tok), BF16), ((slots, wide), BF16), ((slots, k), F32), ((slots, 128), F32),
         ((slots, 256), F32), ((2 * k, wide), BF16), ((slots, deep), F32), ((slots, deep), F32),
         ((slots, deep), BF16), ((slots, deep), BF16), ((slots, chunk_of(slots, wide)), BF16),
         ((n * tok, wide), F32), pltpu.SemaphoreType.DMA],
        (me, *tokens, *pieces, key, share, select_tok, w, w, hid, h, back_down),
        8 * wide * deep * EXPERTS * slots * 1.3,
    )


def qkv_rank(key, select_tok, hi, lo, b_in, gq, gk, gv, rank_q, rank_kv):
    n, tok, k = select_tok.shape
    own, slots, seq = gq.shape[2], n * CAP, n * tok
    total = EXPERTS * slots + 2 * seq
    return run(
        qkv_rank_kernel,
        "qkv_rank",
        (EXPERTS + 2,),
        [by_expert((n, tok), last_expert), whole(select_tok.shape), whole(hi.shape),
         whole(lo.shape), by_expert((k, own)),
         by_expert((slots, own), last_expert), whole((seq, own)), whole((seq, own)),
         by_expert((slots, k), last_expert), by_expert((seq, k), from_expert)],
        [(by_expert((slots, own), last_expert), (EXPERTS, slots, own), BF16),
         (by_expert((seq, own), from_expert), (2, seq, own), BF16),
         (by_expert((slots, k), last_expert), (EXPERTS, slots, k), BF16),
         (by_expert((seq, k), from_expert), (2, seq, k), BF16),
         (whole((RANK, total)), (RANK, total), BF16),
         (by_expert((k, own)), (EXPERTS + 2, k, own), BF16)],
        [((slots, tok), BF16), ((slots, k), F32), ((slots, 2 * HD), F32), ((max(slots, seq), 128), F32)],
        (key, select_tok, hi, lo, b_in, gq, gk, gv, rank_q, rank_kv),
        4 * k * own * (EXPERTS * slots + 2 * seq),
        0,
    )


def qkv_back(me, pieces, key, w, gq, gkv, back_q, back_kv):
    n, tok = key.shape[1:]
    k, own, slots, seq = back_q.shape[2], w.shape[2], n * CAP, n * tok
    wide = pieces[0].shape[1]
    return run(
        partial(qkv_back_kernel, n),
        "qkv_back",
        (EXPERTS + 2,),
        [rows_spec(m, k) for m in pieces]
        + [by_expert((n, tok), last_expert), by_expert((wide, own)),
           by_expert((slots, own), last_expert), by_expert((seq, own), from_expert),
           by_expert((slots, k), last_expert), by_expert((seq, k), from_expert)],
        sides(n, tok, wide),
        [((k, wide), BF16), ((slots, tok), BF16), ((slots, chunk_of(slots, wide)), BF16),
         ((seq, wide), F32), ((seq // 2, own), BF16), ((seq // 2, k), BF16)],
        (me, *pieces, key, w, gq, gkv, back_q, back_kv),
        2 * wide * own * (EXPERTS * slots + 2 * seq) * 1.5,
    )


def members(routes):
    names = jnp.arange(EXPERTS, dtype=jnp.int32)[None, :, None]
    member = (routes[:, :1] == names) | (routes[:, 1:] == names)
    tok = routes.shape[-1]
    before = (jnp.arange(tok)[:, None] < jnp.arange(tok)[None, :]).astype(BF16)
    rank = ein("met,tu->meu", member.astype(BF16), before).astype(jnp.int32)
    return jnp.where(member, rank, -1)


def own_shares(normed, router, routes):
    names = jnp.arange(EXPERTS, dtype=jnp.int32)[:, None]
    member = (routes[:1] == names) | (routes[1:] == names)
    logits = ein("td,de->et", normed, router)
    return jax.nn.softmax(jnp.where(member, logits, -jnp.inf), axis=0)


def route_back(share, grad_share, router):
    grad = share * (grad_share - jnp.sum(share * grad_share, axis=0, keepdims=True))
    return jnp.einsum("et,de->td", grad, router.astype(F32), precision=lax.Precision.HIGHEST)


def local(
    n,
    reps,
    layer_input_state,
    cotangent,
    norm_gain_vectors,
    attention_router_weight,
    feed_router_weight,
    attention_query_weight,
    key_value_weight,
    attention_output_weight,
    feed_expert_weight,
    attention_adapters,
    feed_adapter_width,
    feed_adapter_hidden,
    token_document,
    document_adapter,
    attention_expert_pairs,
    feed_expert_pairs,
):
    tok, wide = layer_input_state.shape
    own, slots = wide // n, n * CAP
    columns = attention_adapters.shape[3]
    me = lax.axis_index("shard")
    me_ref = me.reshape(1).astype(jnp.int32)
    segments = token_document[0]
    seq = segments.shape[0]
    docs = document_adapter[0]
    doc_count = docs.shape[0]
    k = doc_count * RANK

    def one_hot(which):
        at = which[:, None] * RANK + jnp.arange(RANK)[None, :]
        return (at.reshape(-1)[:, None] == jnp.arange(columns)[None, :]).astype(BF16)

    pick = one_hot(docs)
    attn_small = ein("kc,pmwc->pmkw", pick, attention_adapters).astype(BF16)
    width_small = ein("kc,pmwc->pmkw", pick, feed_adapter_width).astype(BF16)
    hidden_small = ein("kc,epcf->epkf", pick, feed_adapter_hidden).astype(BF16)
    b_in, a_out = attn_small[1, : EXPERTS + 2], attn_small[0, EXPERTS + 2 :]

    x = layer_input_state.astype(F32)
    gain_one = norm_gain_vectors[0].astype(F32)
    gain_two = norm_gain_vectors[1].astype(F32)
    normed_own = rms_norm(gain_one, x).astype(BF16)
    routes = jnp.concatenate([attention_expert_pairs.T, feed_expert_pairs.T])
    own_a = own_shares(normed_own, attention_router_weight, routes[:2])
    own_hi = own_a.astype(BF16)
    own_lo = (own_a - lax.reduce_precision(own_a, 8, 7)).astype(BF16)
    spare = jnp.stack([routes.astype(BF16).reshape(-1), own_hi.reshape(-1), own_lo.reshape(-1)])
    first = jnp.concatenate([pack_maps(attn_small[0, : EXPERTS + 2], n, spare), normed_own])
    def send(g):
        return [lax.ppermute(g, "rep", [(i, i ^ d) for i in range(reps)]) if d else g for d in range(reps)]

    weights = [attention_query_weight, key_value_weight]
    picks_sent = send(docs)
    if n == 8:
        cut = (first.shape[0] // 2 + 15) // 16 * 16
        y0, x1 = swap(first[:cut], n, 4), swap(first[cut:], n, 2)
        y1, x0 = swap(first[cut:], n, 4), swap(first[:cut], n, 2)
        y0, x1, *weights = tie(y0, x1, *weights)
        d0, d1, *picks_sent = tie(swap(y0, n, 2), swap(x1, n, 4), *picks_sent)
        chips = {0: first}
        for m, p in ((2, (x0, x1)), (4, (y0, y1)), (6, (d0, d1))):
            chips[m] = jnp.concatenate(p)
    else:
        chips = across(first, n)
    pieces = from_sibling(chips, n)
    w_in = reshard(weights, me, n)

    facts = jnp.stack([p[:3, (EXPERTS + 2) * own : (EXPERTS + 2) * own + EXPERTS * tok] for p in pieces])
    facts = facts[jnp.arange(n) ^ me].reshape(n, 3, EXPERTS, tok)
    routes = facts[:, 0].astype(jnp.int32)
    share_a = facts[:, 1].astype(F32) + facts[:, 2].astype(F32)

    second = jnp.concatenate([attn_small[1, EXPERTS + 2 :], width_small.reshape(-1, k, own)])
    groups = -(-second.shape[0] // n)
    second, w_in = tie(pack_maps(second, n), w_in)
    map_chips = across(second, n)

    begins = jnp.sum((segments[None, :] < jnp.arange(doc_count)[:, None]).astype(jnp.int32), axis=1)
    doc = segments.reshape(n, tok)
    place = jnp.arange(seq, dtype=jnp.int32).reshape(n, tok)
    doc_table = doc[None] == jnp.arange(doc_count, dtype=jnp.int32)[:, None, None]
    begin = jnp.sum(jnp.where(doc_table, begins[:, None, None], 0), axis=0)
    freq = jnp.exp(-jnp.arange(HD // 2, dtype=F32) * (2.0 * math.log(10000.0) / HD))
    angles = (place - begin).astype(F32)[..., None] * freq
    cos, sin = jnp.cos(angles), jnp.sin(angles)
    table = jnp.concatenate([cos, cos, -sin, sin], axis=-1)
    table_hi = table.astype(BF16)
    table_lo = (table - lax.reduce_precision(table, 8, 7)).astype(BF16)
    chosen_doc = jnp.arange(k, dtype=jnp.int32)[None, None, :] // RANK
    select_tok = (doc[:, :, None] == chosen_doc).astype(BF16)
    select_row = doc_table.astype(F32).reshape(1, doc_count, seq)

    slot_a, slot_f = members(routes[:, :2]), members(routes[:, 2:])
    routes_f_own = feed_expert_pairs.T
    key_a, key_f = slot_a.transpose(1, 0, 2), slot_f.transpose(1, 0, 2)

    def slot_select(slot):
        hot = slot[:, :, None, :] == jnp.arange(CAP, dtype=jnp.int32)[None, None, :, None]
        chose = hot[:, :, None] & doc_table.transpose(1, 0, 2)[:, None, :, None, :]
        select = jnp.any(chose, axis=-1).astype(F32)
        return select.transpose(1, 2, 0, 3).reshape(EXPERTS, doc_count, slots)

    select_a, select_f = slot_select(slot_a), slot_select(slot_f)

    share_ae = share_a.transpose(1, 0, 2)
    q, kv, rank_q, rank_kv, rows_a_own, normed_own_columns = qkv(
        me_ref, pieces, key_a, select_tok, table_hi, table_lo, w_in, b_in
    )
    q, cotangent_sent, *sent = tie(q, cotangent, *map_chips.values())
    cotangent_chips = across(cotangent_sent, n)
    maps = from_sibling(dict(zip(map_chips, sent)), n)
    mixed, lse = attend(slot_a, begin[:, None], q, kv[0], kv[1])
    near, far, live_o = project_out(
        "attend_out", me_ref, mixed, key_a, share_ae, select_tok, a_out, attention_output_weight, maps, groups, 0, 1
    )
    near, far, *sent = tie(near, far, *cotangent_chips.values())
    attn_total, attn_low = halve(near, far, n)
    grads_out_all = from_sibling(dict(zip(cotangent_chips, sent)), n)
    *attn_low, key_late = tie(*attn_low, key_f)

    def slot_row(share, slot):
        hot = slot[:, :, None, :] == jnp.arange(CAP, dtype=jnp.int32)[None, None, :, None]
        row = jnp.sum(jnp.where(hot, share[:, :, None, :], 0.0), axis=-1)
        return row.transpose(1, 0, 2).reshape(EXPERTS, 1, slots)

    w_feed = jnp.swapaxes(feed_expert_weight, 2, 3)
    grad_inner, back_down, rows_g_own = feed_back_down(
        me_ref, grads_out_all, maps, groups, EXPERTS + 2, 3, key_late, select_tok, w_feed, hidden_small
    )
    attn_total, grad_inner = tie(attn_total, grad_inner)
    attended = x + collect(attn_total, attn_low, n)
    normed_two_own = rms_norm(gain_two, attended).astype(BF16)
    chips = across(normed_two_own, n)
    scaled_a = select_a * slot_row(share_a, slot_a)
    select_a, select_f, scaled_a, *sent = tie(select_a, select_f, scaled_a, *chips.values())
    normed_two = from_sibling(dict(zip(chips, sent)), n)
    own_f = own_shares(normed_two_own, feed_router_weight, routes_f_own)
    share_f = gather_small(own_f, me, n)
    share_fe = share_f.transpose(1, 0, 2)
    near, far, inner, live_f, dshare_f, hidden_grad, rows_f_own = feed(
        me_ref, normed_two, maps, groups, EXPERTS, 3, key_f, share_fe, select_tok, w_feed, hidden_small,
        grad_inner, back_down,
    )
    near, far = near.reshape(n // 2, tok, wide), far.reshape(n // 2, tok, wide)
    two_total, two_low = halve(near, far, n)
    dshare_f = dshare_f[:1]
    dshare_f = dshare_f + swap(dshare_f, n, 1)
    *two_low, inner, dshare_f, live_f, live_o = tie(*two_low, inner, dshare_f, live_f, live_o)
    live_f = jnp.concatenate([live_f, live_o])
    live_f = live_f + swap(live_f, n, 1)
    near, far, unused = project_out(
        "feed_out", me_ref, inner, key_f, share_fe, select_tok, hidden_small, w_feed, maps, groups, EXPERTS + 2, 3, 2
    )
    two_got = [swap(part, n, 2 * i + 2) for i, part in enumerate(two_low)]
    near, far, *two_got = tie(near, far, *two_got)
    grad_two_own = added([two_total] + two_got)

    def own_tokens(slot, dshare):
        mine = lax.dynamic_slice_in_dim(dshare.reshape(EXPERTS, n, CAP), me, 1, 1)[:, 0]
        hot = lax.dynamic_slice_in_dim(slot, me, 1, 0)[0][:, None, :] == jnp.arange(CAP)[None, :, None]
        return jnp.sum(jnp.where(hot, mine[:, :, None], 0.0), axis=1)

    d = 2
    while d < n:
        dshare_f, d = dshare_f + swap(dshare_f, n, d), 2 * d
    grad_two_own = grad_two_own + route_back(own_f, own_tokens(slot_f, dshare_f), feed_router_weight)
    grad_attended = cotangent.astype(F32) + rms_back(attended, gain_two, grad_two_own)

    grad_sent, near, far = tie(grad_attended.astype(BF16), near, far)
    out_total, out_low = halve(near, far, n)
    chips = across(grad_sent, n)
    out_total, *sent = tie(out_total, *out_low, *chips.values())
    out_low, sent = sent[: n // 2 - 1], sent[n // 2 - 1 :]
    grads_two = from_sibling(dict(zip(chips, sent)), n)
    mixed_late, live_f = tie(mixed, live_f)
    live_f_sent = list(across(live_f, n).values())
    grad_mixed, a_out_grad, dshare_a, rows_ga_own = mixed_back(
        me_ref, grads_two, maps, groups, key_a, share_ae, select_tok, attention_output_weight, a_out, mixed_late
    )
    grad_mixed, *sent = tie(grad_mixed, *live_f_sent, *out_low)
    live_f_sent, out_low = sent[: n // 2], sent[n // 2 :]
    gq, gk, gv = attend_back(slot_a, begin[:, None], q, grad_mixed, mixed, lse, kv[0], kv[1])
    out_got = [swap(part, n, 2 * i + 2) for i, part in enumerate(out_low)]
    gq, *sent = tie(gq, *live_f_sent, *out_got)
    live_f_sent, out_got = sent[: n // 2], sent[n // 2 :]
    live_f = added(live_f_sent)
    live_f, live_o = live_f[: 3 * RANK], live_f[3 * RANK :]

    def spread(live, select):
        both = live.astype(F32)[:, None] * select[:, :, None, :]
        return both.reshape(live.shape[0], k, live.shape[2]).astype(BF16)

    def of_slots(live):
        return live.reshape(RANK, EXPERTS, slots).transpose(1, 0, 2)

    def grads(rank, rows):
        return ein("eks,esw->ekw", rank, rows).astype(BF16)

    def by_stream(sent):
        out = jnp.zeros((reps,) + sent[0].shape, sent[0].dtype)
        for d, got in enumerate(sent):
            out = lax.dynamic_update_slice_in_dim(out, got[None], lax.axis_index("rep") ^ d, 0)
        return out

    scaled_f = select_f * slot_row(share_f, slot_f)
    width_grad = jnp.stack(
        [
            grads(spread(of_slots(live_f[:RANK]), select_f), rows_f_own),
            grads(spread(of_slots(live_f[RANK : 2 * RANK]), select_f), rows_f_own),
            grads(spread(of_slots(live_f[2 * RANK :]), scaled_f), rows_g_own),
        ],
        axis=1,
    )
    b_out_grad = grads(spread(of_slots(live_o), scaled_a), rows_ga_own)
    early_grad = jnp.concatenate([a_out_grad, b_out_grad])
    layer_out = attended + added([out_total] + out_got)
    gq, gkv, back_q, back_kv, live_in, b_in_grad = qkv_rank(
        key_a, select_tok, table_hi, table_lo, b_in, gq, gk, gv, rank_q, rank_kv
    )
    dshare_a = dshare_a[0].astype(BF16).reshape(RANK, -1)
    spare = -dshare_a.shape[1] % 128
    live_in = jnp.concatenate([live_in, jnp.pad(dshare_a, ((0, 0), (0, spare)))], axis=1)
    live_in = live_in + swap(live_in, n, 1)
    gq, live_in, b_in_grad, early_grad, width_grad = tie(gq, live_in, b_in_grad, early_grad, width_grad)
    hidden_all, width_all = lax.all_gather(hidden_grad, "rep"), lax.all_gather(width_grad, "rep")
    early_sent = send(early_grad)
    live_sent, late_b_sent = list(across(live_in, n).values()), send(b_in_grad)
    near, far = qkv_back(me_ref, pieces, key_a, w_in, gq, gkv, back_q, back_kv)
    near, far, *sent = tie(near, far, *live_sent, *early_sent)
    live_sent, early_sent = sent[: n // 2], sent[n // 2 :]
    in_total, in_low = (quarter if n == 8 else halve)(near, far, n)
    *in_low, first_sent = tie(*in_low, live_sent[0])
    in_got = [swap(part, n, 2 * i + 2) for i, part in enumerate(in_low)]
    live_in = added([first_sent] + live_sent[1:])
    width = EXPERTS * slots + 2 * seq
    dshare_a = live_in[:, width : width + EXPERTS * slots // RANK]
    live_kv = live_in[:, EXPERTS * slots : width].reshape(RANK, 2, seq).transpose(1, 0, 2)
    a_in_grad = jnp.concatenate(
        [
            grads(spread(of_slots(live_in[:, : EXPERTS * slots]), select_a), rows_a_own),
            ein("pks,sw->pkw", spread(live_kv, select_row), normed_own_columns).astype(BF16),
        ]
    )
    a_in_grad, hidden_all, *sent = tie(a_in_grad, hidden_all, *late_b_sent, *in_got)
    late_b_sent, in_got = sent[:reps], sent[reps:]
    late_a_sent = send(a_in_grad)
    grad_normed = collect_quarters(in_total, in_got, n) if n == 8 else added([in_total] + in_got)
    grad_normed = grad_normed + route_back(own_a, own_tokens(slot_a, dshare_a), attention_router_weight)
    grad_normed, width_all = tie(grad_normed, width_all)
    grad_in = grad_attended + rms_back(x, gain_one, grad_normed)

    picks = jax.vmap(one_hot)(jnp.stack(picks_sent)[jnp.arange(reps) ^ lax.axis_index("rep")])
    early = by_stream(early_sent)
    hidden_out = ein("rpekf,rkc->pecf", hidden_all, picks)
    width_out = ein("rpmkw,rkc->pmwc", width_all, picks)
    late_b, late_a = by_stream(late_b_sent), by_stream(late_a_sent)
    attn = jnp.concatenate([late_a, early[:, :EXPERTS], late_b, early[:, EXPERTS:]], axis=1)
    attn = attn.reshape(reps, 2, -1, k, own)
    attn_out = ein("rpmkw,rkc->pmwc", attn, picks)
    return (layer_out, grad_in, attn_out, width_out, hidden_out)


def solution(mesh):
    in_specs = (
        P(("rep", "shard"), None),
        P(("rep", "shard"), None),
        P(),
        P(),
        P(),
        P(None, "shard", None),
        P(None, "shard", None),
        P(None, "shard", None),
        P(None, None, None, "shard"),
        P(None, None, "shard", None),
        P(None, None, "shard", None),
        P(None, None, None, "shard"),
        P("rep", None),
        P("rep", None),
        P(("rep", "shard"), None),
        P(("rep", "shard"), None),
    )
    out_specs = (
        P(("rep", "shard"), None),
        P(("rep", "shard"), None),
        P(None, None, "shard", None),
        P(None, None, "shard", None),
        P(None, None, None, "shard"),
    )
    body = partial(local, mesh.shape["shard"], mesh.shape["rep"])
    return jax.shard_map(body, mesh=mesh, in_specs=in_specs, out_specs=out_specs, check_vma=False)
```

```python
from functools import partial
import math

import jax
import jax.numpy as jnp
from jax import lax
from jax.experimental import pallas as pl
from jax.experimental.pallas import tpu as pltpu
from jax.sharding import PartitionSpec as P

HD = 128
RANK = 16
CAP = 80
EXPERTS = 4
CHUNK = 256
EPS = 1e-05
NEG = -1e30
F32 = jnp.float32
BF16 = jnp.bfloat16


def ein(spec, a, b):
    return jnp.einsum(spec, a, b, preferred_element_type=F32)


def rms_norm(gain, values):
    return values * lax.rsqrt(jnp.mean(values * values, axis=-1, keepdims=True) + EPS) * gain


def rms_back(values, gain, grad):
    unused, backward_function = jax.vjp(partial(rms_norm, gain), values)
    return backward_function(grad)[0]


NT = (((1,), (1,)), ((), ()))
TN = (((0,), (0,)), ((), ()))


def dot_nt(a, b):
    return lax.dot_general(a, b, NT, preferred_element_type=F32)


def dot_tn(a, b):
    return lax.dot_general(a, b, TN, preferred_element_type=F32)


def dot_nn(a, b):
    return jnp.dot(a, b, preferred_element_type=F32)


def swap(x, n, d):
    return lax.ppermute(x, "shard", [(i, i ^ d) for i in range(n)])


def tie(*values):
    return lax.optimization_barrier(values)


def across(x, n):
    return {d: swap(x, n, d) if d else x for d in range(0, n, 2)}


def from_sibling(pieces, n):
    other = {m ^ 1: swap(p, n, 1) for m, p in pieces.items()}
    return [p for unused, p in sorted({**pieces, **other}.items())]


def gather_small(x, me, n):
    mine = jnp.stack(list(across(x, n).values()))
    mask = jnp.arange(n) ^ me
    return jnp.concatenate([mine, swap(mine, n, 1)])[mask // 2 + mask % 2 * (n // 2)]


def halve(near, far, n):
    got = swap(far, n, 1)
    sums = [near[i].astype(F32) + got[i].astype(F32) for i in range(n // 2)]
    return sums[0], [one.astype(BF16) for one in sums[1:]]


def added(parts):
    return sum([part.astype(F32) for part in parts[1:]], parts[0].astype(F32))


def quarter(near, far, n):
    got = swap(far, n, 1)
    cut = near.shape[1] // 2

    def total(i, at):
        return near[i, at].astype(F32) + got[i, at].astype(F32)

    top, low = slice(0, cut), slice(cut, None)
    sent = [jnp.stack([total(i, at).astype(BF16) for i in pair]) for at, pair in ((top, (1, 3)), (low, (2, 3)))]
    return [total(0, top), total(2, top), total(0, low), total(1, low)], sent


def collect_quarters(kept, got, n):
    a0, a2, b0, b1 = kept
    ra, rb = got[0].astype(F32), got[1].astype(F32)
    a2, b1 = (a2 + ra[1]).astype(BF16), (b1 + rb[1]).astype(BF16)
    a0 = a0 + ra[0] + swap(a2, n, 4).astype(F32)
    b0 = b0 + rb[0] + swap(b1, n, 2).astype(F32)
    return jnp.concatenate([a0, b0])


def collect(total, low, n):
    for i, part in enumerate(low):
        total = total + swap(part, n, 2 * i + 2).astype(F32)
    return total


def reshard(ws, me, n):
    rows, width = ws[0].shape[1], ws[0].shape[2] // n
    count = sum(w.shape[0] for w in ws)
    out = jnp.zeros((count, n * rows, width), ws[0].dtype)
    for m in sorted(range(n), key=lambda m: -m):
        piece = jnp.concatenate([lax.dynamic_slice_in_dim(w, (me ^ m) * width, width, 2) for w in ws])
        piece = swap(piece, n, m) if m else piece
        out = lax.dynamic_update_slice_in_dim(out, piece, (me ^ m) * rows, 1)
    return out


def pack_maps(maps, n, spare=None):
    count, k, own = maps.shape
    groups = -(-count // n)
    fill = groups * n - count
    flat = [maps[i] for i in range(count)]
    if fill:
        rest = jnp.zeros((k, fill * own), maps.dtype)
        if spare is not None:
            rest = rest.at[: spare.shape[0], : spare.shape[1]].set(spare)
        flat.append(rest)
    rows = [jnp.concatenate(flat[g * n : (g + 1) * n], axis=1) for g in range(groups)]
    return jnp.concatenate(rows) if groups > 1 else rows[0]


def fill_hot(key, hot):
    n, tok = key.shape
    slot = lax.broadcasted_iota(jnp.int32, (CAP, tok), 0)
    for b in range(n):
        one = jnp.where(slot == key[b : b + 1, :], 1.0, 0.0)
        hot[b * CAP : (b + 1) * CAP, :] = one.astype(BF16)


def block_of(b, size):
    return pl.ds(pl.multiple_of(b * size, 16), size)


def fill_rows(me, hot, xs, base, rows):
    tok = hot.shape[1]
    for m, x in enumerate(xs):
        here = block_of(me[0] ^ m, CAP)
        rows[here, :] = dot_nn(hot[here, :], x[pl.ds(base, tok), :]).astype(BF16)


def fill_map(me, xs, index, out):
    n, k = len(xs), out.shape[0]
    own = out.shape[1] // n
    group, column = index // n, index % n
    for m, x in enumerate(xs):
        part = x[block_of(group, k), pl.ds(pl.multiple_of(column * own, own), own)]
        out[:, pl.ds(pl.multiple_of((me[0] ^ m) * own, own), own)] = part


def fill_select(hot, select_tok, sel):
    for b in range(select_tok.shape[0]):
        here = pl.ds(b * CAP, CAP)
        sel[here, :] = dot_nn(hot[here, :], select_tok[b])


def fill_share(hot, share, col):
    for b in range(share.shape[0]):
        here = pl.ds(b * CAP, CAP)
        one = jnp.sum(hot[here, :].astype(F32) * share[b : b + 1, :], axis=1, keepdims=True)
        col[here, :] = jnp.broadcast_to(one, (CAP, col.shape[1]))


def scatter_add(me, hot, y, acc, at):
    tok = hot.shape[1]
    n = acc.shape[0] // tok
    for b in range(n):
        mask = me[0] ^ b
        there = block_of(mask // 2 + (mask % 2) * (n // 2), tok)
        acc[there, at] += dot_tn(hot[pl.ds(b * CAP, CAP), :], y[pl.ds(b * CAP, CAP), :])


def copy_out(acc, rows, near, far, sem):
    half = acc.shape[0] // 2
    for side, ref in enumerate((near, far)):
        rows[:half, :] = acc[side * half : (side + 1) * half, :].astype(BF16)
        copy = pltpu.make_async_copy(rows.at[pl.ds(0, half)], ref, sem)
        copy.start()
        copy.wait()


def write_out(acc, near, far):
    half = acc.shape[0] // 2
    near[...] = acc[:half, :].astype(BF16).reshape(near.shape)
    far[...] = acc[half:, :].astype(BF16).reshape(far.shape)


def live_rows(staged, first, k):
    total = staged[first : first + RANK]
    for d in range(1, k // RANK):
        total = total + staged[first + d * RANK : first + (d + 1) * RANK]
    return total


def lanes(e, size):
    return pl.ds(pl.multiple_of(e * size, 128), size)


def turn(v, cos, sin):
    return v * cos + pltpu.roll(v, HD // 2, 1) * sin


def turn_heads(v, table, sign):
    cos, sin = table[:, :HD], table[:, HD:]
    heads = [turn(v[:, h : h + HD], cos, sign * sin) for h in range(0, v.shape[1], HD)]
    return heads[0] if len(heads) == 1 else jnp.concatenate(heads, axis=1)


def qkv_kernel(n, *refs):
    me, xs, refs = refs[0], refs[1 : 1 + n], refs[1 + n :]
    key, select_tok, hi, lo, w, b_in, q, kv, rank_q, rank_kv, rows_own, tok_own, a_in, wide_w, *refs = refs
    hot, rows, sel, table = refs
    i = pl.program_id(0)
    tok, k, slots = hi.shape[1], b_in.shape[0], hot.shape[0]
    own = w.shape[1]
    mine = pl.ds(pl.multiple_of(me[0] * own, own), own)

    @pl.when(i == 0)
    def start():
        a_in[...] = jnp.zeros(a_in.shape, BF16)

    fill_map(me, xs, i, a_in.at[:k])
    wide_w[:, :own] = w[...]
    wide_w[:, own:] = a_in[...].T

    @pl.when(i < EXPERTS)
    def query():
        fill_hot(key, hot)
        fill_rows(me, hot, xs, k, rows)
        fill_select(hot, select_tok, sel)
        for b in range(n):
            here = pl.ds(b * CAP, CAP)
            table[here, :] = dot_nn(hot[here, :], hi[b]) + dot_nn(hot[here, :], lo[b])
        both = dot_nn(rows[:slots, :], wide_w[...])
        rank = (both[:, own : own + k] * sel[:slots, :]).astype(BF16)
        rank_q[...] = rank
        pre = both[:, :own] + dot_nn(rank, b_in[...])
        q[...] = turn_heads(pre, table[:slots, :], 1.0).astype(BF16)
        rows_own[...] = rows[:slots, mine]

    @pl.when(i >= EXPERTS)
    def key_value():
        group = n // 2
        some = pl.ds(0, group * tok)
        for half in range(2):
            for j in range(group):
                m = half * group + j
                b = me[0] ^ m
                here = pl.ds(j * tok, tok)
                rows[here, :] = xs[m][pl.ds(k, tok), :]
                sel[here, :] = select_tok[b].astype(F32)
                table[here, :] = hi[b].astype(F32) + lo[b].astype(F32)
            both = dot_nn(rows[some, :], wide_w[...])
            rank = (both[:, own : own + k] * sel[some, :]).astype(BF16)
            pre = both[:, :own] + dot_nn(rank, b_in[...])
            turned = turn_heads(pre, table[some, :], 1.0)
            done = jnp.where(i == EXPERTS, turned, pre).astype(BF16)
            for j in range(group):
                there = block_of(me[0] ^ (half * group + j), tok)
                here = slice(j * tok, (j + 1) * tok)
                rank_kv[there, :] = rank[here]
                kv[there, :] = done[here]
                tok_own[there, :] = rows[here, mine]


def limits(key, begin, b):
    tok = begin.shape[1]
    slot = lax.broadcasted_iota(jnp.int32, (CAP, tok), 0)
    token = b * tok + lax.broadcasted_iota(jnp.int32, (CAP, tok), 1)
    first, last = [], []
    for e in range(EXPERTS):
        chosen = slot == key[e : e + 1, :]
        first.append(jnp.sum(jnp.where(chosen, begin[...], 0), axis=1, keepdims=True))
        last.append(jnp.sum(jnp.where(chosen, token, 0), axis=1, keepdims=True))
    return jnp.concatenate(first), jnp.concatenate(last)


def attend_kernel(key, begin, q, k, v, mixed, lse, scores, mx, tot, acc):
    b = pl.program_id(0)
    tok, own = begin.shape[1], q.shape[2]
    rows = q.shape[0] * q.shape[1]
    first, last = limits(key, begin, b)
    query = q[...].reshape(rows, own)
    heads = [slice(h, h + HD) for h in range(0, own, HD)]
    count = (b * tok + tok + CHUNK - 1) // CHUNK
    mx[...] = jnp.full(mx.shape, NEG, F32)

    def score(j, carry):
        start = pl.multiple_of(j * CHUNK, CHUNK)
        here = pl.ds(start, CHUNK)
        at = start + lax.broadcasted_iota(jnp.int32, (rows, CHUNK), 1)
        seen = (at >= first) & (at <= last)
        raw = [dot_nt(query[:, h], k[here, h]) for h in heads]
        for i, h in enumerate(heads):
            s = jnp.where(seen, raw[i] * HD ** (-0.5), NEG)
            scores[i, :, here] = s
            mx[:, h] = jnp.maximum(mx[:, h], jnp.maximum(s[:, :HD], s[:, HD:]))
        return carry

    lax.fori_loop(0, count, score, 0)
    top = [jnp.max(mx[:, h], axis=1, keepdims=True) for h in heads]
    tot[...] = jnp.zeros(tot.shape, F32)
    acc[...] = jnp.zeros(acc.shape, F32)

    def mix(j, carry):
        here = pl.ds(pl.multiple_of(j * CHUNK, CHUNK), CHUNK)
        for i, h in enumerate(heads):
            p = jnp.exp(scores[i, :, here] - top[i])
            tot[:, h] += p[:, :HD] + p[:, HD:]
            acc[:, h] += dot_nn(p.astype(BF16), v[here, h])
        return carry

    lax.fori_loop(0, count, mix, 0)
    for i, h in enumerate(heads):
        total = jnp.sum(tot[:, h], axis=1, keepdims=True)
        mixed[:, :, h] = (acc[:, h] / total).astype(BF16).reshape(EXPERTS, CAP, HD)
        spread = jnp.broadcast_to(top[i] + jnp.log(total), (rows, HD))
        lse[:, :, h] = spread.reshape(EXPERTS, CAP, HD)


def attend_back_kernel(key, begin, q, g, mixed, lse, k, v, gq, gk, gv, dq):
    b = pl.program_id(0)
    tok, own = begin.shape[1], q.shape[2]
    rows = q.shape[0] * q.shape[1]
    scale = HD ** (-0.5)

    @pl.when(b == 0)
    def start():
        gk[...] = jnp.zeros(gk.shape, F32)
        gv[...] = jnp.zeros(gv.shape, F32)

    first, last = limits(key, begin, b)

    def flat(r):
        return r[...].reshape(rows, own)

    query, grad = flat(q), flat(g)
    heads = [slice(h, h + HD) for h in range(0, own, HD)]
    product = flat(mixed).astype(F32) * grad.astype(F32)
    delta = [jnp.sum(product[:, h], axis=1, keepdims=True) for h in heads]
    logs = flat(lse)
    log_total = [logs[:, h.start : h.start + 1] for h in heads]
    count = (b * tok + tok + CHUNK - 1) // CHUNK
    dq[...] = jnp.zeros(dq.shape, F32)

    def step(j, carry):
        begin_at = pl.multiple_of(j * CHUNK, CHUNK)
        here = pl.ds(begin_at, CHUNK)
        at = begin_at + lax.broadcasted_iota(jnp.int32, (rows, CHUNK), 1)
        seen = (at >= first) & (at <= last)
        raw = [dot_nt(query[:, h], k[here, h]) for h in heads]
        dps = [dot_nt(grad[:, h], v[here, h]) for h in heads]
        for i, h in enumerate(heads):
            p = jnp.where(seen, jnp.exp(raw[i] * scale - log_total[i]), 0.0)
            ds = (p * (dps[i] - delta[i])).astype(BF16)
            dq[:, h] += dot_nn(ds, k[here, h])
            gk[here, h] += dot_tn(ds, query[:, h]) * scale
            gv[here, h] += dot_tn(p.astype(BF16), grad[:, h])
        return carry

    lax.fori_loop(0, count, step, 0)
    gq[...] = (dq[...] * scale).reshape(gq.shape)


def out_kernel(n, first, stride, *refs):
    me, xs, refs = refs[0], refs[1 : 1 + n], refs[1 + n :]
    x, key, share, select_tok, down, w, near, far, live, maps, hot, sel, col, part, stage, acc = refs
    e = pl.program_id(0)
    k, slots = down.shape[0], x.shape[0]

    @pl.when(e == 0)
    def start():
        acc[...] = jnp.zeros(acc.shape, F32)
        stage[...] = jnp.zeros(stage.shape, F32)

    fill_map(me, xs, first + stride * e, maps)
    fill_hot(key, hot)
    fill_select(hot, select_tok, sel)
    fill_share(hot, share, col)
    rank = dot_nt(x[...], down[...]) * sel[...]
    stage[:, :k] = rank
    live[:, lanes(e, slots)] = live_rows(stage[...].T, 0, k).astype(BF16)
    rank = rank.astype(BF16)
    width = part.shape[1]
    for c in range(0, w.shape[1], width):
        at = pl.ds(c, width)
        y = dot_nn(x[...], w[:, at]) + dot_nn(rank, maps[:, at])
        part[...] = (y * col[:, :1]).astype(BF16)
        scatter_add(me, hot, part, acc, at)

    @pl.when(e == EXPERTS - 1)
    def finish():
        write_out(acc, near, far)


def back_kernel(n, first, stride, *refs):
    me, xs, ms, refs = refs[0], refs[1 : 1 + n], refs[1 + n : 1 + 2 * n], refs[1 + 2 * n :]
    key, select_tok, w, small, h, rank, rows_own, maps, hot, rows, sel = refs
    deep = w.shape[0]
    maps[:deep, :] = w[...]
    fill_map(me, ms, first + stride * pl.program_id(0), maps.at[deep:])
    fill_hot(key, hot)
    fill_rows(me, hot, xs, 0, rows)
    fill_select(hot, select_tok, sel)
    both = dot_nt(rows[...], maps[...])
    low = (both[:, deep:] * sel[...]).astype(BF16)
    rank[...] = low
    h[...] = both[:, :deep] + dot_nn(low, small[...])
    rows_own[...] = rows[:, lanes(me[0], rows_own.shape[1])]


def mixed_back_kernel(n, *refs):
    me, xs, ms, refs = refs[0], refs[1 : 1 + n], refs[1 + n : 1 + 2 * n], refs[1 + 2 * n :]
    key, share, select_tok, w, small, mixed, g, a_grad, dshare, rows_own, maps, *refs = refs
    hot, rows, sel, col, stage = refs
    e = pl.program_id(0)
    k, own, slots = small.shape[0], mixed.shape[1], mixed.shape[0]
    maps[:own, :] = w[...]
    fill_map(me, ms, e, maps.at[own:])

    @pl.when(e == 0)
    def start():
        stage[...] = jnp.zeros(stage.shape, F32)

    fill_hot(key, hot)
    fill_rows(me, hot, xs, 0, rows)
    fill_select(hot, select_tok, sel)
    fill_share(hot, share, col)
    both = dot_nt(rows[...], maps[...])
    low = (both[:, own:] * sel[...]).astype(BF16)
    h = both[:, :own] + dot_nn(low, small[...])
    stage[:, :1] = jnp.sum(mixed[...].astype(F32) * h, axis=1, keepdims=True)
    dshare[:, lanes(e, slots)] = stage[...].T[:8]
    g[...] = (h * col[:, :1]).astype(BF16)
    scaled = (low.astype(F32) * col[:, :k]).astype(BF16)
    a_grad[...] = dot_tn(scaled, mixed[...]).astype(BF16)
    rows_own[...] = rows[:, lanes(me[0], own)]


def feed_kernel(n, first, stride, *refs):
    me, xs, ms, refs = refs[0], refs[1 : 1 + n], refs[1 + n : 1 + 2 * n], refs[1 + 2 * n :]
    key, share, select_tok, wg, wu, hid, h, back_down, *refs = refs
    near, far, inner, live, dshare, h_grad, rows_own, *refs = refs
    hot, rows, sel, col, stage, both, gate, up, gg, gu, part, acc, sem = refs
    e = pl.program_id(0)
    k, own, slots = hid.shape[1], rows_own.shape[1], rows.shape[0]

    @pl.when(e == 0)
    def start():
        acc[...] = jnp.zeros(acc.shape, F32)
        stage[...] = jnp.zeros(stage.shape, F32)

    fill_hot(key, hot)
    fill_rows(me, hot, xs, 0, rows)
    fill_select(hot, select_tok, sel)
    fill_share(hot, share, col)
    fill_map(me, ms, first + stride * e, both.at[:k])
    fill_map(me, ms, first + stride * e + 1, both.at[k:])
    ranks = dot_nt(rows[...], both[...])
    rank_gate = (ranks[:, :k] * sel[...]).astype(BF16)
    rank_up = (ranks[:, k:] * sel[...]).astype(BF16)
    gate[...] = dot_nt(rows[...], wg[...]) + dot_nn(rank_gate, hid[0])
    up[...] = dot_nt(rows[...], wu[...]) + dot_nn(rank_up, hid[1])

    def point(b, carry):
        r = block_of(b, CAP)
        a, u, hh, s = gate[r, :], up[r, :], h[r, :], col[r, :1]
        sig = jax.nn.sigmoid(a)
        act = a * sig
        value = act * u
        inner[r, :] = value.astype(BF16)
        stage[r, 2 * k : 2 * k + 1] = jnp.sum(value * hh, axis=1, keepdims=True)
        scaled = hh * s
        gg[r, :] = (scaled * u * sig * (1.0 + a * (1.0 - sig))).astype(BF16)
        gu[r, :] = (scaled * act).astype(BF16)
        return carry

    lax.fori_loop(0, slots // CAP, point, 0)
    stage[:, :k] = dot_nt(gg[...], hid[0]) * sel[...]
    stage[:, k : 2 * k] = dot_nt(gu[...], hid[1]) * sel[...]
    stage[:, 128 : 128 + k] = dot_nt(inner[...], hid[2]) * sel[...]
    staged = stage[...].T
    live[:RANK, lanes(e, slots)] = live_rows(staged, 0, k).astype(BF16)
    live[RANK : 2 * RANK, lanes(e, slots)] = live_rows(staged, k, k).astype(BF16)
    live[2 * RANK :, lanes(e, slots)] = live_rows(staged, 128, k).astype(BF16)
    dshare[:, lanes(e, slots)] = staged[2 * k : 2 * k + 8]
    h_grad[0] = dot_tn(rank_gate, gg[...]).astype(BF16)
    h_grad[1] = dot_tn(rank_up, gu[...]).astype(BF16)
    scaled = (back_down[...].astype(F32) * col[:, :k]).astype(BF16)
    h_grad[2] = dot_tn(scaled, inner[...]).astype(BF16)
    rows_own[...] = rows[:, lanes(me[0], own)]
    back = stage[:, : 2 * k].astype(BF16)
    width = part.shape[1]
    for c in range(0, wg.shape[1], width):
        at = pl.ds(c, width)
        y = dot_nn(gg[...], wg[:, at]) + dot_nn(gu[...], wu[:, at]) + dot_nn(back, both[:, at])
        part[...] = y.astype(BF16)
        scatter_add(me, hot, part, acc, at)

    @pl.when(e == EXPERTS - 1)
    def finish():
        copy_out(acc, rows, near, far, sem)


def qkv_rank_kernel(
    key, select_tok, hi, lo, b_in, gq, gk, gv, rank_q, rank_kv,
    out_q, out_kv, back_q, back_kv, live, b_grad,
    hot, sel, table, stage,
):
    i = pl.program_id(0)
    n, tok, k = hi.shape[0], hi.shape[1], b_in.shape[0]
    slots, seq = gq.shape[0], gk.shape[0]

    @pl.when(i == 0)
    def start():
        stage[...] = jnp.zeros(stage.shape, F32)

    @pl.when(i < EXPERTS)
    def query():
        fill_hot(key, hot)
        fill_select(hot, select_tok, sel)
        for b in range(n):
            here = pl.ds(b * CAP, CAP)
            table[here, :] = dot_nn(hot[here, :], hi[b]) + dot_nn(hot[here, :], lo[b])
        g = turn_heads(gq[...], table[...], -1.0).astype(BF16)
        out_q[...] = g
        rank = dot_nt(g, b_in[...]) * sel[...]
        stage[:slots, :k] = rank
        back_q[...] = rank.astype(BF16)
        live[:, lanes(i, slots)] = live_rows(stage[:slots, :].T, 0, k).astype(BF16)
        b_grad[...] = dot_tn(rank_q[...], g).astype(BF16)

    @pl.when(i >= EXPERTS)
    def key_value():
        for b in range(n):
            here = pl.ds(b * tok, tok)
            both = hi[b].astype(F32) + lo[b].astype(F32)
            turned = turn_heads(gk[here, :], both, -1.0)
            out_kv[here, :] = jnp.where(i == EXPERTS, turned, gv[here, :]).astype(BF16)
            stage[here, k : 2 * k] = select_tok[b].astype(F32)
        g = out_kv[...]
        rank = dot_nt(g, b_in[...]) * stage[:seq, k : 2 * k]
        stage[:seq, :k] = rank
        back_kv[...] = rank.astype(BF16)
        b_grad[...] = dot_tn(rank_kv[...], g).astype(BF16)
        begin = EXPERTS * slots + (i - EXPERTS) * seq
        there = pl.ds(pl.multiple_of(begin, 128), seq)
        live[:, there] = live_rows(stage[:seq, :].T, 0, k).astype(BF16)


def qkv_back_kernel(n, *refs):
    me, xs, refs = refs[0], refs[1 : 1 + n], refs[1 + n :]
    key, w, gq, gkv, back_q, back_kv, near, far, maps, hot, part, acc, some_g, some_rank = refs
    i = pl.program_id(0)
    tok = hot.shape[1]
    wide = maps.shape[1]
    width = part.shape[1]
    fill_map(me, xs, i, maps)

    @pl.when(i == 0)
    def start():
        acc[...] = jnp.zeros(acc.shape, F32)

    @pl.when(i < EXPERTS)
    def query():
        fill_hot(key, hot)
        for c in range(0, wide, width):
            at = pl.ds(c, width)
            y = dot_nt(gq[...], w[at, :]) + dot_nn(back_q[...], maps[:, at])
            part[...] = y.astype(BF16)
            scatter_add(me, hot, part, acc, at)

    @pl.when(i >= EXPERTS)
    def key_value():
        group = n // 2
        size = group * tok
        for half in range(2):
            there = pl.ds(half * size, size)
            for j in range(group):
                block = block_of(me[0] ^ (2 * j + half), tok)
                some_g[j * tok : (j + 1) * tok, :] = gkv[block, :]
                some_rank[j * tok : (j + 1) * tok, :] = back_kv[block, :]
            for c in range(0, wide, width):
                at = pl.ds(c, width)
                acc[there, at] += dot_nt(some_g[...], w[at, :]) + dot_nn(some_rank[...], maps[:, at])

    @pl.when(i == EXPERTS + 1)
    def finish():
        write_out(acc, near, far)


def chunk_of(slots, wide):
    width = wide // 2
    while slots * width > 640 * 1024:
        width //= 2
    return width


def whole(shape):
    zeros = (0,) * len(shape)
    return pl.BlockSpec(shape, lambda *at: zeros, pipeline_mode=pl.Buffered(1))


def by_expert(shape, at=lambda i: i):
    rest = (0,) * len(shape)
    return pl.BlockSpec((None,) + shape, lambda i, *unused: (at(i),) + rest)


def shaped(shape, dtype):
    return jax.ShapeDtypeStruct(shape, dtype)


def run(kernel, name, steps, ins, outs, scratch, args, flops, scalars=1):
    call = pl.pallas_call(
        kernel,
        grid_spec=pltpu.PrefetchScalarGridSpec(
            num_scalar_prefetch=scalars,
            grid=steps,
            in_specs=ins,
            out_specs=[o[0] for o in outs],
            scratch_shapes=[pltpu.VMEM(*one) if isinstance(one, tuple) else one for one in scratch],
        ),
        out_shape=[shaped(o[1], o[2]) for o in outs],
        compiler_params=pltpu.CompilerParams(vmem_limit_bytes=62 << 20),
        cost_estimate=pl.CostEstimate(
            flops=int(flops), bytes_accessed=32 << 20, transcendentals=1 << 20
        ),
        name=name,
    )
    return call(*args)


def last_expert(i):
    return jnp.minimum(i, EXPERTS - 1)


def from_expert(i):
    return jnp.maximum(i - EXPERTS, 0)


def rows_spec(x, rows=None):
    return whole((x.shape[0] if rows is None else rows, x.shape[1]))


def sides(n, tok, wide):
    shape = (n // 2, tok, wide)
    return [(whole(shape), shape, BF16)] * 2


def qkv(me, pieces, key, select_tok, hi, lo, w, b_in):
    n, tok, k = select_tok.shape
    wide, own, slots, seq = pieces[0].shape[1], w.shape[2], n * CAP, n * tok
    return run(
        partial(qkv_kernel, n),
        "qkv",
        (EXPERTS + 2,),
        [rows_spec(p) for p in pieces]
        + [by_expert((n, tok), last_expert), whole(select_tok.shape), whole(hi.shape),
           whole(lo.shape), by_expert((wide, own)), by_expert((k, own))],
        [
            (by_expert((slots, own), last_expert), (EXPERTS, slots, own), BF16),
            (by_expert((seq, own), from_expert), (2, seq, own), BF16),
            (by_expert((slots, k), last_expert), (EXPERTS, slots, k), BF16),
            (by_expert((seq, k), from_expert), (2, seq, k), BF16),
            (by_expert((slots, own), last_expert), (EXPERTS, slots, own), BF16),
            (whole((seq, own)), (seq, own), BF16),
        ],
        [((128, wide), BF16), ((wide, own + 128), BF16), ((slots, tok), BF16),
         ((max(slots, seq // 2), wide), BF16),
         ((max(slots, seq // 2), k), F32), ((max(slots, seq // 2), 2 * HD), F32)],
        (me, *pieces, key, select_tok, hi, lo, w, b_in),
        2 * wide * own * (EXPERTS * slots + 2 * seq) * 1.5,
    )


def attend_specs(n, tok, own):
    slot_spec = pl.BlockSpec((EXPERTS, None, CAP, own), lambda b: (0, b, 0, 0))
    tokens = [pl.BlockSpec((None, EXPERTS, tok), lambda b: (b, 0, 0)),
              pl.BlockSpec((None, 1, tok), lambda b: (b, 0, 0))]
    return slot_spec, tokens, whole((n * tok, own)), (EXPERTS, n, CAP, own)


def attend(key, begin, q, k, v):
    n, tok = begin.shape[0], begin.shape[2]
    own, seq, rows = q.shape[2], n * tok, EXPERTS * CAP
    slot_spec, tokens, all_spec, shape = attend_specs(n, tok, own)
    mixed, lse = run(
        attend_kernel,
        "attend",
        (n,),
        tokens + [slot_spec, all_spec, all_spec],
        [(slot_spec, shape, BF16), (slot_spec, shape, F32)],
        [((own // HD, rows, seq), F32), ((rows, own), F32), ((rows, own), F32), ((rows, own), F32)],
        (key, begin, q.reshape(shape), k, v),
        3 * rows * seq * own * n,
        0,
    )
    return mixed.reshape(q.shape), lse


def attend_back(key, begin, q, g, mixed, lse, k, v):
    n, tok = begin.shape[0], begin.shape[2]
    own, seq, rows = q.shape[2], n * tok, EXPERTS * CAP
    slot_spec, tokens, all_spec, shape = attend_specs(n, tok, own)
    gq, gk, gv = run(
        attend_back_kernel,
        "attend_back",
        (n,),
        tokens + [slot_spec] * 4 + [all_spec] * 2,
        [(slot_spec, shape, F32), (all_spec, (seq, own), F32), (all_spec, (seq, own), F32)],
        [((rows, own), F32)],
        (key, begin, q.reshape(shape), g.reshape(shape), mixed.reshape(shape), lse, k, v),
        7 * rows * seq * own * n,
        0,
    )
    return gq.reshape(q.shape), gk, gv


def weight_spec(w, p=None):
    if p is None:
        return by_expert(w.shape[1:])
    return pl.BlockSpec((None, None) + w.shape[2:], lambda e, *unused: (e, p, 0, 0))


def project_out(name, me, x, key, share, select_tok, down, w, pieces, groups, first, stride, p=None):
    n, tok, k = select_tok.shape
    wide, slots, deep = pieces[0].shape[1], n * CAP, x.shape[2]
    down_spec = by_expert((k, deep)) if p is None else weight_spec(down, p)
    return run(
        partial(out_kernel, n, first, stride),
        name,
        (EXPERTS,),
        [rows_spec(m, groups * k) for m in pieces]
        + [by_expert((slots, deep)), by_expert((n, tok)), by_expert((n, tok)), whole(select_tok.shape),
           down_spec, weight_spec(w, p)],
        sides(n, tok, wide) + [(whole((RANK, EXPERTS * slots)), (RANK, EXPERTS * slots), BF16)],
        [((k, wide), BF16), ((slots, tok), BF16), ((slots, k), F32), ((slots, 128), F32),
         ((slots, chunk_of(slots, wide)), BF16), ((slots, 128), F32), ((n * tok, wide), F32)],
        (me, *pieces, x, key, share, select_tok, down, w),
        2 * wide * deep * EXPERTS * slots * 1.5,
    )


def feed_back_down(me, tokens, pieces, groups, first, stride, key, select_tok, w, small):
    n, tok, k = select_tok.shape
    wide, slots, deep = pieces[0].shape[1], n * CAP, w.shape[2]
    own = wide // n
    return run(
        partial(back_kernel, n, first, stride),
        "feed_down_back",
        (EXPERTS,),
        [rows_spec(m) for m in tokens] + [rows_spec(m, groups * k) for m in pieces]
        + [by_expert((n, tok)), whole(select_tok.shape), weight_spec(w, 2), weight_spec(small, 2)],
        [(by_expert((slots, deep)), (EXPERTS, slots, deep), F32),
         (by_expert((slots, k)), (EXPERTS, slots, k), BF16),
         (by_expert((slots, own)), (EXPERTS, slots, own), BF16)],
        [((deep + k, wide), BF16), ((slots, tok), BF16), ((slots, wide), BF16), ((slots, k), F32)],
        (me, *tokens, *pieces, key, select_tok, w, small),
        2 * wide * deep * EXPERTS * slots * 1.3,
    )


def mixed_back(me, tokens, pieces, groups, key, share, select_tok, w, small, mixed):
    n, tok, k = select_tok.shape
    wide, slots, own = pieces[0].shape[1], n * CAP, w.shape[1]
    return run(
        partial(mixed_back_kernel, n),
        "mixed_back",
        (EXPERTS,),
        [rows_spec(m) for m in tokens] + [rows_spec(m, groups * k) for m in pieces]
        + [by_expert((n, tok)), by_expert((n, tok)), whole(select_tok.shape),
           weight_spec(w), by_expert((k, own)), by_expert((slots, own))],
        [(by_expert((slots, own)), (EXPERTS, slots, own), BF16),
         (by_expert((k, own)), (EXPERTS, k, own), BF16),
         (whole((8, EXPERTS * slots)), (8, EXPERTS * slots), F32),
         (by_expert((slots, own)), (EXPERTS, slots, own), BF16)],
        [((own + k, wide), BF16), ((slots, tok), BF16), ((slots, wide), BF16), ((slots, k), F32),
         ((slots, 128), F32), ((slots, 128), F32)],
        (me, *tokens, *pieces, key, share, select_tok, w, small, mixed),
        2 * wide * own * EXPERTS * slots * 1.5,
    )


def feed(me, tokens, pieces, groups, first, stride, key, share, select_tok, w, hid, h, back_down):
    n, tok, k = select_tok.shape
    wide, slots, deep = pieces[0].shape[1], n * CAP, w.shape[2]
    own = wide // n
    return run(
        partial(feed_kernel, n, first, stride),
        "feed",
        (EXPERTS,),
        [rows_spec(m) for m in tokens] + [rows_spec(m, groups * k) for m in pieces]
        + [by_expert((n, tok)), by_expert((n, tok)),
           whole(select_tok.shape), weight_spec(w, 0), weight_spec(w, 1), by_expert((3, k, deep)),
           by_expert((slots, deep)), by_expert((slots, k))],
        [(pl.BlockSpec(memory_space=pl.ANY), (n // 2 * tok, wide), BF16)] * 2
        + [(by_expert((slots, deep)), (EXPERTS, slots, deep), BF16),
           (whole((3 * RANK, EXPERTS * slots)), (3 * RANK, EXPERTS * slots), BF16),
           (whole((8, EXPERTS * slots)), (8, EXPERTS * slots), F32),
           (by_expert((3, k, deep)), (EXPERTS, 3, k, deep), BF16),
           (by_expert((slots, own)), (EXPERTS, slots, own), BF16)],
        [((slots, tok), BF16), ((slots, wide), BF16), ((slots, k), F32), ((slots, 128), F32),
         ((slots, 256), F32), ((2 * k, wide), BF16), ((slots, deep), F32), ((slots, deep), F32),
         ((slots, deep), BF16), ((slots, deep), BF16), ((slots, chunk_of(slots, wide)), BF16),
         ((n * tok, wide), F32), pltpu.SemaphoreType.DMA],
        (me, *tokens, *pieces, key, share, select_tok, w, w, hid, h, back_down),
        8 * wide * deep * EXPERTS * slots * 1.3,
    )


def qkv_rank(key, select_tok, hi, lo, b_in, gq, gk, gv, rank_q, rank_kv):
    n, tok, k = select_tok.shape
    own, slots, seq = gq.shape[2], n * CAP, n * tok
    total = EXPERTS * slots + 2 * seq
    return run(
        qkv_rank_kernel,
        "qkv_rank",
        (EXPERTS + 2,),
        [by_expert((n, tok), last_expert), whole(select_tok.shape), whole(hi.shape),
         whole(lo.shape), by_expert((k, own)),
         by_expert((slots, own), last_expert), whole((seq, own)), whole((seq, own)),
         by_expert((slots, k), last_expert), by_expert((seq, k), from_expert)],
        [(by_expert((slots, own), last_expert), (EXPERTS, slots, own), BF16),
         (by_expert((seq, own), from_expert), (2, seq, own), BF16),
         (by_expert((slots, k), last_expert), (EXPERTS, slots, k), BF16),
         (by_expert((seq, k), from_expert), (2, seq, k), BF16),
         (whole((RANK, total)), (RANK, total), BF16),
         (by_expert((k, own)), (EXPERTS + 2, k, own), BF16)],
        [((slots, tok), BF16), ((slots, k), F32), ((slots, 2 * HD), F32), ((max(slots, seq), 128), F32)],
        (key, select_tok, hi, lo, b_in, gq, gk, gv, rank_q, rank_kv),
        4 * k * own * (EXPERTS * slots + 2 * seq),
        0,
    )


def qkv_back(me, pieces, key, w, gq, gkv, back_q, back_kv):
    n, tok = key.shape[1:]
    k, own, slots, seq = back_q.shape[2], w.shape[2], n * CAP, n * tok
    wide = pieces[0].shape[1]
    return run(
        partial(qkv_back_kernel, n),
        "qkv_back",
        (EXPERTS + 2,),
        [rows_spec(m, k) for m in pieces]
        + [by_expert((n, tok), last_expert), by_expert((wide, own)),
           by_expert((slots, own), last_expert), by_expert((seq, own), from_expert),
           by_expert((slots, k), last_expert), by_expert((seq, k), from_expert)],
        sides(n, tok, wide),
        [((k, wide), BF16), ((slots, tok), BF16), ((slots, chunk_of(slots, wide)), BF16),
         ((seq, wide), F32), ((seq // 2, own), BF16), ((seq // 2, k), BF16)],
        (me, *pieces, key, w, gq, gkv, back_q, back_kv),
        2 * wide * own * (EXPERTS * slots + 2 * seq) * 1.5,
    )


def members(routes):
    names = jnp.arange(EXPERTS, dtype=jnp.int32)[None, :, None]
    member = (routes[:, :1] == names) | (routes[:, 1:] == names)
    tok = routes.shape[-1]
    before = (jnp.arange(tok)[:, None] < jnp.arange(tok)[None, :]).astype(BF16)
    rank = ein("met,tu->meu", member.astype(BF16), before).astype(jnp.int32)
    return jnp.where(member, rank, -1)


def own_shares(normed, router, routes):
    names = jnp.arange(EXPERTS, dtype=jnp.int32)[:, None]
    member = (routes[:1] == names) | (routes[1:] == names)
    logits = ein("td,de->et", normed, router)
    return jax.nn.softmax(jnp.where(member, logits, -jnp.inf), axis=0)


def route_back(share, grad_share, router):
    grad = share * (grad_share - jnp.sum(share * grad_share, axis=0, keepdims=True))
    return jnp.einsum("et,de->td", grad, router.astype(F32), precision=lax.Precision.HIGHEST)


def local(
    n,
    reps,
    layer_input_state,
    cotangent,
    norm_gain_vectors,
    attention_router_weight,
    feed_router_weight,
    attention_query_weight,
    key_value_weight,
    attention_output_weight,
    feed_expert_weight,
    attention_adapters,
    feed_adapter_width,
    feed_adapter_hidden,
    token_document,
    document_adapter,
    attention_expert_pairs,
    feed_expert_pairs,
):
    tok, wide = layer_input_state.shape
    own, slots = wide // n, n * CAP
    columns = attention_adapters.shape[3]
    me = lax.axis_index("shard")
    me_ref = me.reshape(1).astype(jnp.int32)
    segments = token_document[0]
    seq = segments.shape[0]
    docs = document_adapter[0]
    doc_count = docs.shape[0]
    k = doc_count * RANK

    def one_hot(which):
        at = which[:, None] * RANK + jnp.arange(RANK)[None, :]
        return (at.reshape(-1)[:, None] == jnp.arange(columns)[None, :]).astype(BF16)

    pick = one_hot(docs)
    attn_small = ein("kc,pmwc->pmkw", pick, attention_adapters).astype(BF16)
    width_small = ein("kc,pmwc->pmkw", pick, feed_adapter_width).astype(BF16)
    hidden_small = ein("kc,epcf->epkf", pick, feed_adapter_hidden).astype(BF16)
    b_in, a_out = attn_small[1, : EXPERTS + 2], attn_small[0, EXPERTS + 2 :]

    x = layer_input_state.astype(F32)
    gain_one = norm_gain_vectors[0].astype(F32)
    gain_two = norm_gain_vectors[1].astype(F32)
    normed_own = rms_norm(gain_one, x).astype(BF16)
    routes = jnp.concatenate([attention_expert_pairs.T, feed_expert_pairs.T])
    own_a = own_shares(normed_own, attention_router_weight, routes[:2])
    own_hi = own_a.astype(BF16)
    own_lo = (own_a - lax.reduce_precision(own_a, 8, 7)).astype(BF16)
    spare = jnp.stack([routes.astype(BF16).reshape(-1), own_hi.reshape(-1), own_lo.reshape(-1)])
    first = jnp.concatenate([pack_maps(attn_small[0, : EXPERTS + 2], n, spare), normed_own])
    def send(g):
        return [lax.ppermute(g, "rep", [(i, i ^ d) for i in range(reps)]) if d else g for d in range(reps)]

    weights = [attention_query_weight, key_value_weight]
    if n == 8:
        cut = (first.shape[0] // 2 + 15) // 16 * 16
        y0, x1 = swap(first[:cut], n, 4), swap(first[cut:], n, 2)
        y1, x0 = swap(first[cut:], n, 4), swap(first[:cut], n, 2)
        y0, x1, docs_sent, *weights = tie(y0, x1, docs, *weights)
        d0, d1 = swap(y0, n, 2), swap(x1, n, 4)
        chips = {0: first}
        for m, p in ((2, (x0, x1)), (4, (y0, y1)), (6, (d0, d1))):
            chips[m] = jnp.concatenate(p)
    else:
        chips, docs_sent = across(first, n), docs
    pieces = from_sibling(chips, n)
    w_in = reshard(weights, me, n)

    facts = jnp.stack([p[:3, (EXPERTS + 2) * own : (EXPERTS + 2) * own + EXPERTS * tok] for p in pieces])
    facts = facts[jnp.arange(n) ^ me].reshape(n, 3, EXPERTS, tok)
    routes = facts[:, 0].astype(jnp.int32)
    share_a = facts[:, 1].astype(F32) + facts[:, 2].astype(F32)

    second = jnp.concatenate([attn_small[1, EXPERTS + 2 :], width_small.reshape(-1, k, own)])
    groups = -(-second.shape[0] // n)

    begins = jnp.sum((segments[None, :] < jnp.arange(doc_count)[:, None]).astype(jnp.int32), axis=1)
    doc = segments.reshape(n, tok)
    place = jnp.arange(seq, dtype=jnp.int32).reshape(n, tok)
    doc_table = doc[None] == jnp.arange(doc_count, dtype=jnp.int32)[:, None, None]
    begin = jnp.sum(jnp.where(doc_table, begins[:, None, None], 0), axis=0)
    freq = jnp.exp(-jnp.arange(HD // 2, dtype=F32) * (2.0 * math.log(10000.0) / HD))
    angles = (place - begin).astype(F32)[..., None] * freq
    cos, sin = jnp.cos(angles), jnp.sin(angles)
    table = jnp.concatenate([cos, cos, -sin, sin], axis=-1)
    table_hi = table.astype(BF16)
    table_lo = (table - lax.reduce_precision(table, 8, 7)).astype(BF16)
    chosen_doc = jnp.arange(k, dtype=jnp.int32)[None, None, :] // RANK
    select_tok = (doc[:, :, None] == chosen_doc).astype(BF16)
    select_row = doc_table.astype(F32).reshape(1, doc_count, seq)

    slot_a, slot_f = members(routes[:, :2]), members(routes[:, 2:])
    routes_f_own = feed_expert_pairs.T
    key_a, key_f = slot_a.transpose(1, 0, 2), slot_f.transpose(1, 0, 2)

    def slot_select(slot):
        hot = slot[:, :, None, :] == jnp.arange(CAP, dtype=jnp.int32)[None, None, :, None]
        chose = hot[:, :, None] & doc_table.transpose(1, 0, 2)[:, None, :, None, :]
        select = jnp.any(chose, axis=-1).astype(F32)
        return select.transpose(1, 2, 0, 3).reshape(EXPERTS, doc_count, slots)

    select_a, select_f = slot_select(slot_a), slot_select(slot_f)

    def slot_row(share, slot):
        hot = slot[:, :, None, :] == jnp.arange(CAP, dtype=jnp.int32)[None, None, :, None]
        row = jnp.sum(jnp.where(hot, share[:, :, None, :], 0.0), axis=-1)
        return row.transpose(1, 0, 2).reshape(EXPERTS, 1, slots)

    picks_sent = send(docs_sent)
    second, w_in, hidden_small, *picks_sent = tie(pack_maps(second, n), w_in, hidden_small, *picks_sent)
    map_chips = across(second, n)

    share_ae = share_a.transpose(1, 0, 2)
    q, kv, rank_q, rank_kv, rows_a_own, normed_own_columns = qkv(
        me_ref, pieces, key_a, select_tok, table_hi, table_lo, w_in, b_in
    )
    q, cotangent_sent, *sent = tie(q, cotangent, *map_chips.values())
    cotangent_chips = across(cotangent_sent, n)
    maps = from_sibling(dict(zip(map_chips, sent)), n)
    mixed, lse = attend(slot_a, begin[:, None], q, kv[0], kv[1])
    near, far, live_o = project_out(
        "attend_out", me_ref, mixed, key_a, share_ae, select_tok, a_out, attention_output_weight, maps, groups, 0, 1
    )
    near, far, *sent = tie(near, far, *cotangent_chips.values())
    attn_total, attn_low = halve(near, far, n)
    grads_out_all = from_sibling(dict(zip(cotangent_chips, sent)), n)
    *attn_low, key_late = tie(*attn_low, key_f)

    w_feed = jnp.swapaxes(feed_expert_weight, 2, 3)
    grad_inner, back_down, rows_g_own = feed_back_down(
        me_ref, grads_out_all, maps, groups, EXPERTS + 2, 3, key_late, select_tok, w_feed, hidden_small
    )
    attn_total, grad_inner = tie(attn_total, grad_inner)
    attended = x + collect(attn_total, attn_low, n)
    normed_two_own = rms_norm(gain_two, attended).astype(BF16)
    chips = across(normed_two_own, n)
    scaled_a = select_a * slot_row(share_a, slot_a)
    select_a, select_f, scaled_a, *sent = tie(select_a, select_f, scaled_a, *chips.values())
    normed_two = from_sibling(dict(zip(chips, sent)), n)
    own_f = own_shares(normed_two_own, feed_router_weight, routes_f_own)
    share_f = gather_small(own_f, me, n)
    share_fe = share_f.transpose(1, 0, 2)
    near, far, inner, live_f, dshare_f, hidden_grad, rows_f_own = feed(
        me_ref, normed_two, maps, groups, EXPERTS, 3, key_f, share_fe, select_tok, w_feed, hidden_small,
        grad_inner, back_down,
    )
    near, far = near.reshape(n // 2, tok, wide), far.reshape(n // 2, tok, wide)
    two_total, two_low = halve(near, far, n)
    dshare_f = dshare_f[:1]
    dshare_f = dshare_f + swap(dshare_f, n, 1)
    *two_low, inner, dshare_f, live_f, live_o = tie(*two_low, inner, dshare_f, live_f, live_o)
    live_f = jnp.concatenate([live_f, live_o])
    live_f = live_f + swap(live_f, n, 1)
    near, far, unused = project_out(
        "feed_out", me_ref, inner, key_f, share_fe, select_tok, hidden_small, w_feed, maps, groups, EXPERTS + 2, 3, 2
    )
    two_got = [swap(part, n, 2 * i + 2) for i, part in enumerate(two_low)]
    near, far, *two_got = tie(near, far, *two_got)
    grad_two_own = added([two_total] + two_got)

    def own_tokens(slot, dshare):
        mine = lax.dynamic_slice_in_dim(dshare.reshape(EXPERTS, n, CAP), me, 1, 1)[:, 0]
        hot = lax.dynamic_slice_in_dim(slot, me, 1, 0)[0][:, None, :] == jnp.arange(CAP)[None, :, None]
        return jnp.sum(jnp.where(hot, mine[:, :, None], 0.0), axis=1)

    d = 2
    while d < n:
        dshare_f, d = dshare_f + swap(dshare_f, n, d), 2 * d
    grad_two_own = grad_two_own + route_back(own_f, own_tokens(slot_f, dshare_f), feed_router_weight)
    grad_attended = cotangent.astype(F32) + rms_back(attended, gain_two, grad_two_own)

    grad_sent, near, far = tie(grad_attended.astype(BF16), near, far)
    out_total, out_low = halve(near, far, n)
    chips = across(grad_sent, n)
    out_total, *sent = tie(out_total, *out_low, *chips.values())
    out_low, sent = sent[: n // 2 - 1], sent[n // 2 - 1 :]
    grads_two = from_sibling(dict(zip(chips, sent)), n)
    mixed_late, live_f = tie(mixed, live_f)
    live_f_sent = list(across(live_f, n).values())
    grad_mixed, a_out_grad, dshare_a, rows_ga_own = mixed_back(
        me_ref, grads_two, maps, groups, key_a, share_ae, select_tok, attention_output_weight, a_out, mixed_late
    )
    grad_mixed, *sent = tie(grad_mixed, *live_f_sent, *out_low)
    live_f_sent, out_low = sent[: n // 2], sent[n // 2 :]
    gq, gk, gv = attend_back(slot_a, begin[:, None], q, grad_mixed, mixed, lse, kv[0], kv[1])
    out_got = [swap(part, n, 2 * i + 2) for i, part in enumerate(out_low)]
    gq, *sent = tie(gq, *live_f_sent, *out_got)
    live_f_sent, out_got = sent[: n // 2], sent[n // 2 :]
    live_f = added(live_f_sent)
    live_f, live_o = live_f[: 3 * RANK], live_f[3 * RANK :]

    def spread(live, select):
        both = live.astype(F32)[:, None] * select[:, :, None, :]
        return both.reshape(live.shape[0], k, live.shape[2]).astype(BF16)

    def of_slots(live):
        return live.reshape(RANK, EXPERTS, slots).transpose(1, 0, 2)

    def grads(rank, rows):
        return ein("eks,esw->ekw", rank, rows).astype(BF16)

    def by_stream(sent):
        out = jnp.zeros((reps,) + sent[0].shape, sent[0].dtype)
        for d, got in enumerate(sent):
            out = lax.dynamic_update_slice_in_dim(out, got[None], lax.axis_index("rep") ^ d, 0)
        return out

    scaled_f = select_f * slot_row(share_f, slot_f)
    width_grad = jnp.stack(
        [
            grads(spread(of_slots(live_f[:RANK]), select_f), rows_f_own),
            grads(spread(of_slots(live_f[RANK : 2 * RANK]), select_f), rows_f_own),
            grads(spread(of_slots(live_f[2 * RANK :]), scaled_f), rows_g_own),
        ],
        axis=1,
    )
    b_out_grad = grads(spread(of_slots(live_o), scaled_a), rows_ga_own)
    early_grad = jnp.concatenate([a_out_grad, b_out_grad])
    layer_out = attended + added([out_total] + out_got)
    gq, gkv, back_q, back_kv, live_in, b_in_grad = qkv_rank(
        key_a, select_tok, table_hi, table_lo, b_in, gq, gk, gv, rank_q, rank_kv
    )
    dshare_a = dshare_a[0].astype(BF16).reshape(RANK, -1)
    spare = -dshare_a.shape[1] % 128
    live_in = jnp.concatenate([live_in, jnp.pad(dshare_a, ((0, 0), (0, spare)))], axis=1)
    live_in = live_in + swap(live_in, n, 1)
    gq, live_in, b_in_grad, early_grad, width_grad = tie(gq, live_in, b_in_grad, early_grad, width_grad)
    hidden_all, width_all = lax.all_gather(hidden_grad, "rep"), lax.all_gather(width_grad, "rep")
    early_sent = send(early_grad)
    live_sent, late_b_sent = list(across(live_in, n).values()), send(b_in_grad)
    near, far = qkv_back(me_ref, pieces, key_a, w_in, gq, gkv, back_q, back_kv)
    near, far, *sent = tie(near, far, *live_sent, *early_sent)
    live_sent, early_sent = sent[: n // 2], sent[n // 2 :]
    in_total, in_low = (quarter if n == 8 else halve)(near, far, n)
    *in_low, first_sent = tie(*in_low, live_sent[0])
    in_got = [swap(part, n, 2 * i + 2) for i, part in enumerate(in_low)]
    live_in = added([first_sent] + live_sent[1:])
    width = EXPERTS * slots + 2 * seq
    dshare_a = live_in[:, width : width + EXPERTS * slots // RANK]
    live_kv = live_in[:, EXPERTS * slots : width].reshape(RANK, 2, seq).transpose(1, 0, 2)
    a_in_grad = jnp.concatenate(
        [
            grads(spread(of_slots(live_in[:, : EXPERTS * slots]), select_a), rows_a_own),
            ein("pks,sw->pkw", spread(live_kv, select_row), normed_own_columns).astype(BF16),
        ]
    )
    a_in_grad, hidden_all, *sent = tie(a_in_grad, hidden_all, *late_b_sent, *in_got)
    late_b_sent, in_got = sent[:reps], sent[reps:]
    late_a_sent = send(a_in_grad)
    grad_normed = collect_quarters(in_total, in_got, n) if n == 8 else added([in_total] + in_got)
    grad_normed = grad_normed + route_back(own_a, own_tokens(slot_a, dshare_a), attention_router_weight)
    grad_normed, width_all = tie(grad_normed, width_all)
    grad_in = grad_attended + rms_back(x, gain_one, grad_normed)

    picks = jax.vmap(one_hot)(jnp.stack(picks_sent)[jnp.arange(reps) ^ lax.axis_index("rep")])
    early = by_stream(early_sent)
    hidden_out = ein("rpekf,rkc->pecf", hidden_all, picks)
    width_out = ein("rpmkw,rkc->pmwc", width_all, picks)
    late_b, late_a = by_stream(late_b_sent), by_stream(late_a_sent)
    attn = jnp.concatenate([late_a, early[:, :EXPERTS], late_b, early[:, EXPERTS:]], axis=1)
    attn = attn.reshape(reps, 2, -1, k, own)
    attn_out = ein("rpmkw,rkc->pmwc", attn, picks)
    return (layer_out, grad_in, attn_out, width_out, hidden_out)


def solution(mesh):
    in_specs = (
        P(("rep", "shard"), None),
        P(("rep", "shard"), None),
        P(),
        P(),
        P(),
        P(None, "shard", None),
        P(None, "shard", None),
        P(None, "shard", None),
        P(None, None, None, "shard"),
        P(None, None, "shard", None),
        P(None, None, "shard", None),
        P(None, None, None, "shard"),
        P("rep", None),
        P("rep", None),
        P(("rep", "shard"), None),
        P(("rep", "shard"), None),
    )
    out_specs = (
        P(("rep", "shard"), None),
        P(("rep", "shard"), None),
        P(None, None, "shard", None),
        P(None, None, "shard", None),
        P(None, None, None, "shard"),
    )
    body = partial(local, mesh.shape["shard"], mesh.shape["rep"])
    return jax.shard_map(body, mesh=mesh, in_specs=in_specs, out_specs=out_specs, check_vma=False)
```

```python
from functools import partial
import math

import jax
import jax.numpy as jnp
from jax import lax
from jax.experimental import pallas as pl
from jax.experimental.pallas import tpu as pltpu
from jax.sharding import PartitionSpec as P

HD = 128
RANK = 16
CAP = 80
EXPERTS = 4
CHUNK = 256
EPS = 1e-05
NEG = -1e30
F32 = jnp.float32
BF16 = jnp.bfloat16


def ein(spec, a, b):
    return jnp.einsum(spec, a, b, preferred_element_type=F32)


def rms_norm(gain, values):
    return values * lax.rsqrt(jnp.mean(values * values, axis=-1, keepdims=True) + EPS) * gain


def rms_back(values, gain, grad):
    unused, backward_function = jax.vjp(partial(rms_norm, gain), values)
    return backward_function(grad)[0]


NT = (((1,), (1,)), ((), ()))
TN = (((0,), (0,)), ((), ()))


def dot_nt(a, b):
    return lax.dot_general(a, b, NT, preferred_element_type=F32)


def dot_tn(a, b):
    return lax.dot_general(a, b, TN, preferred_element_type=F32)


def dot_nn(a, b):
    return jnp.dot(a, b, preferred_element_type=F32)


def swap(x, n, d):
    return lax.ppermute(x, "shard", [(i, i ^ d) for i in range(n)])


def tie(*values):
    return lax.optimization_barrier(values)


def across(x, n):
    return {d: swap(x, n, d) if d else x for d in range(0, n, 2)}


def from_sibling(pieces, n):
    other = {m ^ 1: swap(p, n, 1) for m, p in pieces.items()}
    return [p for unused, p in sorted({**pieces, **other}.items())]


def gather_small(x, me, n):
    mine = jnp.stack(list(across(x, n).values()))
    mask = jnp.arange(n) ^ me
    return jnp.concatenate([mine, swap(mine, n, 1)])[mask // 2 + mask % 2 * (n // 2)]


def halve(near, far, n):
    got = swap(far, n, 1)
    sums = [near[i].astype(F32) + got[i].astype(F32) for i in range(n // 2)]
    return sums[0], [one.astype(BF16) for one in sums[1:]]


def added(parts):
    return sum([part.astype(F32) for part in parts[1:]], parts[0].astype(F32))


def quarter(near, far, n):
    got = swap(far, n, 1)
    cut = near.shape[1] // 2

    def total(i, at):
        return near[i, at].astype(F32) + got[i, at].astype(F32)

    top, low = slice(0, cut), slice(cut, None)
    sent = [jnp.stack([total(i, at).astype(BF16) for i in pair]) for at, pair in ((top, (1, 3)), (low, (2, 3)))]
    return [total(0, top), total(2, top), total(0, low), total(1, low)], sent


def collect_quarters(kept, got, n):
    a0, a2, b0, b1 = kept
    ra, rb = got[0].astype(F32), got[1].astype(F32)
    a2, b1 = (a2 + ra[1]).astype(BF16), (b1 + rb[1]).astype(BF16)
    a0 = a0 + ra[0] + swap(a2, n, 4).astype(F32)
    b0 = b0 + rb[0] + swap(b1, n, 2).astype(F32)
    return jnp.concatenate([a0, b0])


def collect(total, low, n):
    for i, part in enumerate(low):
        total = total + swap(part, n, 2 * i + 2).astype(F32)
    return total


def reshard(ws, me, n):
    rows, width = ws[0].shape[1], ws[0].shape[2] // n
    count = sum(w.shape[0] for w in ws)
    out = jnp.zeros((count, n * rows, width), ws[0].dtype)
    for m in sorted(range(n), key=lambda m: -m):
        piece = jnp.concatenate([lax.dynamic_slice_in_dim(w, (me ^ m) * width, width, 2) for w in ws])
        piece = swap(piece, n, m) if m else piece
        out = lax.dynamic_update_slice_in_dim(out, piece, (me ^ m) * rows, 1)
    return out


def pack_maps(maps, n, spare=None):
    count, k, own = maps.shape
    groups = -(-count // n)
    fill = groups * n - count
    flat = [maps[i] for i in range(count)]
    if fill:
        rest = jnp.zeros((k, fill * own), maps.dtype)
        if spare is not None:
            rest = rest.at[: spare.shape[0], : spare.shape[1]].set(spare)
        flat.append(rest)
    rows = [jnp.concatenate(flat[g * n : (g + 1) * n], axis=1) for g in range(groups)]
    return jnp.concatenate(rows) if groups > 1 else rows[0]


def fill_hot(key, hot):
    n, tok = key.shape
    slot = lax.broadcasted_iota(jnp.int32, (CAP, tok), 0)
    for b in range(n):
        one = jnp.where(slot == key[b : b + 1, :], 1.0, 0.0)
        hot[b * CAP : (b + 1) * CAP, :] = one.astype(BF16)


def block_of(b, size):
    return pl.ds(pl.multiple_of(b * size, 16), size)


def fill_rows(me, hot, xs, base, rows):
    tok = hot.shape[1]
    for m, x in enumerate(xs):
        here = block_of(me[0] ^ m, CAP)
        rows[here, :] = dot_nn(hot[here, :], x[pl.ds(base, tok), :]).astype(BF16)


def fill_map(me, xs, index, out):
    n, k = len(xs), out.shape[0]
    own = out.shape[1] // n
    group, column = index // n, index % n
    for m, x in enumerate(xs):
        part = x[block_of(group, k), pl.ds(pl.multiple_of(column * own, own), own)]
        out[:, pl.ds(pl.multiple_of((me[0] ^ m) * own, own), own)] = part


def fill_select(hot, select_tok, sel):
    for b in range(select_tok.shape[0]):
        here = pl.ds(b * CAP, CAP)
        sel[here, :] = dot_nn(hot[here, :], select_tok[b])


def fill_share(hot, share, col):
    for b in range(share.shape[0]):
        here = pl.ds(b * CAP, CAP)
        one = jnp.sum(hot[here, :].astype(F32) * share[b : b + 1, :], axis=1, keepdims=True)
        col[here, :] = jnp.broadcast_to(one, (CAP, col.shape[1]))


def scatter_add(me, hot, y, acc, at):
    tok = hot.shape[1]
    n = acc.shape[0] // tok
    for b in range(n):
        mask = me[0] ^ b
        there = block_of(mask // 2 + (mask % 2) * (n // 2), tok)
        acc[there, at] += dot_tn(hot[pl.ds(b * CAP, CAP), :], y[pl.ds(b * CAP, CAP), :])


def copy_out(acc, rows, near, far, sem):
    half = acc.shape[0] // 2
    for side, ref in enumerate((near, far)):
        rows[:half, :] = acc[side * half : (side + 1) * half, :].astype(BF16)
        copy = pltpu.make_async_copy(rows.at[pl.ds(0, half)], ref, sem)
        copy.start()
        copy.wait()


def write_out(acc, near, far):
    half = acc.shape[0] // 2
    near[...] = acc[:half, :].astype(BF16).reshape(near.shape)
    far[...] = acc[half:, :].astype(BF16).reshape(far.shape)


def live_rows(staged, first, k):
    total = staged[first : first + RANK]
    for d in range(1, k // RANK):
        total = total + staged[first + d * RANK : first + (d + 1) * RANK]
    return total


def lanes(e, size):
    return pl.ds(pl.multiple_of(e * size, 128), size)


def turn(v, cos, sin):
    return v * cos + pltpu.roll(v, HD // 2, 1) * sin


def turn_heads(v, table, sign):
    cos, sin = table[:, :HD], table[:, HD:]
    heads = [turn(v[:, h : h + HD], cos, sign * sin) for h in range(0, v.shape[1], HD)]
    return heads[0] if len(heads) == 1 else jnp.concatenate(heads, axis=1)


def qkv_kernel(n, *refs):
    me, xs, refs = refs[0], refs[1 : 1 + n], refs[1 + n :]
    key, select_tok, hi, lo, w, b_in, q, kv, rank_q, rank_kv, rows_own, tok_own, a_in, wide_w, *refs = refs
    hot, rows, sel, table = refs
    i = pl.program_id(0)
    tok, k, slots = hi.shape[1], b_in.shape[0], hot.shape[0]
    own = w.shape[1]
    mine = pl.ds(pl.multiple_of(me[0] * own, own), own)

    @pl.when(i == 0)
    def start():
        a_in[...] = jnp.zeros(a_in.shape, BF16)

    fill_map(me, xs, i, a_in.at[:k])
    wide_w[:, :own] = w[...]
    wide_w[:, own:] = a_in[...].T

    @pl.when(i < EXPERTS)
    def query():
        fill_hot(key, hot)
        fill_rows(me, hot, xs, k, rows)
        fill_select(hot, select_tok, sel)
        for b in range(n):
            here = pl.ds(b * CAP, CAP)
            table[here, :] = dot_nn(hot[here, :], hi[b]) + dot_nn(hot[here, :], lo[b])
        both = dot_nn(rows[:slots, :], wide_w[...])
        rank = (both[:, own : own + k] * sel[:slots, :]).astype(BF16)
        rank_q[...] = rank
        pre = both[:, :own] + dot_nn(rank, b_in[...])
        q[...] = turn_heads(pre, table[:slots, :], 1.0).astype(BF16)
        rows_own[...] = rows[:slots, mine]

    @pl.when(i >= EXPERTS)
    def key_value():
        group = n // 2
        some = pl.ds(0, group * tok)
        for half in range(2):
            for j in range(group):
                m = half * group + j
                b = me[0] ^ m
                here = pl.ds(j * tok, tok)
                rows[here, :] = xs[m][pl.ds(k, tok), :]
                sel[here, :] = select_tok[b].astype(F32)
                table[here, :] = hi[b].astype(F32) + lo[b].astype(F32)
            both = dot_nn(rows[some, :], wide_w[...])
            rank = (both[:, own : own + k] * sel[some, :]).astype(BF16)
            pre = both[:, :own] + dot_nn(rank, b_in[...])
            turned = turn_heads(pre, table[some, :], 1.0)
            done = jnp.where(i == EXPERTS, turned, pre).astype(BF16)
            for j in range(group):
                there = block_of(me[0] ^ (half * group + j), tok)
                here = slice(j * tok, (j + 1) * tok)
                rank_kv[there, :] = rank[here]
                kv[there, :] = done[here]
                tok_own[there, :] = rows[here, mine]


def limits(key, begin, b):
    tok = begin.shape[1]
    slot = lax.broadcasted_iota(jnp.int32, (CAP, tok), 0)
    token = b * tok + lax.broadcasted_iota(jnp.int32, (CAP, tok), 1)
    first, last = [], []
    for e in range(EXPERTS):
        chosen = slot == key[e : e + 1, :]
        first.append(jnp.sum(jnp.where(chosen, begin[...], 0), axis=1, keepdims=True))
        last.append(jnp.sum(jnp.where(chosen, token, 0), axis=1, keepdims=True))
    return jnp.concatenate(first), jnp.concatenate(last)


def attend_kernel(key, begin, q, k, v, mixed, lse, scores, mx, tot, acc):
    b = pl.program_id(0)
    tok, own = begin.shape[1], q.shape[2]
    rows = q.shape[0] * q.shape[1]
    first, last = limits(key, begin, b)
    query = q[...].reshape(rows, own)
    heads = [slice(h, h + HD) for h in range(0, own, HD)]
    count = (b * tok + tok + CHUNK - 1) // CHUNK
    mx[...] = jnp.full(mx.shape, NEG, F32)

    def score(j, carry):
        start = pl.multiple_of(j * CHUNK, CHUNK)
        here = pl.ds(start, CHUNK)
        at = start + lax.broadcasted_iota(jnp.int32, (rows, CHUNK), 1)
        seen = (at >= first) & (at <= last)
        raw = [dot_nt(query[:, h], k[here, h]) for h in heads]
        for i, h in enumerate(heads):
            s = jnp.where(seen, raw[i] * HD ** (-0.5), NEG)
            scores[i, :, here] = s
            mx[:, h] = jnp.maximum(mx[:, h], jnp.maximum(s[:, :HD], s[:, HD:]))
        return carry

    lax.fori_loop(0, count, score, 0)
    top = [jnp.max(mx[:, h], axis=1, keepdims=True) for h in heads]
    tot[...] = jnp.zeros(tot.shape, F32)
    acc[...] = jnp.zeros(acc.shape, F32)

    def mix(j, carry):
        here = pl.ds(pl.multiple_of(j * CHUNK, CHUNK), CHUNK)
        for i, h in enumerate(heads):
            p = jnp.exp(scores[i, :, here] - top[i])
            tot[:, h] += p[:, :HD] + p[:, HD:]
            acc[:, h] += dot_nn(p.astype(BF16), v[here, h])
        return carry

    lax.fori_loop(0, count, mix, 0)
    for i, h in enumerate(heads):
        total = jnp.sum(tot[:, h], axis=1, keepdims=True)
        mixed[:, :, h] = (acc[:, h] / total).astype(BF16).reshape(EXPERTS, CAP, HD)
        spread = jnp.broadcast_to(top[i] + jnp.log(total), (rows, HD))
        lse[:, :, h] = spread.reshape(EXPERTS, CAP, HD)


def attend_back_kernel(key, begin, q, g, mixed, lse, k, v, gq, gk, gv, dq):
    b = pl.program_id(0)
    tok, own = begin.shape[1], q.shape[2]
    rows = q.shape[0] * q.shape[1]
    scale = HD ** (-0.5)

    @pl.when(b == 0)
    def start():
        gk[...] = jnp.zeros(gk.shape, F32)
        gv[...] = jnp.zeros(gv.shape, F32)

    first, last = limits(key, begin, b)

    def flat(r):
        return r[...].reshape(rows, own)

    query, grad = flat(q), flat(g)
    heads = [slice(h, h + HD) for h in range(0, own, HD)]
    product = flat(mixed).astype(F32) * grad.astype(F32)
    delta = [jnp.sum(product[:, h], axis=1, keepdims=True) for h in heads]
    logs = flat(lse)
    log_total = [logs[:, h.start : h.start + 1] for h in heads]
    count = (b * tok + tok + CHUNK - 1) // CHUNK
    dq[...] = jnp.zeros(dq.shape, F32)

    def step(j, carry):
        begin_at = pl.multiple_of(j * CHUNK, CHUNK)
        here = pl.ds(begin_at, CHUNK)
        at = begin_at + lax.broadcasted_iota(jnp.int32, (rows, CHUNK), 1)
        seen = (at >= first) & (at <= last)
        raw = [dot_nt(query[:, h], k[here, h]) for h in heads]
        dps = [dot_nt(grad[:, h], v[here, h]) for h in heads]
        for i, h in enumerate(heads):
            p = jnp.where(seen, jnp.exp(raw[i] * scale - log_total[i]), 0.0)
            ds = (p * (dps[i] - delta[i])).astype(BF16)
            dq[:, h] += dot_nn(ds, k[here, h])
            gk[here, h] += dot_tn(ds, query[:, h]) * scale
            gv[here, h] += dot_tn(p.astype(BF16), grad[:, h])
        return carry

    lax.fori_loop(0, count, step, 0)
    gq[...] = (dq[...] * scale).reshape(gq.shape)


def out_kernel(n, first, stride, *refs):
    me, xs, refs = refs[0], refs[1 : 1 + n], refs[1 + n :]
    x, key, share, select_tok, down, w, near, far, live, maps, hot, sel, col, part, stage, acc = refs
    e = pl.program_id(0)
    k, slots = down.shape[0], x.shape[0]

    @pl.when(e == 0)
    def start():
        acc[...] = jnp.zeros(acc.shape, F32)
        stage[...] = jnp.zeros(stage.shape, F32)

    fill_map(me, xs, first + stride * e, maps)
    fill_hot(key, hot)
    fill_select(hot, select_tok, sel)
    fill_share(hot, share, col)
    rank = dot_nt(x[...], down[...]) * sel[...]
    stage[:, :k] = rank
    live[:, lanes(e, slots)] = live_rows(stage[...].T, 0, k).astype(BF16)
    rank = rank.astype(BF16)
    width = part.shape[1]
    for c in range(0, w.shape[1], width):
        at = pl.ds(c, width)
        y = dot_nn(x[...], w[:, at]) + dot_nn(rank, maps[:, at])
        part[...] = (y * col[:, :1]).astype(BF16)
        scatter_add(me, hot, part, acc, at)

    @pl.when(e == EXPERTS - 1)
    def finish():
        write_out(acc, near, far)


def back_kernel(n, first, stride, *refs):
    me, xs, ms, refs = refs[0], refs[1 : 1 + n], refs[1 + n : 1 + 2 * n], refs[1 + 2 * n :]
    key, select_tok, w, small, h, rank, rows_own, maps, hot, rows, sel = refs
    deep = w.shape[0]
    maps[:deep, :] = w[...]
    fill_map(me, ms, first + stride * pl.program_id(0), maps.at[deep:])
    fill_hot(key, hot)
    fill_rows(me, hot, xs, 0, rows)
    fill_select(hot, select_tok, sel)
    both = dot_nt(rows[...], maps[...])
    low = (both[:, deep:] * sel[...]).astype(BF16)
    rank[...] = low
    h[...] = both[:, :deep] + dot_nn(low, small[...])
    rows_own[...] = rows[:, lanes(me[0], rows_own.shape[1])]


def mixed_back_kernel(n, *refs):
    me, xs, ms, refs = refs[0], refs[1 : 1 + n], refs[1 + n : 1 + 2 * n], refs[1 + 2 * n :]
    key, share, select_tok, w, small, mixed, g, a_grad, dshare, rows_own, maps, *refs = refs
    hot, rows, sel, col, stage = refs
    e = pl.program_id(0)
    k, own, slots = small.shape[0], mixed.shape[1], mixed.shape[0]
    maps[:own, :] = w[...]
    fill_map(me, ms, e, maps.at[own:])

    @pl.when(e == 0)
    def start():
        stage[...] = jnp.zeros(stage.shape, F32)

    fill_hot(key, hot)
    fill_rows(me, hot, xs, 0, rows)
    fill_select(hot, select_tok, sel)
    fill_share(hot, share, col)
    both = dot_nt(rows[...], maps[...])
    low = (both[:, own:] * sel[...]).astype(BF16)
    h = both[:, :own] + dot_nn(low, small[...])
    stage[:, :1] = jnp.sum(mixed[...].astype(F32) * h, axis=1, keepdims=True)
    dshare[:, lanes(e, slots)] = stage[...].T[:8]
    g[...] = (h * col[:, :1]).astype(BF16)
    scaled = (low.astype(F32) * col[:, :k]).astype(BF16)
    a_grad[...] = dot_tn(scaled, mixed[...]).astype(BF16)
    rows_own[...] = rows[:, lanes(me[0], own)]


def feed_kernel(n, first, stride, *refs):
    me, xs, ms, refs = refs[0], refs[1 : 1 + n], refs[1 + n : 1 + 2 * n], refs[1 + 2 * n :]
    key, share, select_tok, wg, wu, hid, h, back_down, *refs = refs
    near, far, inner, live, dshare, h_grad, rows_own, *refs = refs
    hot, rows, sel, col, stage, both, gate, up, gg, gu, part, acc, sem = refs
    e = pl.program_id(0)
    k, own, slots = hid.shape[1], rows_own.shape[1], rows.shape[0]

    @pl.when(e == 0)
    def start():
        acc[...] = jnp.zeros(acc.shape, F32)
        stage[...] = jnp.zeros(stage.shape, F32)

    fill_hot(key, hot)
    fill_rows(me, hot, xs, 0, rows)
    fill_select(hot, select_tok, sel)
    fill_share(hot, share, col)
    fill_map(me, ms, first + stride * e, both.at[:k])
    fill_map(me, ms, first + stride * e + 1, both.at[k:])
    ranks = dot_nt(rows[...], both[...])
    rank_gate = (ranks[:, :k] * sel[...]).astype(BF16)
    rank_up = (ranks[:, k:] * sel[...]).astype(BF16)
    gate[...] = dot_nt(rows[...], wg[...]) + dot_nn(rank_gate, hid[0])
    up[...] = dot_nt(rows[...], wu[...]) + dot_nn(rank_up, hid[1])

    def point(b, carry):
        r = block_of(b, CAP)
        a, u, hh, s = gate[r, :], up[r, :], h[r, :], col[r, :1]
        sig = jax.nn.sigmoid(a)
        act = a * sig
        value = act * u
        inner[r, :] = value.astype(BF16)
        stage[r, 2 * k : 2 * k + 1] = jnp.sum(value * hh, axis=1, keepdims=True)
        scaled = hh * s
        gg[r, :] = (scaled * u * sig * (1.0 + a * (1.0 - sig))).astype(BF16)
        gu[r, :] = (scaled * act).astype(BF16)
        return carry

    lax.fori_loop(0, slots // CAP, point, 0)
    stage[:, :k] = dot_nt(gg[...], hid[0]) * sel[...]
    stage[:, k : 2 * k] = dot_nt(gu[...], hid[1]) * sel[...]
    stage[:, 128 : 128 + k] = dot_nt(inner[...], hid[2]) * sel[...]
    staged = stage[...].T
    live[:RANK, lanes(e, slots)] = live_rows(staged, 0, k).astype(BF16)
    live[RANK : 2 * RANK, lanes(e, slots)] = live_rows(staged, k, k).astype(BF16)
    live[2 * RANK :, lanes(e, slots)] = live_rows(staged, 128, k).astype(BF16)
    dshare[:, lanes(e, slots)] = staged[2 * k : 2 * k + 8]
    h_grad[0] = dot_tn(rank_gate, gg[...]).astype(BF16)
    h_grad[1] = dot_tn(rank_up, gu[...]).astype(BF16)
    scaled = (back_down[...].astype(F32) * col[:, :k]).astype(BF16)
    h_grad[2] = dot_tn(scaled, inner[...]).astype(BF16)
    rows_own[...] = rows[:, lanes(me[0], own)]
    back = stage[:, : 2 * k].astype(BF16)
    width = part.shape[1]
    for c in range(0, wg.shape[1], width):
        at = pl.ds(c, width)
        y = dot_nn(gg[...], wg[:, at]) + dot_nn(gu[...], wu[:, at]) + dot_nn(back, both[:, at])
        part[...] = y.astype(BF16)
        scatter_add(me, hot, part, acc, at)

    @pl.when(e == EXPERTS - 1)
    def finish():
        copy_out(acc, rows, near, far, sem)


def qkv_rank_kernel(
    key, select_tok, hi, lo, b_in, gq, gk, gv, rank_q, rank_kv,
    out_q, out_kv, back_q, back_kv, live, b_grad,
    hot, sel, table, stage,
):
    i = pl.program_id(0)
    n, tok, k = hi.shape[0], hi.shape[1], b_in.shape[0]
    slots, seq = gq.shape[0], gk.shape[0]

    @pl.when(i == 0)
    def start():
        stage[...] = jnp.zeros(stage.shape, F32)

    @pl.when(i < EXPERTS)
    def query():
        fill_hot(key, hot)
        fill_select(hot, select_tok, sel)
        for b in range(n):
            here = pl.ds(b * CAP, CAP)
            table[here, :] = dot_nn(hot[here, :], hi[b]) + dot_nn(hot[here, :], lo[b])
        g = turn_heads(gq[...], table[...], -1.0).astype(BF16)
        out_q[...] = g
        rank = dot_nt(g, b_in[...]) * sel[...]
        stage[:slots, :k] = rank
        back_q[...] = rank.astype(BF16)
        live[:, lanes(i, slots)] = live_rows(stage[:slots, :].T, 0, k).astype(BF16)
        b_grad[...] = dot_tn(rank_q[...], g).astype(BF16)

    @pl.when(i >= EXPERTS)
    def key_value():
        for b in range(n):
            here = pl.ds(b * tok, tok)
            both = hi[b].astype(F32) + lo[b].astype(F32)
            turned = turn_heads(gk[here, :], both, -1.0)
            out_kv[here, :] = jnp.where(i == EXPERTS, turned, gv[here, :]).astype(BF16)
            stage[here, k : 2 * k] = select_tok[b].astype(F32)
        g = out_kv[...]
        rank = dot_nt(g, b_in[...]) * stage[:seq, k : 2 * k]
        stage[:seq, :k] = rank
        back_kv[...] = rank.astype(BF16)
        b_grad[...] = dot_tn(rank_kv[...], g).astype(BF16)
        begin = EXPERTS * slots + (i - EXPERTS) * seq
        there = pl.ds(pl.multiple_of(begin, 128), seq)
        live[:, there] = live_rows(stage[:seq, :].T, 0, k).astype(BF16)


def qkv_back_kernel(n, *refs):
    me, xs, refs = refs[0], refs[1 : 1 + n], refs[1 + n :]
    key, w, gq, gkv, back_q, back_kv, near, far, maps, hot, part, acc, some_g, some_rank = refs
    i = pl.program_id(0)
    tok = hot.shape[1]
    wide = maps.shape[1]
    width = part.shape[1]
    fill_map(me, xs, i, maps)

    @pl.when(i == 0)
    def start():
        acc[...] = jnp.zeros(acc.shape, F32)

    @pl.when(i < EXPERTS)
    def query():
        fill_hot(key, hot)
        for c in range(0, wide, width):
            at = pl.ds(c, width)
            y = dot_nt(gq[...], w[at, :]) + dot_nn(back_q[...], maps[:, at])
            part[...] = y.astype(BF16)
            scatter_add(me, hot, part, acc, at)

    @pl.when(i >= EXPERTS)
    def key_value():
        group = n // 2
        size = group * tok
        for half in range(2):
            there = pl.ds(half * size, size)
            for j in range(group):
                block = block_of(me[0] ^ (2 * j + half), tok)
                some_g[j * tok : (j + 1) * tok, :] = gkv[block, :]
                some_rank[j * tok : (j + 1) * tok, :] = back_kv[block, :]
            for c in range(0, wide, width):
                at = pl.ds(c, width)
                acc[there, at] += dot_nt(some_g[...], w[at, :]) + dot_nn(some_rank[...], maps[:, at])

    @pl.when(i == EXPERTS + 1)
    def finish():
        write_out(acc, near, far)


def chunk_of(slots, wide):
    width = wide // 2
    while slots * width > 640 * 1024:
        width //= 2
    return width


def whole(shape):
    zeros = (0,) * len(shape)
    return pl.BlockSpec(shape, lambda *at: zeros, pipeline_mode=pl.Buffered(1))


def by_expert(shape, at=lambda i: i):
    rest = (0,) * len(shape)
    return pl.BlockSpec((None,) + shape, lambda i, *unused: (at(i),) + rest)


def shaped(shape, dtype):
    return jax.ShapeDtypeStruct(shape, dtype)


def run(kernel, name, steps, ins, outs, scratch, args, flops, scalars=1):
    call = pl.pallas_call(
        kernel,
        grid_spec=pltpu.PrefetchScalarGridSpec(
            num_scalar_prefetch=scalars,
            grid=steps,
            in_specs=ins,
            out_specs=[o[0] for o in outs],
            scratch_shapes=[pltpu.VMEM(*one) if isinstance(one, tuple) else one for one in scratch],
        ),
        out_shape=[shaped(o[1], o[2]) for o in outs],
        compiler_params=pltpu.CompilerParams(vmem_limit_bytes=62 << 20),
        cost_estimate=pl.CostEstimate(
            flops=int(flops), bytes_accessed=32 << 20, transcendentals=1 << 20
        ),
        name=name,
    )
    return call(*args)


def last_expert(i):
    return jnp.minimum(i, EXPERTS - 1)


def from_expert(i):
    return jnp.maximum(i - EXPERTS, 0)


def rows_spec(x, rows=None):
    return whole((x.shape[0] if rows is None else rows, x.shape[1]))


def sides(n, tok, wide):
    shape = (n // 2, tok, wide)
    return [(whole(shape), shape, BF16)] * 2


def qkv(me, pieces, key, select_tok, hi, lo, w, b_in):
    n, tok, k = select_tok.shape
    wide, own, slots, seq = pieces[0].shape[1], w.shape[2], n * CAP, n * tok
    return run(
        partial(qkv_kernel, n),
        "qkv",
        (EXPERTS + 2,),
        [rows_spec(p) for p in pieces]
        + [by_expert((n, tok), last_expert), whole(select_tok.shape), whole(hi.shape),
           whole(lo.shape), by_expert((wide, own)), by_expert((k, own))],
        [
            (by_expert((slots, own), last_expert), (EXPERTS, slots, own), BF16),
            (by_expert((seq, own), from_expert), (2, seq, own), BF16),
            (by_expert((slots, k), last_expert), (EXPERTS, slots, k), BF16),
            (by_expert((seq, k), from_expert), (2, seq, k), BF16),
            (by_expert((slots, own), last_expert), (EXPERTS, slots, own), BF16),
            (whole((seq, own)), (seq, own), BF16),
        ],
        [((128, wide), BF16), ((wide, own + 128), BF16), ((slots, tok), BF16),
         ((max(slots, seq // 2), wide), BF16),
         ((max(slots, seq // 2), k), F32), ((max(slots, seq // 2), 2 * HD), F32)],
        (me, *pieces, key, select_tok, hi, lo, w, b_in),
        2 * wide * own * (EXPERTS * slots + 2 * seq) * 1.5,
    )


def attend_specs(n, tok, own):
    slot_spec = pl.BlockSpec((EXPERTS, None, CAP, own), lambda b: (0, b, 0, 0))
    tokens = [pl.BlockSpec((None, EXPERTS, tok), lambda b: (b, 0, 0)),
              pl.BlockSpec((None, 1, tok), lambda b: (b, 0, 0))]
    return slot_spec, tokens, whole((n * tok, own)), (EXPERTS, n, CAP, own)


def attend(key, begin, q, k, v):
    n, tok = begin.shape[0], begin.shape[2]
    own, seq, rows = q.shape[2], n * tok, EXPERTS * CAP
    slot_spec, tokens, all_spec, shape = attend_specs(n, tok, own)
    mixed, lse = run(
        attend_kernel,
        "attend",
        (n,),
        tokens + [slot_spec, all_spec, all_spec],
        [(slot_spec, shape, BF16), (slot_spec, shape, F32)],
        [((own // HD, rows, seq), F32), ((rows, own), F32), ((rows, own), F32), ((rows, own), F32)],
        (key, begin, q.reshape(shape), k, v),
        3 * rows * seq * own * n,
        0,
    )
    return mixed.reshape(q.shape), lse


def attend_back(key, begin, q, g, mixed, lse, k, v):
    n, tok = begin.shape[0], begin.shape[2]
    own, seq, rows = q.shape[2], n * tok, EXPERTS * CAP
    slot_spec, tokens, all_spec, shape = attend_specs(n, tok, own)
    gq, gk, gv = run(
        attend_back_kernel,
        "attend_back",
        (n,),
        tokens + [slot_spec] * 4 + [all_spec] * 2,
        [(slot_spec, shape, F32), (all_spec, (seq, own), F32), (all_spec, (seq, own), F32)],
        [((rows, own), F32)],
        (key, begin, q.reshape(shape), g.reshape(shape), mixed.reshape(shape), lse, k, v),
        7 * rows * seq * own * n,
        0,
    )
    return gq.reshape(q.shape), gk, gv


def weight_spec(w, p=None):
    if p is None:
        return by_expert(w.shape[1:])
    return pl.BlockSpec((None, None) + w.shape[2:], lambda e, *unused: (e, p, 0, 0))


def project_out(name, me, x, key, share, select_tok, down, w, pieces, groups, first, stride, p=None):
    n, tok, k = select_tok.shape
    wide, slots, deep = pieces[0].shape[1], n * CAP, x.shape[2]
    down_spec = by_expert((k, deep)) if p is None else weight_spec(down, p)
    return run(
        partial(out_kernel, n, first, stride),
        name,
        (EXPERTS,),
        [rows_spec(m, groups * k) for m in pieces]
        + [by_expert((slots, deep)), by_expert((n, tok)), by_expert((n, tok)), whole(select_tok.shape),
           down_spec, weight_spec(w, p)],
        sides(n, tok, wide) + [(whole((RANK, EXPERTS * slots)), (RANK, EXPERTS * slots), BF16)],
        [((k, wide), BF16), ((slots, tok), BF16), ((slots, k), F32), ((slots, 128), F32),
         ((slots, chunk_of(slots, wide)), BF16), ((slots, 128), F32), ((n * tok, wide), F32)],
        (me, *pieces, x, key, share, select_tok, down, w),
        2 * wide * deep * EXPERTS * slots * 1.5,
    )


def feed_back_down(me, tokens, pieces, groups, first, stride, key, select_tok, w, small):
    n, tok, k = select_tok.shape
    wide, slots, deep = pieces[0].shape[1], n * CAP, w.shape[2]
    own = wide // n
    return run(
        partial(back_kernel, n, first, stride),
        "feed_down_back",
        (EXPERTS,),
        [rows_spec(m) for m in tokens] + [rows_spec(m, groups * k) for m in pieces]
        + [by_expert((n, tok)), whole(select_tok.shape), weight_spec(w, 2), weight_spec(small, 2)],
        [(by_expert((slots, deep)), (EXPERTS, slots, deep), F32),
         (by_expert((slots, k)), (EXPERTS, slots, k), BF16),
         (by_expert((slots, own)), (EXPERTS, slots, own), BF16)],
        [((deep + k, wide), BF16), ((slots, tok), BF16), ((slots, wide), BF16), ((slots, k), F32)],
        (me, *tokens, *pieces, key, select_tok, w, small),
        2 * wide * deep * EXPERTS * slots * 1.3,
    )


def mixed_back(me, tokens, pieces, groups, key, share, select_tok, w, small, mixed):
    n, tok, k = select_tok.shape
    wide, slots, own = pieces[0].shape[1], n * CAP, w.shape[1]
    return run(
        partial(mixed_back_kernel, n),
        "mixed_back",
        (EXPERTS,),
        [rows_spec(m) for m in tokens] + [rows_spec(m, groups * k) for m in pieces]
        + [by_expert((n, tok)), by_expert((n, tok)), whole(select_tok.shape),
           weight_spec(w), by_expert((k, own)), by_expert((slots, own))],
        [(by_expert((slots, own)), (EXPERTS, slots, own), BF16),
         (by_expert((k, own)), (EXPERTS, k, own), BF16),
         (whole((8, EXPERTS * slots)), (8, EXPERTS * slots), F32),
         (by_expert((slots, own)), (EXPERTS, slots, own), BF16)],
        [((own + k, wide), BF16), ((slots, tok), BF16), ((slots, wide), BF16), ((slots, k), F32),
         ((slots, 128), F32), ((slots, 128), F32)],
        (me, *tokens, *pieces, key, share, select_tok, w, small, mixed),
        2 * wide * own * EXPERTS * slots * 1.5,
    )


def feed(me, tokens, pieces, groups, first, stride, key, share, select_tok, w, hid, h, back_down):
    n, tok, k = select_tok.shape
    wide, slots, deep = pieces[0].shape[1], n * CAP, w.shape[2]
    own = wide // n
    return run(
        partial(feed_kernel, n, first, stride),
        "feed",
        (EXPERTS,),
        [rows_spec(m) for m in tokens] + [rows_spec(m, groups * k) for m in pieces]
        + [by_expert((n, tok)), by_expert((n, tok)),
           whole(select_tok.shape), weight_spec(w, 0), weight_spec(w, 1), by_expert((3, k, deep)),
           by_expert((slots, deep)), by_expert((slots, k))],
        [(pl.BlockSpec(memory_space=pl.ANY), (n // 2 * tok, wide), BF16)] * 2
        + [(by_expert((slots, deep)), (EXPERTS, slots, deep), BF16),
           (whole((3 * RANK, EXPERTS * slots)), (3 * RANK, EXPERTS * slots), BF16),
           (whole((8, EXPERTS * slots)), (8, EXPERTS * slots), F32),
           (by_expert((3, k, deep)), (EXPERTS, 3, k, deep), BF16),
           (by_expert((slots, own)), (EXPERTS, slots, own), BF16)],
        [((slots, tok), BF16), ((slots, wide), BF16), ((slots, k), F32), ((slots, 128), F32),
         ((slots, 256), F32), ((2 * k, wide), BF16), ((slots, deep), F32), ((slots, deep), F32),
         ((slots, deep), BF16), ((slots, deep), BF16), ((slots, chunk_of(slots, wide)), BF16),
         ((n * tok, wide), F32), pltpu.SemaphoreType.DMA],
        (me, *tokens, *pieces, key, share, select_tok, w, w, hid, h, back_down),
        8 * wide * deep * EXPERTS * slots * 1.3,
    )


def qkv_rank(key, select_tok, hi, lo, b_in, gq, gk, gv, rank_q, rank_kv):
    n, tok, k = select_tok.shape
    own, slots, seq = gq.shape[2], n * CAP, n * tok
    total = EXPERTS * slots + 2 * seq
    return run(
        qkv_rank_kernel,
        "qkv_rank",
        (EXPERTS + 2,),
        [by_expert((n, tok), last_expert), whole(select_tok.shape), whole(hi.shape),
         whole(lo.shape), by_expert((k, own)),
         by_expert((slots, own), last_expert), whole((seq, own)), whole((seq, own)),
         by_expert((slots, k), last_expert), by_expert((seq, k), from_expert)],
        [(by_expert((slots, own), last_expert), (EXPERTS, slots, own), BF16),
         (by_expert((seq, own), from_expert), (2, seq, own), BF16),
         (by_expert((slots, k), last_expert), (EXPERTS, slots, k), BF16),
         (by_expert((seq, k), from_expert), (2, seq, k), BF16),
         (whole((RANK, total)), (RANK, total), BF16),
         (by_expert((k, own)), (EXPERTS + 2, k, own), BF16)],
        [((slots, tok), BF16), ((slots, k), F32), ((slots, 2 * HD), F32), ((max(slots, seq), 128), F32)],
        (key, select_tok, hi, lo, b_in, gq, gk, gv, rank_q, rank_kv),
        4 * k * own * (EXPERTS * slots + 2 * seq),
        0,
    )


def qkv_back(me, pieces, key, w, gq, gkv, back_q, back_kv):
    n, tok = key.shape[1:]
    k, own, slots, seq = back_q.shape[2], w.shape[2], n * CAP, n * tok
    wide = pieces[0].shape[1]
    return run(
        partial(qkv_back_kernel, n),
        "qkv_back",
        (EXPERTS + 2,),
        [rows_spec(m, k) for m in pieces]
        + [by_expert((n, tok), last_expert), by_expert((wide, own)),
           by_expert((slots, own), last_expert), by_expert((seq, own), from_expert),
           by_expert((slots, k), last_expert), by_expert((seq, k), from_expert)],
        sides(n, tok, wide),
        [((k, wide), BF16), ((slots, tok), BF16), ((slots, chunk_of(slots, wide)), BF16),
         ((seq, wide), F32), ((seq // 2, own), BF16), ((seq // 2, k), BF16)],
        (me, *pieces, key, w, gq, gkv, back_q, back_kv),
        2 * wide * own * (EXPERTS * slots + 2 * seq) * 1.5,
    )


def members(routes):
    names = jnp.arange(EXPERTS, dtype=jnp.int32)[None, :, None]
    member = (routes[:, :1] == names) | (routes[:, 1:] == names)
    tok = routes.shape[-1]
    before = (jnp.arange(tok)[:, None] < jnp.arange(tok)[None, :]).astype(BF16)
    rank = ein("met,tu->meu", member.astype(BF16), before).astype(jnp.int32)
    return jnp.where(member, rank, -1)


def own_shares(normed, router, routes):
    names = jnp.arange(EXPERTS, dtype=jnp.int32)[:, None]
    member = (routes[:1] == names) | (routes[1:] == names)
    logits = ein("td,de->et", normed, router)
    return jax.nn.softmax(jnp.where(member, logits, -jnp.inf), axis=0)


def route_back(share, grad_share, router):
    grad = share * (grad_share - jnp.sum(share * grad_share, axis=0, keepdims=True))
    return jnp.einsum("et,de->td", grad, router.astype(F32), precision=lax.Precision.HIGHEST)


def local(
    n,
    reps,
    layer_input_state,
    cotangent,
    norm_gain_vectors,
    attention_router_weight,
    feed_router_weight,
    attention_query_weight,
    key_value_weight,
    attention_output_weight,
    feed_expert_weight,
    attention_adapters,
    feed_adapter_width,
    feed_adapter_hidden,
    token_document,
    document_adapter,
    attention_expert_pairs,
    feed_expert_pairs,
):
    tok, wide = layer_input_state.shape
    own, slots = wide // n, n * CAP
    columns = attention_adapters.shape[3]
    me = lax.axis_index("shard")
    me_ref = me.reshape(1).astype(jnp.int32)
    segments = token_document[0]
    seq = segments.shape[0]
    docs = document_adapter[0]
    doc_count = docs.shape[0]
    k = doc_count * RANK

    def one_hot(which):
        at = which[:, None] * RANK + jnp.arange(RANK)[None, :]
        return (at.reshape(-1)[:, None] == jnp.arange(columns)[None, :]).astype(BF16)

    pick = one_hot(docs)
    attn_small = ein("kc,pmwc->pmkw", pick, attention_adapters).astype(BF16)
    width_small = ein("kc,pmwc->pmkw", pick, feed_adapter_width).astype(BF16)
    hidden_small = ein("kc,epcf->epkf", pick, feed_adapter_hidden).astype(BF16)
    b_in, a_out = attn_small[1, : EXPERTS + 2], attn_small[0, EXPERTS + 2 :]

    x = layer_input_state.astype(F32)
    gain_one = norm_gain_vectors[0].astype(F32)
    gain_two = norm_gain_vectors[1].astype(F32)
    normed_own = rms_norm(gain_one, x).astype(BF16)
    routes = jnp.concatenate([attention_expert_pairs.T, feed_expert_pairs.T])
    own_a = own_shares(normed_own, attention_router_weight, routes[:2])
    own_hi = own_a.astype(BF16)
    own_lo = (own_a - lax.reduce_precision(own_a, 8, 7)).astype(BF16)
    spare = jnp.stack([routes.astype(BF16).reshape(-1), own_hi.reshape(-1), own_lo.reshape(-1)])
    first = jnp.concatenate([pack_maps(attn_small[0, : EXPERTS + 2], n, spare), normed_own])
    def send(g):
        return [lax.ppermute(g, "rep", [(i, i ^ d) for i in range(reps)]) if d else g for d in range(reps)]

    weights = [attention_query_weight, key_value_weight]
    if n == 8:
        cut = (first.shape[0] // 2 + 15) // 16 * 16
        y0, x1 = swap(first[:cut], n, 4), swap(first[cut:], n, 2)
        y1, x0 = swap(first[cut:], n, 4), swap(first[:cut], n, 2)
        y0, x1, docs_sent, *weights = tie(y0, x1, docs, *weights)
        d0, d1 = swap(y0, n, 2), swap(x1, n, 4)
        chips = {0: first}
        for m, p in ((2, (x0, x1)), (4, (y0, y1)), (6, (d0, d1))):
            chips[m] = jnp.concatenate(p)
    else:
        chips, docs_sent = across(first, n), docs
    pieces = from_sibling(chips, n)
    w_in = reshard(weights, me, n)

    facts = jnp.stack([p[:3, (EXPERTS + 2) * own : (EXPERTS + 2) * own + EXPERTS * tok] for p in pieces])
    facts = facts[jnp.arange(n) ^ me].reshape(n, 3, EXPERTS, tok)
    routes = facts[:, 0].astype(jnp.int32)
    share_a = facts[:, 1].astype(F32) + facts[:, 2].astype(F32)

    second = jnp.concatenate([attn_small[1, EXPERTS + 2 :], width_small.reshape(-1, k, own)])
    groups = -(-second.shape[0] // n)

    begins = jnp.sum((segments[None, :] < jnp.arange(doc_count)[:, None]).astype(jnp.int32), axis=1)
    doc = segments.reshape(n, tok)
    place = jnp.arange(seq, dtype=jnp.int32).reshape(n, tok)
    doc_table = doc[None] == jnp.arange(doc_count, dtype=jnp.int32)[:, None, None]
    begin = jnp.sum(jnp.where(doc_table, begins[:, None, None], 0), axis=0)
    freq = jnp.exp(-jnp.arange(HD // 2, dtype=F32) * (2.0 * math.log(10000.0) / HD))
    angles = (place - begin).astype(F32)[..., None] * freq
    cos, sin = jnp.cos(angles), jnp.sin(angles)
    table = jnp.concatenate([cos, cos, -sin, sin], axis=-1)
    table_hi = table.astype(BF16)
    table_lo = (table - lax.reduce_precision(table, 8, 7)).astype(BF16)
    chosen_doc = jnp.arange(k, dtype=jnp.int32)[None, None, :] // RANK
    select_tok = (doc[:, :, None] == chosen_doc).astype(BF16)
    select_row = doc_table.astype(F32).reshape(1, doc_count, seq)

    slot_a, slot_f = members(routes[:, :2]), members(routes[:, 2:])
    routes_f_own = feed_expert_pairs.T
    key_a, key_f = slot_a.transpose(1, 0, 2), slot_f.transpose(1, 0, 2)

    def slot_select(slot):
        hot = slot[:, :, None, :] == jnp.arange(CAP, dtype=jnp.int32)[None, None, :, None]
        chose = hot[:, :, None] & doc_table.transpose(1, 0, 2)[:, None, :, None, :]
        select = jnp.any(chose, axis=-1).astype(F32)
        return select.transpose(1, 2, 0, 3).reshape(EXPERTS, doc_count, slots)

    select_a, select_f = slot_select(slot_a), slot_select(slot_f)

    def slot_row(share, slot):
        hot = slot[:, :, None, :] == jnp.arange(CAP, dtype=jnp.int32)[None, None, :, None]
        row = jnp.sum(jnp.where(hot, share[:, :, None, :], 0.0), axis=-1)
        return row.transpose(1, 0, 2).reshape(EXPERTS, 1, slots)

    picks_sent = send(docs_sent)
    second, w_in, hidden_small, *picks_sent = tie(pack_maps(second, n), w_in, hidden_small, *picks_sent)
    map_chips = across(second, n)

    share_ae = share_a.transpose(1, 0, 2)
    q, kv, rank_q, rank_kv, rows_a_own, normed_own_columns = qkv(
        me_ref, pieces, key_a, select_tok, table_hi, table_lo, w_in, b_in
    )
    q, cotangent_sent, *sent = tie(q, cotangent, *map_chips.values())
    cotangent_chips = across(cotangent_sent, n)
    maps = from_sibling(dict(zip(map_chips, sent)), n)
    mixed, lse = attend(slot_a, begin[:, None], q, kv[0], kv[1])
    near, far, live_o = project_out(
        "attend_out", me_ref, mixed, key_a, share_ae, select_tok, a_out, attention_output_weight, maps, groups, 0, 1
    )
    near, far, *sent = tie(near, far, *cotangent_chips.values())
    attn_total, attn_low = halve(near, far, n)
    grads_out_all = from_sibling(dict(zip(cotangent_chips, sent)), n)
    *attn_low, key_late = tie(*attn_low, key_f)

    w_feed = jnp.swapaxes(feed_expert_weight, 2, 3)
    grad_inner, back_down, rows_g_own = feed_back_down(
        me_ref, grads_out_all, maps, groups, EXPERTS + 2, 3, key_late, select_tok, w_feed, hidden_small
    )
    attn_total, grad_inner = tie(attn_total, grad_inner)
    attended = x + collect(attn_total, attn_low, n)
    normed_two_own = rms_norm(gain_two, attended).astype(BF16)
    chips = across(normed_two_own, n)
    scaled_a = select_a * slot_row(share_a, slot_a)
    select_a, select_f, scaled_a, *sent = tie(select_a, select_f, scaled_a, *chips.values())
    normed_two = from_sibling(dict(zip(chips, sent)), n)
    own_f = own_shares(normed_two_own, feed_router_weight, routes_f_own)
    share_f = gather_small(own_f, me, n)
    share_fe = share_f.transpose(1, 0, 2)
    near, far, inner, live_f, dshare_f, hidden_grad, rows_f_own = feed(
        me_ref, normed_two, maps, groups, EXPERTS, 3, key_f, share_fe, select_tok, w_feed, hidden_small,
        grad_inner, back_down,
    )
    near, far = near.reshape(n // 2, tok, wide), far.reshape(n // 2, tok, wide)
    two_total, two_low = halve(near, far, n)
    dshare_f = dshare_f[:1]
    dshare_f = dshare_f + swap(dshare_f, n, 1)
    *two_low, inner, dshare_f, live_f, live_o = tie(*two_low, inner, dshare_f, live_f, live_o)
    live_f = jnp.concatenate([live_f, live_o])
    live_f = live_f + swap(live_f, n, 1)
    near, far, unused = project_out(
        "feed_out", me_ref, inner, key_f, share_fe, select_tok, hidden_small, w_feed, maps, groups, EXPERTS + 2, 3, 2
    )
    two_got = [swap(part, n, 2 * i + 2) for i, part in enumerate(two_low)]
    near, far, *two_got = tie(near, far, *two_got)
    grad_two_own = added([two_total] + two_got)

    def own_tokens(slot, dshare):
        mine = lax.dynamic_slice_in_dim(dshare.reshape(EXPERTS, n, CAP), me, 1, 1)[:, 0]
        hot = lax.dynamic_slice_in_dim(slot, me, 1, 0)[0][:, None, :] == jnp.arange(CAP)[None, :, None]
        return jnp.sum(jnp.where(hot, mine[:, :, None], 0.0), axis=1)

    d = 2
    while d < n:
        dshare_f, d = dshare_f + swap(dshare_f, n, d), 2 * d
    grad_two_own = grad_two_own + route_back(own_f, own_tokens(slot_f, dshare_f), feed_router_weight)
    grad_attended = cotangent.astype(F32) + rms_back(attended, gain_two, grad_two_own)

    grad_sent, near, far = tie(grad_attended.astype(BF16), near, far)
    out_total, out_low = halve(near, far, n)
    chips = across(grad_sent, n)
    out_total, *sent = tie(out_total, *out_low, *chips.values())
    out_low, sent = sent[: n // 2 - 1], sent[n // 2 - 1 :]
    grads_two = from_sibling(dict(zip(chips, sent)), n)
    mixed_late, live_f = tie(mixed, live_f)
    live_f_sent = list(across(live_f, n).values())
    grad_mixed, a_out_grad, dshare_a, rows_ga_own = mixed_back(
        me_ref, grads_two, maps, groups, key_a, share_ae, select_tok, attention_output_weight, a_out, mixed_late
    )
    grad_mixed, *sent = tie(grad_mixed, *live_f_sent, *out_low)
    live_f_sent, out_low = sent[: n // 2], sent[n // 2 :]
    gq, gk, gv = attend_back(slot_a, begin[:, None], q, grad_mixed, mixed, lse, kv[0], kv[1])
    out_got = [swap(part, n, 2 * i + 2) for i, part in enumerate(out_low)]
    gq, *sent = tie(gq, *live_f_sent, *out_got)
    live_f_sent, out_got = sent[: n // 2], sent[n // 2 :]
    live_f = added(live_f_sent)
    live_f, live_o = live_f[: 3 * RANK], live_f[3 * RANK :]

    def spread(live, select):
        both = live.astype(F32)[:, None] * select[:, :, None, :]
        return both.reshape(live.shape[0], k, live.shape[2]).astype(BF16)

    def of_slots(live):
        return live.reshape(RANK, EXPERTS, slots).transpose(1, 0, 2)

    def grads(rank, rows):
        return ein("eks,esw->ekw", rank, rows).astype(BF16)

    def by_stream(sent):
        out = jnp.zeros((reps,) + sent[0].shape, sent[0].dtype)
        for d, got in enumerate(sent):
            out = lax.dynamic_update_slice_in_dim(out, got[None], lax.axis_index("rep") ^ d, 0)
        return out

    scaled_f = select_f * slot_row(share_f, slot_f)
    width_grad = jnp.stack(
        [
            grads(spread(of_slots(live_f[:RANK]), select_f), rows_f_own),
            grads(spread(of_slots(live_f[RANK : 2 * RANK]), select_f), rows_f_own),
            grads(spread(of_slots(live_f[2 * RANK :]), scaled_f), rows_g_own),
        ],
        axis=1,
    )
    b_out_grad = grads(spread(of_slots(live_o), scaled_a), rows_ga_own)
    early_grad = jnp.concatenate([a_out_grad, b_out_grad])
    layer_out = attended + added([out_total] + out_got)
    gq, gkv, back_q, back_kv, live_in, b_in_grad = qkv_rank(
        key_a, select_tok, table_hi, table_lo, b_in, gq, gk, gv, rank_q, rank_kv
    )
    dshare_a = dshare_a[0].astype(BF16).reshape(RANK, -1)
    spare = -dshare_a.shape[1] % 128
    live_in = jnp.concatenate([live_in, jnp.pad(dshare_a, ((0, 0), (0, spare)))], axis=1)
    live_in = live_in + swap(live_in, n, 1)
    gq, live_in, b_in_grad, early_grad, width_grad = tie(gq, live_in, b_in_grad, early_grad, width_grad)
    hidden_all, width_all = lax.all_gather(hidden_grad, "rep"), lax.all_gather(width_grad, "rep")
    early_sent = send(jnp.concatenate([early_grad, b_in_grad]))
    live_sent = list(across(live_in, n).values())
    near, far = qkv_back(me_ref, pieces, key_a, w_in, gq, gkv, back_q, back_kv)
    near, far, *sent = tie(near, far, *live_sent, *early_sent)
    live_sent, early_sent = sent[: n // 2], sent[n // 2 :]
    in_total, in_low = (quarter if n == 8 else halve)(near, far, n)
    *in_low, first_sent = tie(*in_low, live_sent[0])
    in_got = [swap(part, n, 2 * i + 2) for i, part in enumerate(in_low)]
    live_in = added([first_sent] + live_sent[1:])
    width = EXPERTS * slots + 2 * seq
    dshare_a = live_in[:, width : width + EXPERTS * slots // RANK]
    live_kv = live_in[:, EXPERTS * slots : width].reshape(RANK, 2, seq).transpose(1, 0, 2)
    a_in_grad = jnp.concatenate(
        [
            grads(spread(of_slots(live_in[:, : EXPERTS * slots]), select_a), rows_a_own),
            ein("pks,sw->pkw", spread(live_kv, select_row), normed_own_columns).astype(BF16),
        ]
    )
    a_in_grad, hidden_all, *in_got = tie(a_in_grad, hidden_all, *in_got)
    late_a_sent = send(a_in_grad)
    grad_normed = collect_quarters(in_total, in_got, n) if n == 8 else added([in_total] + in_got)
    grad_normed = grad_normed + route_back(own_a, own_tokens(slot_a, dshare_a), attention_router_weight)
    grad_normed, width_all = tie(grad_normed, width_all)
    grad_in = grad_attended + rms_back(x, gain_one, grad_normed)

    picks = jax.vmap(one_hot)(jnp.stack(picks_sent)[jnp.arange(reps) ^ lax.axis_index("rep")])
    early = by_stream(early_sent)
    hidden_out = ein("rpekf,rkc->pecf", hidden_all, picks)
    width_out = ein("rpmkw,rkc->pmwc", width_all, picks)
    late = by_stream(late_a_sent)
    first, second, third = jnp.split(early, [EXPERTS, 2 * EXPERTS], axis=1)
    attn = jnp.concatenate([late, first, third, second], axis=1)
    attn = attn.reshape(reps, 2, -1, k, own)
    attn_out = ein("rpmkw,rkc->pmwc", attn, picks)
    return (layer_out, grad_in, attn_out, width_out, hidden_out)


def solution(mesh):
    in_specs = (
        P(("rep", "shard"), None),
        P(("rep", "shard"), None),
        P(),
        P(),
        P(),
        P(None, "shard", None),
        P(None, "shard", None),
        P(None, "shard", None),
        P(None, None, None, "shard"),
        P(None, None, "shard", None),
        P(None, None, "shard", None),
        P(None, None, None, "shard"),
        P("rep", None),
        P("rep", None),
        P(("rep", "shard"), None),
        P(("rep", "shard"), None),
    )
    out_specs = (
        P(("rep", "shard"), None),
        P(("rep", "shard"), None),
        P(None, None, "shard", None),
        P(None, None, "shard", None),
        P(None, None, None, "shard"),
    )
    body = partial(local, mesh.shape["shard"], mesh.shape["rep"])
    return jax.shard_map(body, mesh=mesh, in_specs=in_specs, out_specs=out_specs, check_vma=False)
```
